128 devices in a mesh: psg: 32 (over z, x, core), head: 4 (over y).
Axes of the slice: x: 4, y: 4, z: 4, core: 2. Of those that a mesh axis runs over, the one named last changes fastest.
Arguments:
- q_psg: bfloat16 [8192, 8192], P('psg', 'head'), may hold values from -10 to 10
- k_psg: bfloat16 [8192, 1024], P('psg', 'head'), may hold values from -10 to 10
- v_psg: bfloat16 [8192, 1024], P('psg', 'head'), may hold values from -6 to 6
- do_psg: bfloat16 [8192, 8192], P('psg', 'head'), may hold values from -6 to 6
- q_qry: bfloat16 [4096, 8192], P('psg', 'head'), may hold values from -10 to 10
- k_qry: bfloat16 [4096, 1024], P('psg', 'head'), may hold values from -10 to 10
- v_qry: bfloat16 [4096, 1024], P('psg', 'head'), may hold values from -6 to 6
- do_qry: bfloat16 [4096, 8192], P('psg', 'head'), may hold values from -6 to 6
- w_key: bfloat16 [8192, 1024], P(None, 'head'), may hold values from -0.1875 to 0.1875
- w_value: bfloat16 [8192, 1024], P(None, 'head'), may hold values from -0.1875 to 0.1875
- req_passages: int32 [32, 16], replicated, may hold values from 0 to 63, as said below
- passage_slot: int32 [64], replicated, may hold values from 0 to 63, as said below
- query_owner: int32 [32], replicated, may hold values from 0 to 31, each once
Outputs:
- dq_psg: bfloat16 [8192, 8192], P('psg', 'head')
- dq_qry: bfloat16 [4096, 8192], P('psg', 'head')
- dx_psg: bfloat16 [8192, 8192], P(('psg', 'head'))
- dx_qry: bfloat16 [4096, 8192], P(('psg', 'head'))
The draws below stay inside these ranges and needn't reach their ends.
Inputs may be any that keep to these rules, and one draw needn't show every extreme that they name: `req_passages`: the 16 passages of one request lie in 16 different row blocks of 2 passages each, passage_slot[id] // 2 being all different within the request. `passage_slot`: A permutation of the passage ids.
All inputs are finite; a program needn't handle non-finite values.
Results may differ from the reference program's by a relative error of at most 0.018.
Values may be sent and summed in bfloat16 or wider, within the bound.
A program may use at most 128 MiB of HBM per device.

```python
import jax
import jax.numpy as jnp
from jax import lax

HEADS = 64
KV_HEADS = 8
HEAD_DIM = 128
WIDTH = 8192
PLEN = 128
PSG_DEV = 2
QLEN = 128
NPSG = 64
REQ = 32
P_REQ = 16
PROWS = 8192
QROWS = 4096
N_HEAD = 4


def passage_layout(key):
    key = jax.random.fold_in(key, 900)
    shuffle = jax.random.permutation(jax.random.fold_in(key, 1), NPSG).astype(jnp.int32)
    device_count = NPSG // PSG_DEV
    scores = jax.random.randint(jax.random.fold_in(key, 2), (REQ, device_count), 0, 65536) * device_count + jnp.arange(device_count, dtype=jnp.int32)[None, :]
    unused, picked_dev = lax.top_k(scores, P_REQ)
    common = jax.random.randint(jax.random.fold_in(key, 3), (REQ, P_REQ), 0, 4)
    spread = jax.random.randint(jax.random.fold_in(key, 4), (REQ, P_REQ), 0, PSG_DEV)
    local_index = jnp.where(common < 3, 0, spread)
    slot_ids = picked_dev.astype(jnp.int32) * PSG_DEV + local_index
    inverse = jnp.argsort(shuffle, stable=True).astype(jnp.int32)
    passage_ids = inverse[slot_ids]
    return (shuffle, passage_ids.astype(jnp.int32))


def draw_req_passages(key, part):
    return passage_layout(key)[1]


def draw_passage_slot(key, part):
    return passage_layout(key)[0]


def draw_q_psg(key, part):
    key = jax.random.fold_in(key, 21)
    array_shape = (NPSG * PLEN, HEADS, HEAD_DIM)
    samples = jnp.clip(jax.random.normal(key, array_shape, jnp.float32), -5.0, 5.0)
    return samples.reshape(NPSG * PLEN, HEADS * HEAD_DIM).astype(jnp.bfloat16)


def draw_k_psg(key, part):
    key = jax.random.fold_in(key, 22)
    array_shape = (NPSG * PLEN, KV_HEADS, HEAD_DIM)
    samples = jnp.clip(jax.random.normal(key, array_shape, jnp.float32), -5.0, 5.0)
    return samples.reshape(NPSG * PLEN, KV_HEADS * HEAD_DIM).astype(jnp.bfloat16)


def draw_q_qry(key, part):
    key = jax.random.fold_in(key, 23)
    array_shape = (REQ * QLEN, HEADS, HEAD_DIM)
    samples = jnp.clip(jax.random.normal(key, array_shape, jnp.float32), -5.0, 5.0)
    return samples.reshape(REQ * QLEN, HEADS * HEAD_DIM).astype(jnp.bfloat16)


def draw_k_qry(key, part):
    key = jax.random.fold_in(key, 24)
    array_shape = (REQ * QLEN, KV_HEADS, HEAD_DIM)
    samples = jnp.clip(jax.random.normal(key, array_shape, jnp.float32), -5.0, 5.0)
    return samples.reshape(REQ * QLEN, KV_HEADS * HEAD_DIM).astype(jnp.bfloat16)


def levels(key, extent, shards, smallest, top_value):
    def one(axis_at, parts):
        heights = jax.random.uniform(jax.random.fold_in(jax.random.fold_in(key, 6), axis_at), (parts,), jnp.float32, smallest / len(shards), top_value / len(shards))
        return jnp.repeat(jnp.exp(heights), extent[axis_at] // parts).reshape((-1,) + (1,) * (len(extent) - axis_at - 1))

    loudness = one(*shards[0])
    for cut in shards[1:]:
        loudness = loudness * one(*cut)
    return loudness


def gaussian(stream_key, extent, scale, limit, cuts=(), held_as=jnp.bfloat16):
    entries = jax.random.normal(stream_key, extent, jnp.float32) * scale
    if len(cuts) > 0:
        entries = levels(stream_key, extent, cuts, -0.22, 0.18) * entries
    return jnp.clip(entries, min=-limit, max=limit).astype(held_as)


def setup_inputs(seed: int = 0) -> dict:
    key_of = jax.random.split(jax.random.key(seed), 14)
    q_psg = draw_q_psg(jax.random.fold_in(key_of[13], 71), 0)
    k_psg = draw_k_psg(jax.random.fold_in(key_of[13], 71), 0)
    v_psg = gaussian(key_of[2], (PROWS, KV_HEADS * HEAD_DIM), 1.0, 6.0, ((0, 32), (1, 4)))
    do_psg = gaussian(key_of[3], (PROWS, HEADS * HEAD_DIM), 1.0, 6.0, ((0, 32), (1, 4)))
    q_qry = draw_q_qry(jax.random.fold_in(key_of[13], 71), 0)
    k_qry = draw_k_qry(jax.random.fold_in(key_of[13], 71), 0)
    v_qry = gaussian(key_of[6], (QROWS, KV_HEADS * HEAD_DIM), 1.0, 6.0, ((0, 32), (1, 4)))
    do_qry = gaussian(key_of[7], (QROWS, HEADS * HEAD_DIM), 1.0, 6.0, ((0, 32), (1, 4)))
    w_key = gaussian(key_of[8], (WIDTH, KV_HEADS * HEAD_DIM), (KV_HEADS * HEAD_DIM) ** -0.5, 0.1875, ((1, 4),))
    w_value = gaussian(key_of[9], (WIDTH, KV_HEADS * HEAD_DIM), (KV_HEADS * HEAD_DIM) ** -0.5, 0.1875, ((1, 4),))
    req_passages = draw_req_passages(jax.random.fold_in(key_of[13], 71), 0)
    passage_slot = draw_passage_slot(jax.random.fold_in(key_of[13], 71), 0)
    query_owner = jax.random.permutation(key_of[12], REQ).astype(jnp.int32)
    return dict(q_psg=q_psg, k_psg=k_psg, v_psg=v_psg, do_psg=do_psg, q_qry=q_qry, k_qry=k_qry, v_qry=v_qry, do_qry=do_qry, w_key=w_key, w_value=w_value, req_passages=req_passages, passage_slot=passage_slot, query_owner=query_owner)


def rounded(array_in):
    return lax.optimization_barrier(array_in.astype(jnp.bfloat16)).astype(jnp.float32)


def attend_back(query_rows, key_rows, value_rows, cotangent, allowed, softmax_scale):
    query_rows = query_rows.astype(jnp.float32)
    key_rows = key_rows.astype(jnp.float32)
    value_rows = value_rows.astype(jnp.float32)
    cotangent = cotangent.astype(jnp.float32)
    scores = jnp.einsum("qhgd,khd->hgqk", query_rows, key_rows) * softmax_scale
    scores = jnp.where(allowed, scores, -1e30)
    row_max = jnp.max(scores, axis=-1, keepdims=True)
    weights = jnp.exp(scores - row_max)
    probs = weights / jnp.sum(weights, axis=-1, keepdims=True)
    probs_low = rounded(probs)
    dprobs = jnp.einsum("qhgd,khd->hgqk", cotangent, value_rows)
    delta_rows = jnp.sum(probs * dprobs, axis=-1, keepdims=True)
    dscore = rounded(probs * (dprobs - delta_rows) * softmax_scale)
    grad_q = jnp.einsum("hgqk,khd->qhgd", dscore, key_rows)
    grad_k = jnp.einsum("hgqk,qhgd->khd", dscore, query_rows)
    grad_v = jnp.einsum("hgqk,qhgd->khd", probs_low, cotangent)
    return grad_q, grad_k, grad_v


def project_block(pieces, w_key, w_value):
    rows_k, rows_v = pieces
    group_cols = rows_k.shape[1] // N_HEAD
    total = jnp.zeros((rows_k.shape[0], WIDTH), jnp.float32)
    for group_index in range(N_HEAD):
        col_start = group_index * group_cols
        col_end = col_start + group_cols
        product = jnp.dot(rows_k[:, col_start:col_end], w_key[:, col_start:col_end].T, preferred_element_type=jnp.float32)
        product = product + jnp.dot(rows_v[:, col_start:col_end], w_value[:, col_start:col_end].T, preferred_element_type=jnp.float32)
        total = total + rounded(product)
    return total.astype(jnp.bfloat16)


def reference(q_psg, k_psg, v_psg, do_psg, q_qry, k_qry, v_qry, do_qry, w_key, w_value, req_passages, passage_slot, query_owner):
    group_size = HEADS // KV_HEADS
    softmax_scale = HEAD_DIM ** -0.5
    q_blocks = q_psg.reshape(NPSG, PLEN, KV_HEADS, group_size, HEAD_DIM)
    k_blocks = k_psg.reshape(NPSG, PLEN, KV_HEADS, HEAD_DIM)
    v_blocks = v_psg.reshape(NPSG, PLEN, KV_HEADS, HEAD_DIM)
    d_blocks = do_psg.reshape(NPSG, PLEN, KV_HEADS, group_size, HEAD_DIM)
    causal = jnp.arange(PLEN)[None, :] <= jnp.arange(PLEN)[:, None]

    def passage_step(pieces):
        return attend_back(pieces[0], pieces[1], pieces[2], pieces[3], causal, softmax_scale)

    grad_qp, own_k, own_v = lax.map(passage_step, (q_blocks, k_blocks, v_blocks, d_blocks))
    dq_psg = grad_qp.reshape(PROWS, HEADS * HEAD_DIM).astype(jnp.bfloat16)

    qq_blocks = q_qry.reshape(REQ, QLEN, KV_HEADS, group_size, HEAD_DIM)
    kq_blocks = k_qry.reshape(REQ, QLEN, KV_HEADS, HEAD_DIM)
    vq_blocks = v_qry.reshape(REQ, QLEN, KV_HEADS, HEAD_DIM)
    dq_blocks = do_qry.reshape(REQ, QLEN, KV_HEADS, group_size, HEAD_DIM)
    front_keys = P_REQ * PLEN
    row_ids = jnp.arange(QLEN)[:, None]
    col_ids = jnp.arange(front_keys + QLEN)[None, :]
    allowed = (col_ids < front_keys) | (col_ids - front_keys <= row_ids)

    def request_step(totals, request):
        acc_k, acc_v = totals
        owner_slot = query_owner[request]
        slot_ids = passage_slot[req_passages[request]].astype(jnp.int32)
        key_rows = jnp.concatenate([k_blocks[slot_ids].reshape(front_keys, KV_HEADS, HEAD_DIM), kq_blocks[owner_slot]], 0)
        value_rows = jnp.concatenate([v_blocks[slot_ids].reshape(front_keys, KV_HEADS, HEAD_DIM), vq_blocks[owner_slot]], 0)
        grad_q, grad_k, grad_v = attend_back(qq_blocks[owner_slot], key_rows, value_rows, dq_blocks[owner_slot], allowed, softmax_scale)
        part_k = rounded(grad_k[:front_keys]).reshape(P_REQ, PLEN, KV_HEADS, HEAD_DIM)
        part_v = rounded(grad_v[:front_keys]).reshape(P_REQ, PLEN, KV_HEADS, HEAD_DIM)
        acc_k = acc_k.at[slot_ids].add(part_k)
        acc_v = acc_v.at[slot_ids].add(part_v)
        return (acc_k, acc_v), (grad_q, grad_k[front_keys:], grad_v[front_keys:])

    empty = jnp.zeros((NPSG, PLEN, KV_HEADS, HEAD_DIM), jnp.float32)
    (acc_k, acc_v), (grad_qr, grad_kr, grad_vr) = lax.scan(request_step, (empty, empty), jnp.arange(REQ, dtype=jnp.int32))
    grad_qs = jnp.zeros_like(grad_qr).at[query_owner].set(grad_qr)
    grad_ks = jnp.zeros_like(grad_kr).at[query_owner].set(grad_kr)
    grad_vs = jnp.zeros_like(grad_vr).at[query_owner].set(grad_vr)
    dq_qry = grad_qs.reshape(QROWS, HEADS * HEAD_DIM).astype(jnp.bfloat16)

    key_grad_psg = (own_k + acc_k).astype(jnp.bfloat16).reshape(NPSG, PLEN, KV_HEADS * HEAD_DIM)
    value_grad_psg = (own_v + acc_v).astype(jnp.bfloat16).reshape(NPSG, PLEN, KV_HEADS * HEAD_DIM)
    key_grad_qry = grad_ks.astype(jnp.bfloat16).reshape(REQ, QLEN, KV_HEADS * HEAD_DIM)
    value_grad_qry = grad_vs.astype(jnp.bfloat16).reshape(REQ, QLEN, KV_HEADS * HEAD_DIM)

    def project_one(pieces):
        return project_block(pieces, w_key, w_value)

    dx_psg = lax.map(project_one, (key_grad_psg, value_grad_psg)).reshape(PROWS, WIDTH)
    dx_qry = lax.map(project_one, (key_grad_qry, value_grad_qry)).reshape(QROWS, WIDTH)
    return dq_psg, dq_qry, dx_psg, dx_qry
```

```python
import functools

import jax
import jax.numpy as jnp
from jax import lax
from jax.experimental import pallas as pl
from jax.experimental.pallas import tpu as pltpu
from jax.sharding import PartitionSpec as P

D = 128
G = 8
PLEN = 128
KV = 2
NPSG = 64
REQ = 32
P_REQ = 16
CB = 256
C = D ** -0.5
C2 = C * 1.4426950408889634
F32 = jnp.float32
BF16 = jnp.bfloat16


def stack(x):
    return jnp.concatenate([x[:, g * D:(g + 1) * D] for g in range(G)], axis=0)


def dot(a, b):
    return jnp.dot(a, b, preferred_element_type=F32)


def dot_t(a, b):
    return lax.dot_general(a, b, (((1,), (1,)), ((), ())), preferred_element_type=F32)


def causal_cols(shape):
    key = lax.broadcasted_iota(jnp.int32, shape, 0)
    qry = lax.broadcasted_iota(jnp.int32, shape, 1) % PLEN
    return key <= qry


def psg_kernel(q_ref, k_ref, v_ref, do_ref, dq_ref, gk_ref, gv_ref):
    qs = stack(q_ref[...])
    dos = stack(do_ref[...])
    k = k_ref[...]
    v = v_ref[...]
    kt = k.T
    gk = jnp.zeros((PLEN, D), F32)
    gv = jnp.zeros((PLEN, D), F32)
    for b in range(G * PLEN // CB):
        cols = slice(b * CB, (b + 1) * CB)
        s = dot_t(k, qs[cols])
        s = jnp.where(causal_cols(s.shape), s, -1e30)
        e = jnp.exp2((s - jnp.max(s, axis=0, keepdims=True)) * C2)
        inv = 1.0 / jnp.sum(e, axis=0, keepdims=True)
        dp = dot_t(v, dos[cols])
        p = e * inv
        delta = jnp.sum(p * dp, axis=0, keepdims=True)
        ds = (p * (dp - delta)).astype(BF16)
        gk += dot(ds, qs[cols])
        gv += dot(p.astype(BF16), dos[cols])
        dqt = dot(kt, ds) * C
        for i in range(CB // PLEN):
            g = b * (CB // PLEN) + i
            dq_ref[:, g * D:(g + 1) * D] = dqt[:, i * PLEN:(i + 1) * PLEN].T.astype(BF16)
    gk_ref[...] = gk * C
    gv_ref[...] = gv


def psg_back(q, k, v, do):
    rows = q.shape[0]
    wide = pl.BlockSpec((PLEN, G * D), lambda n, h: (n, h))
    thin = pl.BlockSpec((PLEN, D), lambda n, h: (n, h))
    return pl.pallas_call(
        psg_kernel,
        grid=(rows // PLEN, KV),
        in_specs=[wide, thin, thin, wide],
        out_specs=[wide, thin, thin],
        out_shape=[
            jax.ShapeDtypeStruct(q.shape, BF16),
            jax.ShapeDtypeStruct(k.shape, F32),
            jax.ShapeDtypeStruct(v.shape, F32),
        ],
        compiler_params=pltpu.CompilerParams(vmem_limit_bytes=40 * 1024 * 1024),
        cost_estimate=pl.CostEstimate(flops=4 * 5 * 2 * 1024 * 128 * 128, bytes_accessed=4 * 1024 * 1024, transcendentals=4 * 1024 * 128),
        name="psg_back",
    )(q, k, v, do)


TK = 256
NT = P_REQ * PLEN // TK


def qry_kernel(
    req_ref, slot_ref, owner_ref, kvg_ref, q_ref, do_ref, kq_ref, vq_ref, me_ref,
    dq_ref, gk_ref, gv_ref, full_ref,
    qs, dos, qst, dost, kbuf, vbuf, ktbuf, ebuf, dpbuf, mt, dqt, gkbuf, gvbuf, zeros, slots, mask,
    in_sem, out_sem, zero_sem,
):
    h = pl.program_id(0)
    me = me_ref[0]

    @pl.when(h == 0)
    def _():
        zeros[...] = jnp.zeros_like(zeros)
        request = jnp.int32(0)
        for r in range(REQ):
            request = jnp.where(owner_ref[r] == me, r, request)

        def clear(i, c):
            mask[i] = 0
            return c

        lax.fori_loop(0, NPSG, clear, 0)

        def pick(j, c):
            slot = slot_ref[req_ref[request, j]]
            slots[j] = slot
            mask[slot] = 1
            return c

        lax.fori_loop(0, P_REQ, pick, 0)

        def blank(i, c):
            @pl.when(mask[i] == 0)
            def _():
                pltpu.make_async_copy(zeros, full_ref.at[i], zero_sem).start()

            return c

        lax.fori_loop(0, NPSG, blank, 0)

    kcols = pl.ds(pl.multiple_of(h * D, D), D)
    vcols = pl.ds(pl.multiple_of(KV * D + h * D, D), D)
    copies = []
    for j in range(P_REQ):
        rows = pl.ds(j * PLEN, PLEN)
        copies.append(pltpu.make_async_copy(kvg_ref.at[slots[j], :, kcols], kbuf.at[rows], in_sem.at[0]))
        copies.append(pltpu.make_async_copy(kvg_ref.at[slots[j], :, vcols], vbuf.at[rows], in_sem.at[1]))
    for copy in copies:
        copy.start()
    qs[...] = stack(q_ref[...])
    dos[...] = stack(do_ref[...])
    qst[...] = qs[...].T
    dost[...] = dos[...].T

    def first(t, keys, values, rows, masked, carry):
        m, l, num = carry
        ms, ls, nums = [], [], []
        for b in range(G * PLEN // CB):
            cols = slice(b * CB, (b + 1) * CB)
            s = dot(keys, qst[:, cols])
            if masked:
                s = jnp.where(causal_cols(s.shape), s, -1e30)
            m_old = m[:, cols]
            m_new = jnp.maximum(m_old, jnp.max(s, axis=0, keepdims=True))
            alpha = jnp.exp2((m_old - m_new) * C2)
            e = jnp.exp2((s - m_new) * C2)
            dp = dot(values, dost[:, cols])
            ebuf[rows, cols] = e
            dpbuf[rows, cols] = dp
            ms.append(m_new)
            ls.append(l[:, cols] * alpha + jnp.sum(e, axis=0, keepdims=True))
            nums.append(num[:, cols] * alpha + jnp.sum(e * dp, axis=0, keepdims=True))
        m = jnp.concatenate(ms, axis=1)
        mt[t] = m
        return m, jnp.concatenate(ls, axis=1), jnp.concatenate(nums, axis=1)

    wide = (1, G * PLEN)
    own = slice(P_REQ * PLEN, P_REQ * PLEN + PLEN)
    carry = (jnp.full(wide, -1e30, F32), jnp.zeros(wide, F32), jnp.zeros(wide, F32))
    carry = first(NT, kq_ref[...], vq_ref[...], own, True, carry)
    for copy in copies:
        copy.wait()

    def step(t, carry):
        rows = pl.ds(pl.multiple_of(t * TK, TK), TK)
        keys = kbuf[rows, :]
        ktbuf[t] = keys.T
        return first(t, keys, vbuf[rows, :], rows, False, carry)

    m, l, num = lax.fori_loop(0, NT, step, carry)
    inv = 1.0 / l
    delta = num * inv

    def second(t, kt, rows, out_rows, acc):
        scale = jnp.exp2((mt[t] - m) * C2) * inv
        gk = gv = None
        for b in range(G * PLEN // CB):
            cols = slice(b * CB, (b + 1) * CB)
            p = ebuf[rows, cols] * scale[:, cols]
            ds = (p * (dpbuf[rows, cols] - delta[:, cols])).astype(BF16)
            dk = dot(ds, qs[cols, :])
            dv = dot(p.astype(BF16), dos[cols, :])
            gk = dk if gk is None else gk + dk
            gv = dv if gv is None else gv + dv
            more = dot(kt, ds)
            dqt[:, cols] = dqt[:, cols] + more if acc else more
        return (gk * C).astype(BF16), gv.astype(BF16)

    gk, gv = second(NT, kq_ref[...].T, own, None, False)
    gk_ref[...] = gk
    gv_ref[...] = gv

    def back(t, c):
        rows = pl.ds(pl.multiple_of(t * TK, TK), TK)
        gk, gv = second(t, ktbuf[t], rows, rows, True)
        gkbuf[rows, :] = gk
        gvbuf[rows, :] = gv
        for i in range(TK // PLEN):
            j = t * (TK // PLEN) + i
            part = pl.ds(pl.multiple_of(j * PLEN, PLEN), PLEN)
            slot = slots[j]
            pltpu.make_async_copy(gkbuf.at[part], full_ref.at[slot, :, kcols], out_sem.at[0]).start()
            pltpu.make_async_copy(gvbuf.at[part], full_ref.at[slot, :, vcols], out_sem.at[1]).start()
        return c

    lax.fori_loop(0, NT, back, 0)
    for g in range(G):
        dq_ref[:, g * D:(g + 1) * D] = (dqt[:, g * PLEN:(g + 1) * PLEN] * C).T.astype(BF16)

    def drain(j, c):
        rows = pl.ds(pl.multiple_of(j * PLEN, PLEN), PLEN)
        pltpu.make_async_copy(gkbuf.at[rows], full_ref.at[slots[j], :, kcols], out_sem.at[0]).wait()
        pltpu.make_async_copy(gvbuf.at[rows], full_ref.at[slots[j], :, vcols], out_sem.at[1]).wait()
        return c

    lax.fori_loop(0, P_REQ, drain, 0)

    @pl.when(h == KV - 1)
    def _():
        def blanked(i, c):
            @pl.when(mask[i] == 0)
            def _():
                pltpu.make_async_copy(zeros, full_ref.at[i], zero_sem).wait()

            return c

        lax.fori_loop(0, NPSG, blanked, 0)


def qry_back(req, slot, owner, kvg, q, do, kq, vq, me):
    keys = P_REQ * PLEN + PLEN
    wide = pl.BlockSpec((PLEN, G * D), lambda h: (0, h))
    thin = pl.BlockSpec((PLEN, D), lambda h: (0, h))
    smem = pl.BlockSpec(memory_space=pltpu.SMEM)
    hbm = pl.BlockSpec(memory_space=pl.ANY)
    return pl.pallas_call(
        qry_kernel,
        grid=(KV,),
        in_specs=[smem, smem, smem, hbm, wide, wide, thin, thin, smem],
        out_specs=[wide, thin, thin, hbm],
        out_shape=[
            jax.ShapeDtypeStruct(q.shape, BF16),
            jax.ShapeDtypeStruct(kq.shape, BF16),
            jax.ShapeDtypeStruct(vq.shape, BF16),
            jax.ShapeDtypeStruct((NPSG, PLEN, 2 * KV * D), BF16),
        ],
        scratch_shapes=[
            pltpu.VMEM((G * PLEN, D), BF16),
            pltpu.VMEM((G * PLEN, D), BF16),
            pltpu.VMEM((D, G * PLEN), BF16),
            pltpu.VMEM((D, G * PLEN), BF16),
            pltpu.VMEM((P_REQ * PLEN, D), BF16),
            pltpu.VMEM((P_REQ * PLEN, D), BF16),
            pltpu.VMEM((NT, D, TK), BF16),
            pltpu.VMEM((keys, G * PLEN), F32),
            pltpu.VMEM((keys, G * PLEN), F32),
            pltpu.VMEM((NT + 1, 1, G * PLEN), F32),
            pltpu.VMEM((D, G * PLEN), F32),
            pltpu.VMEM((P_REQ * PLEN, D), BF16),
            pltpu.VMEM((P_REQ * PLEN, D), BF16),
            pltpu.VMEM((PLEN, 2 * KV * D), BF16),
            pltpu.SMEM((P_REQ,), jnp.int32),
            pltpu.SMEM((NPSG,), jnp.int32),
            pltpu.SemaphoreType.DMA((2,)),
            pltpu.SemaphoreType.DMA((2,)),
            pltpu.SemaphoreType.DMA,
        ],
        compiler_params=pltpu.CompilerParams(vmem_limit_bytes=48 * 1024 * 1024),
        cost_estimate=pl.CostEstimate(flops=2 * 5 * 2 * 1024 * 2176 * 128, bytes_accessed=16 * 1024 * 1024, transcendentals=2 * 1024 * 2176),
        name="qry_back",
    )(req, slot, owner, kvg, q, do, kq, vq, me)


WB = 1024


def term_kernel(k_ref, v_ref, wk_ref, wv_ref, out_ref):
    out_ref[...] = (dot_t(k_ref[...], wk_ref[...]) + dot_t(v_ref[...], wv_ref[...])).astype(BF16)


def term(rows_k, rows_v, w_key, w_value):
    rows = rows_k.shape[0]
    width, depth = w_key.shape
    return pl.pallas_call(
        term_kernel,
        grid=(width // WB,),
        in_specs=[
            pl.BlockSpec((rows, depth), lambda i: (0, 0)),
            pl.BlockSpec((rows, depth), lambda i: (0, 0)),
            pl.BlockSpec((WB, depth), lambda i: (i, 0)),
            pl.BlockSpec((WB, depth), lambda i: (i, 0)),
        ],
        out_specs=pl.BlockSpec((rows, WB), lambda i: (0, i)),
        out_shape=jax.ShapeDtypeStruct((rows, width), BF16),
        compiler_params=pltpu.CompilerParams(vmem_limit_bytes=32 * 1024 * 1024),
        cost_estimate=pl.CostEstimate(flops=4 * rows * width * depth, bytes_accessed=4 * width * depth + 2 * rows * width, transcendentals=0),
        name="term",
    )(rows_k, rows_v, w_key, w_value)


def local(q_psg, k_psg, v_psg, do_psg, q_qry, k_qry, v_qry, do_qry, w_key, w_value, req_passages, passage_slot, query_owner):
    me = lax.axis_index("psg").astype(jnp.int32).reshape(1)
    kv = jnp.concatenate([k_psg, v_psg], axis=1)
    every = lax.all_gather(kv, "psg", axis=0, tiled=True)
    dq_psg, own_k, own_v = psg_back(q_psg, k_psg, v_psg, do_psg)
    dq_qry, gk_qry, gv_qry, full = qry_back(
        req_passages, passage_slot, query_owner, every.reshape(NPSG, PLEN, -1), q_qry, do_qry, k_qry, v_qry, me
    )
    summed = lax.psum_scatter(full.reshape(NPSG * PLEN, -1), "psg", scatter_dimension=0, tiled=True)
    dx_qry = lax.psum_scatter(term(gk_qry, gv_qry, w_key, w_value), "head", scatter_dimension=0, tiled=True)
    cols = KV * D
    gk = (own_k + summed[:, :cols].astype(F32)).astype(BF16)
    gv = (own_v + summed[:, cols:].astype(F32)).astype(BF16)
    dx_psg = lax.psum_scatter(term(gk, gv, w_key, w_value), "head", scatter_dimension=0, tiled=True)
    return dq_psg, dq_qry, dx_psg, dx_qry


def solution(mesh):
    rows = P("psg", "head")
    return jax.shard_map(
        local,
        mesh=mesh,
        in_specs=(rows,) * 8 + (P(None, "head"),) * 2 + (P(),) * 3,
        out_specs=(rows, rows, P(("psg", "head"), None), P(("psg", "head"), None)),
        check_vma=False,
    )
```

```python
import functools

import jax
import jax.numpy as jnp
from jax import lax
from jax.experimental import pallas as pl
from jax.experimental.pallas import tpu as pltpu
from jax.sharding import PartitionSpec as P

D = 128
G = 8
PLEN = 128
KV = 2
NPSG = 64
REQ = 32
P_REQ = 16
CB = 256
C = D ** -0.5
C2 = C * 1.4426950408889634
F32 = jnp.float32
BF16 = jnp.bfloat16


def stack(x):
    return jnp.concatenate([x[:, g * D:(g + 1) * D] for g in range(G)], axis=0)


def dot(a, b):
    return jnp.dot(a, b, preferred_element_type=F32)


def dot_t(a, b):
    return lax.dot_general(a, b, (((1,), (1,)), ((), ())), preferred_element_type=F32)


def causal_cols(shape):
    key = lax.broadcasted_iota(jnp.int32, shape, 0)
    qry = lax.broadcasted_iota(jnp.int32, shape, 1) % PLEN
    return key <= qry


def psg_kernel(q_ref, k_ref, v_ref, do_ref, dq_ref, gk_ref, gv_ref):
    qs = stack(q_ref[...])
    dos = stack(do_ref[...])
    k = k_ref[...]
    v = v_ref[...]
    kt = k.T
    gk = jnp.zeros((PLEN, D), F32)
    gv = jnp.zeros((PLEN, D), F32)
    for b in range(G * PLEN // CB):
        cols = slice(b * CB, (b + 1) * CB)
        s = dot_t(k, qs[cols])
        s = jnp.where(causal_cols(s.shape), s, -1e30)
        e = jnp.exp2((s - jnp.max(s, axis=0, keepdims=True)) * C2)
        inv = 1.0 / jnp.sum(e, axis=0, keepdims=True)
        dp = dot_t(v, dos[cols])
        p = e * inv
        delta = jnp.sum(p * dp, axis=0, keepdims=True)
        ds = (p * (dp - delta)).astype(BF16)
        gk += dot(ds, qs[cols])
        gv += dot(p.astype(BF16), dos[cols])
        dqt = dot(kt, ds) * C
        for i in range(CB // PLEN):
            g = b * (CB // PLEN) + i
            dq_ref[:, g * D:(g + 1) * D] = dqt[:, i * PLEN:(i + 1) * PLEN].T.astype(BF16)
    gk_ref[...] = gk * C
    gv_ref[...] = gv


def psg_back(q, k, v, do):
    rows = q.shape[0]
    wide = pl.BlockSpec((PLEN, G * D), lambda n, h: (n, h))
    thin = pl.BlockSpec((PLEN, D), lambda n, h: (n, h))
    return pl.pallas_call(
        psg_kernel,
        grid=(rows // PLEN, KV),
        in_specs=[wide, thin, thin, wide],
        out_specs=[wide, thin, thin],
        out_shape=[
            jax.ShapeDtypeStruct(q.shape, BF16),
            jax.ShapeDtypeStruct(k.shape, F32),
            jax.ShapeDtypeStruct(v.shape, F32),
        ],
        compiler_params=pltpu.CompilerParams(vmem_limit_bytes=40 * 1024 * 1024),
        cost_estimate=pl.CostEstimate(flops=4 * 5 * 2 * 1024 * 128 * 128, bytes_accessed=4 * 1024 * 1024, transcendentals=4 * 1024 * 128),
        name="psg_back",
    )(q, k, v, do)


TK = 256
NT = P_REQ * PLEN // TK


def spot(slot):
    n = slot % 2
    c = slot // 2 % 2
    x = slot // 4 % 4
    z = slot // 16
    return jnp.where(n == 0, c * 16 + z * 4 + x, 32 + c * 16 + x * 4 + z)


def qry_kernel(
    req_ref, slot_ref, owner_ref, kvg_ref, q_ref, do_ref, kq_ref, vq_ref, me_ref,
    dq_ref, gk_ref, gv_ref, full_ref,
    qs, dos, qst, dost, kbuf, vbuf, ktbuf, ebuf, dpbuf, mt, dqt, gkbuf, gvbuf, zeros, slots, mask,
    in_sem, out_sem, zero_sem,
):
    h = pl.program_id(0)
    me = me_ref[0]

    @pl.when(h == 0)
    def _():
        zeros[...] = jnp.zeros_like(zeros)
        request = jnp.int32(0)
        for r in range(REQ):
            request = jnp.where(owner_ref[r] == me, r, request)

        def clear(i, c):
            mask[i] = 0
            return c

        lax.fori_loop(0, NPSG, clear, 0)

        def pick(j, c):
            slot = spot(slot_ref[req_ref[request, j]])
            slots[j] = slot
            mask[slot] = 1
            return c

        lax.fori_loop(0, P_REQ, pick, 0)

        def blank(i, c):
            @pl.when(mask[i] == 0)
            def _():
                pltpu.make_async_copy(zeros, full_ref.at[i], zero_sem).start()

            return c

        lax.fori_loop(0, NPSG, blank, 0)

    cols = pl.ds(pl.multiple_of(h * D, D), D)
    copies = []
    for j in range(P_REQ):
        rows = pl.ds(j * PLEN, PLEN)
        copies.append(pltpu.make_async_copy(kvg_ref.at[slots[j], 0, :, cols], kbuf.at[rows], in_sem.at[0]))
        copies.append(pltpu.make_async_copy(kvg_ref.at[slots[j], 1, :, cols], vbuf.at[rows], in_sem.at[1]))
    for copy in copies:
        copy.start()
    qs[...] = stack(q_ref[...])
    dos[...] = stack(do_ref[...])
    qst[...] = qs[...].T
    dost[...] = dos[...].T

    def first(t, keys, values, rows, masked, carry):
        m, l, num = carry
        ms, ls, nums = [], [], []
        for b in range(G * PLEN // CB):
            cols = slice(b * CB, (b + 1) * CB)
            s = dot(keys, qst[:, cols])
            if masked:
                s = jnp.where(causal_cols(s.shape), s, -1e30)
            m_old = m[:, cols]
            m_new = jnp.maximum(m_old, jnp.max(s, axis=0, keepdims=True))
            alpha = jnp.exp2((m_old - m_new) * C2)
            e = jnp.exp2((s - m_new) * C2)
            dp = dot(values, dost[:, cols])
            ebuf[rows, cols] = e
            dpbuf[rows, cols] = dp
            ms.append(m_new)
            ls.append(l[:, cols] * alpha + jnp.sum(e, axis=0, keepdims=True))
            nums.append(num[:, cols] * alpha + jnp.sum(e * dp, axis=0, keepdims=True))
        m = jnp.concatenate(ms, axis=1)
        mt[t] = m
        return m, jnp.concatenate(ls, axis=1), jnp.concatenate(nums, axis=1)

    wide = (1, G * PLEN)
    own = slice(P_REQ * PLEN, P_REQ * PLEN + PLEN)
    carry = (jnp.full(wide, -1e30, F32), jnp.zeros(wide, F32), jnp.zeros(wide, F32))
    carry = first(NT, kq_ref[...], vq_ref[...], own, True, carry)
    for copy in copies:
        copy.wait()

    def step(t, carry):
        rows = pl.ds(pl.multiple_of(t * TK, TK), TK)
        keys = kbuf[rows, :]
        ktbuf[t] = keys.T
        return first(t, keys, vbuf[rows, :], rows, False, carry)

    m, l, num = lax.fori_loop(0, NT, step, carry)
    inv = 1.0 / l
    delta = num * inv

    def second(t, kt, rows, out_rows, acc):
        scale = jnp.exp2((mt[t] - m) * C2) * inv
        gk = gv = None
        for b in range(G * PLEN // CB):
            cols = slice(b * CB, (b + 1) * CB)
            p = ebuf[rows, cols] * scale[:, cols]
            ds = (p * (dpbuf[rows, cols] - delta[:, cols])).astype(BF16)
            dk = dot(ds, qs[cols, :])
            dv = dot(p.astype(BF16), dos[cols, :])
            gk = dk if gk is None else gk + dk
            gv = dv if gv is None else gv + dv
            more = dot(kt, ds)
            dqt[:, cols] = dqt[:, cols] + more if acc else more
        return (gk * C).astype(BF16), gv.astype(BF16)

    gk, gv = second(NT, kq_ref[...].T, own, None, False)
    gk_ref[...] = gk
    gv_ref[...] = gv

    def back(t, c):
        rows = pl.ds(pl.multiple_of(t * TK, TK), TK)
        gk, gv = second(t, ktbuf[t], rows, rows, True)
        gkbuf[rows, :] = gk
        gvbuf[rows, :] = gv
        for i in range(TK // PLEN):
            j = t * (TK // PLEN) + i
            part = pl.ds(pl.multiple_of(j * PLEN, PLEN), PLEN)
            slot = slots[j]
            pltpu.make_async_copy(gkbuf.at[part], full_ref.at[slot, 0, :, cols], out_sem.at[0]).start()
            pltpu.make_async_copy(gvbuf.at[part], full_ref.at[slot, 1, :, cols], out_sem.at[1]).start()
        return c

    lax.fori_loop(0, NT, back, 0)
    for g in range(G):
        dq_ref[:, g * D:(g + 1) * D] = (dqt[:, g * PLEN:(g + 1) * PLEN] * C).T.astype(BF16)

    def drain(j, c):
        rows = pl.ds(pl.multiple_of(j * PLEN, PLEN), PLEN)
        pltpu.make_async_copy(gkbuf.at[rows], full_ref.at[slots[j], 0, :, cols], out_sem.at[0]).wait()
        pltpu.make_async_copy(gvbuf.at[rows], full_ref.at[slots[j], 1, :, cols], out_sem.at[1]).wait()
        return c

    lax.fori_loop(0, P_REQ, drain, 0)

    @pl.when(h == KV - 1)
    def _():
        def blanked(i, c):
            @pl.when(mask[i] == 0)
            def _():
                pltpu.make_async_copy(zeros, full_ref.at[i], zero_sem).wait()

            return c

        lax.fori_loop(0, NPSG, blanked, 0)


def qry_back(req, slot, owner, kvg, q, do, kq, vq, me):
    keys = P_REQ * PLEN + PLEN
    wide = pl.BlockSpec((PLEN, G * D), lambda h: (0, h))
    thin = pl.BlockSpec((PLEN, D), lambda h: (0, h))
    smem = pl.BlockSpec(memory_space=pltpu.SMEM)
    hbm = pl.BlockSpec(memory_space=pl.ANY)
    return pl.pallas_call(
        qry_kernel,
        grid=(KV,),
        in_specs=[smem, smem, smem, hbm, wide, wide, thin, thin, smem],
        out_specs=[wide, thin, thin, hbm],
        out_shape=[
            jax.ShapeDtypeStruct(q.shape, BF16),
            jax.ShapeDtypeStruct(kq.shape, BF16),
            jax.ShapeDtypeStruct(vq.shape, BF16),
            jax.ShapeDtypeStruct((NPSG, 2, PLEN, KV * D), BF16),
        ],
        scratch_shapes=[
            pltpu.VMEM((G * PLEN, D), BF16),
            pltpu.VMEM((G * PLEN, D), BF16),
            pltpu.VMEM((D, G * PLEN), BF16),
            pltpu.VMEM((D, G * PLEN), BF16),
            pltpu.VMEM((P_REQ * PLEN, D), BF16),
            pltpu.VMEM((P_REQ * PLEN, D), BF16),
            pltpu.VMEM((NT, D, TK), BF16),
            pltpu.VMEM((keys, G * PLEN), F32),
            pltpu.VMEM((keys, G * PLEN), F32),
            pltpu.VMEM((NT + 1, 1, G * PLEN), F32),
            pltpu.VMEM((D, G * PLEN), F32),
            pltpu.VMEM((P_REQ * PLEN, D), BF16),
            pltpu.VMEM((P_REQ * PLEN, D), BF16),
            pltpu.VMEM((2, PLEN, KV * D), BF16),
            pltpu.SMEM((P_REQ,), jnp.int32),
            pltpu.SMEM((NPSG,), jnp.int32),
            pltpu.SemaphoreType.DMA((2,)),
            pltpu.SemaphoreType.DMA((2,)),
            pltpu.SemaphoreType.DMA,
        ],
        compiler_params=pltpu.CompilerParams(vmem_limit_bytes=48 * 1024 * 1024),
        cost_estimate=pl.CostEstimate(flops=2 * 5 * 2 * 1024 * 2176 * 128, bytes_accessed=16 * 1024 * 1024, transcendentals=2 * 1024 * 2176),
        name="qry_back",
    )(req, slot, owner, kvg, q, do, kq, vq, me)


WB = 1024


def term_kernel(k_ref, v_ref, wk_ref, wv_ref, out_ref):
    out_ref[...] = (dot_t(k_ref[...], wk_ref[...]) + dot_t(v_ref[...], wv_ref[...])).astype(BF16)


def term(rows_k, rows_v, w_key, w_value):
    rows = rows_k.shape[0]
    width, depth = w_key.shape
    return pl.pallas_call(
        term_kernel,
        grid=(width // WB,),
        in_specs=[
            pl.BlockSpec((rows, depth), lambda i: (0, 0)),
            pl.BlockSpec((rows, depth), lambda i: (0, 0)),
            pl.BlockSpec((WB, depth), lambda i: (i, 0)),
            pl.BlockSpec((WB, depth), lambda i: (i, 0)),
        ],
        out_specs=pl.BlockSpec((rows, WB), lambda i: (0, i)),
        out_shape=jax.ShapeDtypeStruct((rows, width), BF16),
        compiler_params=pltpu.CompilerParams(vmem_limit_bytes=32 * 1024 * 1024),
        cost_estimate=pl.CostEstimate(flops=4 * rows * width * depth, bytes_accessed=4 * width * depth + 2 * rows * width, transcendentals=0),
        name="term",
    )(rows_k, rows_v, w_key, w_value)


MESH = pl.DeviceIdType.MESH


def place():
    me = lax.axis_index("psg")
    return me // 8, lax.rem(me // 2, 4), lax.rem(me, 2)


def at_plane(z, x, c):
    return {"psg": (z * 4 + x) * 2 + c}


def turn(i, by):
    return lax.rem(i + by + 4, 4)


def greet(devices):
    barrier = pltpu.get_barrier_semaphore()
    for device in devices:
        pl.semaphore_signal(barrier, inc=1, device_id=device, device_id_type=MESH)
    pl.semaphore_wait(barrier, len(devices))


def plane_neighbours(z, x, c):
    return [
        at_plane(turn(z, 1), x, c),
        at_plane(turn(z, -1), x, c),
        at_plane(z, turn(x, 1), c),
        at_plane(z, turn(x, -1), c),
        at_plane(z, x, 1 - c),
    ]


class Sender:
    def __init__(self, sems):
        self.sems = sems
        self.started = []

    def __call__(self, src, dst, recv_sem, device):
        copy = pltpu.make_async_remote_copy(
            src_ref=src, dst_ref=dst, send_sem=self.sems.at[len(self.started)], recv_sem=recv_sem,
            device_id=device, device_id_type=MESH,
        )
        copy.start()
        self.started.append(copy)

    def finish(self):
        for copy in self.started:
            copy.wait_send()


def arrived(ref, sem):
    pltpu.make_async_copy(ref, ref, sem).wait()


def gather_kernel(k_ref, v_ref, all_ref, send_sem, recv_sem, core_sem, local_sem):
    z, x, c = place()
    greet(plane_neighbours(z, x, c))
    send = Sender(send_sem)
    half = k_ref.shape[0] // 2
    own = [(z, x), (x, z)]
    copies = []
    for n in range(2):
        a, b = own[n]
        for part, ref in enumerate((k_ref, v_ref)):
            copies.append(pltpu.make_async_copy(ref.at[pl.ds(n * half, half)], all_ref.at[n, c, a, b, part], local_sem.at[n, part]))
    for copy in copies:
        copy.start()
    for copy in copies:
        copy.wait()

    def device(n, a, b, core):
        return at_plane(a, b, core) if n == 0 else at_plane(b, a, core)

    def whole(n, a, b, to):
        block = all_ref.at[n, c, a, b]
        send(block, block, recv_sem.at[0, n, a, b], to)

    def piece(n, a, b, part, to):
        block = all_ref.at[n, c, a, b, part]
        send(block, block, recv_sem.at[part, n, a, b], to)

    def core(n, a, b):
        block = all_ref.at[n, c, a, b]
        send(block, block, core_sem.at[n, a, b], device(n, own[n][0], own[n][1], 1 - c))

    def wait_whole(n, a, b):
        arrived(all_ref.at[n, c, a, b], recv_sem.at[0, n, a, b])

    def wait_pieces(n, a, b):
        for part in range(2):
            arrived(all_ref.at[n, c, a, b, part], recv_sem.at[part, n, a, b])

    def along_a(n, a, b):
        for by in (1, -1):
            whole(n, a, b, device(n, turn(a, by), own[n][1], c))

    for n in range(2):
        a, b = own[n]
        for by in (1, -1):
            whole(n, a, b, device(n, a, turn(b, by), c))
        along_a(n, a, b)
    for n in range(2):
        core(n, *own[n])
    for by, part in ((-1, 0), (1, 1)):
        for n in range(2):
            a, b = own[n]
            o = turn(b, by)
            wait_whole(n, a, o)
            piece(n, a, o, part, device(n, a, turn(b, -by), c))
            along_a(n, a, o)
            core(n, a, o)
    def far(n, bo):
        a, b = own[n]
        col = turn(b, bo)
        for by, part in ((-1, 0), (1, 1)):
            o = turn(a, by)
            wait_whole(n, o, col)
            piece(n, o, col, part, device(n, turn(a, -by), b, c))
            core(n, o, col)

    for n in range(2):
        far(n, 0)
    for n in range(2):
        a, b = own[n]
        o = turn(b, 2)
        wait_pieces(n, a, o)
        along_a(n, a, o)
        core(n, a, o)
    for bo in (-1, 1, 2):
        for n in range(2):
            far(n, bo)
    for bo in (0, -1, 1, 2):
        for n in range(2):
            a, b = own[n]
            o, col = turn(a, 2), turn(b, bo)
            wait_pieces(n, o, col)
            core(n, o, col)
    for n in range(2):
        for a in range(4):
            for b in range(4):
                arrived(all_ref.at[n, 1 - c, a, b], core_sem.at[n, a, b])
    send.finish()


def gather_plane(k, v):
    rows, cols = k.shape
    hbm = pl.BlockSpec(memory_space=pl.ANY)
    return pl.pallas_call(
        gather_kernel,
        in_specs=[hbm, hbm],
        out_specs=hbm,
        out_shape=jax.ShapeDtypeStruct((2, 2, 4, 4, 2, rows // 2, cols), BF16),
        scratch_shapes=[
            pltpu.SemaphoreType.DMA((72,)),
            pltpu.SemaphoreType.DMA((2, 2, 4, 4)),
            pltpu.SemaphoreType.DMA((2, 4, 4)),
            pltpu.SemaphoreType.DMA((2, 2)),
        ],
        compiler_params=pltpu.CompilerParams(collective_id=0, has_side_effects=True),
        name="gather_plane",
    )(k, v)


def add(x, y):
    return (x.astype(F32) + y.astype(F32)).astype(BF16)


def reduce_kernel(
    full_ref, own_k_ref, own_v_ref, gk_ref, gv_ref,
    mine, other, relay1, side1, part, relay2, side2,
    send_sem, core_sem, relay1_sem, side1_sem, relay2_sem, side2_sem, local_sem,
):
    z, x, c = place()
    own = [(z, x), (x, z)]

    def device(n, a, b, core):
        return at_plane(a, b, core) if n == 0 else at_plane(b, a, core)

    loads = {}
    for by in (2, 1, -1, 0):
        for n in range(2):
            a = turn(own[n][0], by)
            loads[n, by] = pltpu.make_async_copy(full_ref.at[n, c, a], mine.at[n, a], local_sem.at[n, a])
            loads[n, by].start()
    greet(plane_neighbours(z, x, c))
    send = Sender(send_sem)
    for by in (2, 1, -1, 0):
        for n in range(2):
            a = turn(own[n][0], by)
            send(full_ref.at[n, 1 - c, a], other.at[n, a], core_sem.at[n, a], device(n, *own[n], 1 - c))

    def pair(n, by):
        a = turn(own[n][0], by)
        loads[n, by].wait()
        arrived(other.at[n, a], core_sem.at[n, a])
        mine[n, a] = add(mine[n, a], other[n, a])
        return a

    halves = (pl.ds(0, 2), pl.ds(2, 2))
    steps = (1, -1)
    for n in range(2):
        a = pair(n, 2)
        for s in range(2):
            to = device(n, turn(own[n][0], steps[s]), own[n][1], c)
            send(mine.at[n, a, halves[s]], relay1.at[n, s], relay1_sem.at[n, s], to)
    for s in range(2):
        for n in range(2):
            a = pair(n, steps[s])
            to = device(n, a, own[n][1], c)
            send(mine.at[n, a, halves[1 - s]], side1.at[n, s, halves[1 - s]], side1_sem.at[n, s, 1 - s], to)
    for s in range(2):
        for n in range(2):
            a = turn(own[n][0], steps[s])
            to = device(n, a, own[n][1], c)
            arrived(relay1.at[n, s], relay1_sem.at[n, s])
            mine[n, a, halves[s]] = add(mine[n, a, halves[s]], relay1[n, s])
            send(mine.at[n, a, halves[s]], side1.at[n, s, halves[s]], side1_sem.at[n, s, s], to)
    for n in range(2):
        pair(n, 0)

    def join1(n, b):
        a = own[n][0]
        total = mine[n, a, b].astype(F32)
        for s in range(2):
            total = total + side1[n, s, b].astype(F32)
        part[n, b] = total.astype(BF16)

    for n in range(2):
        a, b = own[n]
        for s in range(2):
            for t in range(2):
                arrived(side1.at[n, s, halves[t]], side1_sem.at[n, s, t])
        far = turn(b, 2)
        join1(n, far)
        for s in range(2):
            send(part.at[n, far, s], relay2.at[n, s], relay2_sem.at[n, s], device(n, a, turn(b, steps[s]), c))
        for s in range(2):
            near = turn(b, steps[s])
            join1(n, near)
            send(part.at[n, near, 1 - s], side2.at[n, s, 1 - s], side2_sem.at[n, s, 1 - s], device(n, a, near, c))
        join1(n, b)
    for n in range(2):
        a, b = own[n]
        for s in range(2):
            near = turn(b, steps[s])
            arrived(relay2.at[n, s], relay2_sem.at[n, s])
            part[n, near, s] = add(part[n, near, s], relay2[n, s])
            send(part.at[n, near, s], side2.at[n, s, s], side2_sem.at[n, s, s], device(n, a, near, c))
    half = own_k_ref.shape[0] // 2
    for n in range(2):
        rows = slice(n * half, (n + 1) * half)
        for t, (own_ref, out_ref) in enumerate(((own_k_ref, gk_ref), (own_v_ref, gv_ref))):
            total = own_ref[rows, :] + part[n, own[n][1], t].astype(F32)
            for s in range(2):
                arrived(side2.at[n, s, t], side2_sem.at[n, s, t])
                total = total + side2[n, s, t].astype(F32)
            out_ref[rows, :] = total.astype(BF16)
    send.finish()


def reduce_plane(full, own_k, own_v):
    rows, cols = own_k.shape
    half = rows // 2
    hbm = pl.BlockSpec(memory_space=pl.ANY)
    vmem = pl.BlockSpec(memory_space=pltpu.VMEM)
    dma = pltpu.SemaphoreType.DMA
    block = (2, half, cols)
    return pl.pallas_call(
        reduce_kernel,
        in_specs=[hbm, vmem, vmem],
        out_specs=[vmem, vmem],
        out_shape=[jax.ShapeDtypeStruct((rows, cols), BF16)] * 2,
        scratch_shapes=[
            pltpu.VMEM((2, 4, 4) + block, BF16),
            pltpu.VMEM((2, 4, 4) + block, BF16),
            pltpu.VMEM((2, 2, 2) + block, BF16),
            pltpu.VMEM((2, 2, 4) + block, BF16),
            pltpu.VMEM((2, 4) + block, BF16),
            pltpu.VMEM((2, 2, half, cols), BF16),
            pltpu.VMEM((2, 2) + block, BF16),
            dma((32,)),
            dma((2, 4)),
            dma((2, 2)),
            dma((2, 2, 2)),
            dma((2, 2)),
            dma((2, 2, 2)),
            dma((2, 4)),
        ],
        compiler_params=pltpu.CompilerParams(collective_id=1, has_side_effects=True, vmem_limit_bytes=40 * 1024 * 1024),
        name="reduce_plane",
    )(full, own_k, own_v)


def local(q_psg, k_psg, v_psg, do_psg, q_qry, k_qry, v_qry, do_qry, w_key, w_value, req_passages, passage_slot, query_owner):
    me = lax.axis_index("psg").astype(jnp.int32).reshape(1)
    every = gather_plane(k_psg, v_psg)
    dq_psg, own_k, own_v = psg_back(q_psg, k_psg, v_psg, do_psg)
    dq_qry, gk_qry, gv_qry, full = qry_back(
        req_passages, passage_slot, query_owner, every.reshape(NPSG, 2, PLEN, -1), q_qry, do_qry, k_qry, v_qry, me
    )
    dx_qry = lax.psum_scatter(term(gk_qry, gv_qry, w_key, w_value), "head", scatter_dimension=0, tiled=True)
    gk, gv = reduce_plane(full.reshape(every.shape), own_k, own_v)
    dx_psg = lax.psum_scatter(term(gk, gv, w_key, w_value), "head", scatter_dimension=0, tiled=True)
    return dq_psg, dq_qry, dx_psg, dx_qry


def solution(mesh):
    rows = P("psg", "head")
    return jax.shard_map(
        local,
        mesh=mesh,
        in_specs=(rows,) * 8 + (P(None, "head"),) * 2 + (P(),) * 3,
        out_specs=(rows, rows, P(("psg", "head"), None), P(("psg", "head"), None)),
        check_vma=False,
    )
```

```python
import functools

import jax
import jax.numpy as jnp
from jax import lax
from jax.experimental import pallas as pl
from jax.experimental.pallas import tpu as pltpu
from jax.sharding import PartitionSpec as P

D = 128
G = 8
PLEN = 128
KV = 2
NPSG = 64
REQ = 32
P_REQ = 16
CB = 256
C = D ** -0.5
C2 = C * 1.4426950408889634
F32 = jnp.float32
BF16 = jnp.bfloat16


def stack(x):
    return jnp.concatenate([x[:, g * D:(g + 1) * D] for g in range(G)], axis=0)


def dot(a, b):
    return jnp.dot(a, b, preferred_element_type=F32)


def dot_t(a, b):
    return lax.dot_general(a, b, (((1,), (1,)), ((), ())), preferred_element_type=F32)


def causal_cols(shape):
    key = lax.broadcasted_iota(jnp.int32, shape, 0)
    qry = lax.broadcasted_iota(jnp.int32, shape, 1) % PLEN
    return key <= qry


def psg_kernel(q_ref, k_ref, v_ref, do_ref, dq_ref, gk_ref, gv_ref):
    qs = stack(q_ref[...])
    dos = stack(do_ref[...])
    k = k_ref[...]
    v = v_ref[...]
    kt = k.T
    gk = jnp.zeros((PLEN, D), F32)
    gv = jnp.zeros((PLEN, D), F32)
    for b in range(G * PLEN // CB):
        cols = slice(b * CB, (b + 1) * CB)
        s = dot_t(k, qs[cols])
        s = jnp.where(causal_cols(s.shape), s, -1e30)
        e = jnp.exp2((s - jnp.max(s, axis=0, keepdims=True)) * C2)
        inv = 1.0 / jnp.sum(e, axis=0, keepdims=True)
        dp = dot_t(v, dos[cols])
        p = e * inv
        delta = jnp.sum(p * dp, axis=0, keepdims=True)
        ds = (p * (dp - delta)).astype(BF16)
        gk += dot(ds, qs[cols])
        gv += dot(p.astype(BF16), dos[cols])
        dqt = dot(kt, ds) * C
        for i in range(CB // PLEN):
            g = b * (CB // PLEN) + i
            dq_ref[:, g * D:(g + 1) * D] = dqt[:, i * PLEN:(i + 1) * PLEN].T.astype(BF16)
    gk_ref[...] = gk * C
    gv_ref[...] = gv


def psg_back(q, k, v, do):
    rows = q.shape[0]
    wide = pl.BlockSpec((PLEN, G * D), lambda n, h: (n, h))
    thin = pl.BlockSpec((PLEN, D), lambda n, h: (n, h))
    return pl.pallas_call(
        psg_kernel,
        grid=(rows // PLEN, KV),
        in_specs=[wide, thin, thin, wide],
        out_specs=[wide, thin, thin],
        out_shape=[
            jax.ShapeDtypeStruct(q.shape, BF16),
            jax.ShapeDtypeStruct(k.shape, F32),
            jax.ShapeDtypeStruct(v.shape, F32),
        ],
        compiler_params=pltpu.CompilerParams(vmem_limit_bytes=40 * 1024 * 1024),
        cost_estimate=pl.CostEstimate(flops=4 * 5 * 2 * 1024 * 128 * 128, bytes_accessed=4 * 1024 * 1024, transcendentals=4 * 1024 * 128),
        name="psg_back",
    )(q, k, v, do)


TK = 256
NT = P_REQ * PLEN // TK


def spot(slot):
    n = slot % 2
    c = slot // 2 % 2
    x = slot // 4 % 4
    z = slot // 16
    return n * 32 + jnp.where(n == 0, z * 4 + x, x * 4 + z) * 2 + c


def qry_kernel(
    req_ref, slot_ref, owner_ref, kvg_ref, q_ref, do_ref, kq_ref, vq_ref, me_ref,
    dq_ref, gk_ref, gv_ref, full_ref,
    qs, dos, qst, dost, kbuf, vbuf, ktbuf, ebuf, dpbuf, mt, dqt, gkbuf, gvbuf, zeros, slots, mask,
    in_sem, out_sem, zero_sem,
):
    h = pl.program_id(0)
    me = me_ref[0]

    @pl.when(h == 0)
    def _():
        zeros[...] = jnp.zeros_like(zeros)
        request = jnp.int32(0)
        for r in range(REQ):
            request = jnp.where(owner_ref[r] == me, r, request)

        def clear(i, c):
            mask[i] = 0
            return c

        lax.fori_loop(0, NPSG, clear, 0)

        def pick(j, c):
            slot = spot(slot_ref[req_ref[request, j]])
            slots[j] = slot
            mask[slot] = 1
            return c

        lax.fori_loop(0, P_REQ, pick, 0)

        def blank(i, c):
            @pl.when(mask[i] == 0)
            def _():
                pltpu.make_async_copy(zeros, full_ref.at[i], zero_sem).start()

            return c

        lax.fori_loop(0, NPSG, blank, 0)

    cols = pl.ds(pl.multiple_of(h * D, D), D)
    copies = []
    for j in range(P_REQ):
        rows = pl.ds(j * PLEN, PLEN)
        copies.append(pltpu.make_async_copy(kvg_ref.at[slots[j], 0, :, cols], kbuf.at[rows], in_sem.at[0]))
        copies.append(pltpu.make_async_copy(kvg_ref.at[slots[j], 1, :, cols], vbuf.at[rows], in_sem.at[1]))
    for copy in copies:
        copy.start()
    qs[...] = stack(q_ref[...])
    dos[...] = stack(do_ref[...])
    qst[...] = qs[...].T
    dost[...] = dos[...].T

    def first(t, keys, values, rows, masked, carry):
        m, l, num = carry
        ms, ls, nums = [], [], []
        for b in range(G * PLEN // CB):
            cols = slice(b * CB, (b + 1) * CB)
            s = dot(keys, qst[:, cols])
            if masked:
                s = jnp.where(causal_cols(s.shape), s, -1e30)
            m_old = m[:, cols]
            m_new = jnp.maximum(m_old, jnp.max(s, axis=0, keepdims=True))
            alpha = jnp.exp2((m_old - m_new) * C2)
            e = jnp.exp2((s - m_new) * C2)
            dp = dot(values, dost[:, cols])
            ebuf[rows, cols] = e
            dpbuf[rows, cols] = dp
            ms.append(m_new)
            ls.append(l[:, cols] * alpha + jnp.sum(e, axis=0, keepdims=True))
            nums.append(num[:, cols] * alpha + jnp.sum(e * dp, axis=0, keepdims=True))
        m = jnp.concatenate(ms, axis=1)
        mt[t] = m
        return m, jnp.concatenate(ls, axis=1), jnp.concatenate(nums, axis=1)

    wide = (1, G * PLEN)
    own = slice(P_REQ * PLEN, P_REQ * PLEN + PLEN)
    carry = (jnp.full(wide, -1e30, F32), jnp.zeros(wide, F32), jnp.zeros(wide, F32))
    carry = first(NT, kq_ref[...], vq_ref[...], own, True, carry)
    for copy in copies:
        copy.wait()

    def step(t, carry):
        rows = pl.ds(pl.multiple_of(t * TK, TK), TK)
        keys = kbuf[rows, :]
        ktbuf[t] = keys.T
        return first(t, keys, vbuf[rows, :], rows, False, carry)

    m, l, num = lax.fori_loop(0, NT, step, carry)
    inv = 1.0 / l
    delta = num * inv

    def second(t, kt, rows, out_rows, acc):
        scale = jnp.exp2((mt[t] - m) * C2) * inv
        gk = gv = None
        for b in range(G * PLEN // CB):
            cols = slice(b * CB, (b + 1) * CB)
            p = ebuf[rows, cols] * scale[:, cols]
            ds = (p * (dpbuf[rows, cols] - delta[:, cols])).astype(BF16)
            dk = dot(ds, qs[cols, :])
            dv = dot(p.astype(BF16), dos[cols, :])
            gk = dk if gk is None else gk + dk
            gv = dv if gv is None else gv + dv
            more = dot(kt, ds)
            dqt[:, cols] = dqt[:, cols] + more if acc else more
        return (gk * C).astype(BF16), gv.astype(BF16)

    gk, gv = second(NT, kq_ref[...].T, own, None, False)
    gk_ref[...] = gk
    gv_ref[...] = gv

    def back(t, c):
        rows = pl.ds(pl.multiple_of(t * TK, TK), TK)
        gk, gv = second(t, ktbuf[t], rows, rows, True)
        gkbuf[rows, :] = gk
        gvbuf[rows, :] = gv
        for i in range(TK // PLEN):
            j = t * (TK // PLEN) + i
            part = pl.ds(pl.multiple_of(j * PLEN, PLEN), PLEN)
            slot = slots[j]
            pltpu.make_async_copy(gkbuf.at[part], full_ref.at[slot, 0, :, cols], out_sem.at[0]).start()
            pltpu.make_async_copy(gvbuf.at[part], full_ref.at[slot, 1, :, cols], out_sem.at[1]).start()
        return c

    lax.fori_loop(0, NT, back, 0)
    for g in range(G):
        dq_ref[:, g * D:(g + 1) * D] = (dqt[:, g * PLEN:(g + 1) * PLEN] * C).T.astype(BF16)

    def drain(j, c):
        rows = pl.ds(pl.multiple_of(j * PLEN, PLEN), PLEN)
        pltpu.make_async_copy(gkbuf.at[rows], full_ref.at[slots[j], 0, :, cols], out_sem.at[0]).wait()
        pltpu.make_async_copy(gvbuf.at[rows], full_ref.at[slots[j], 1, :, cols], out_sem.at[1]).wait()
        return c

    lax.fori_loop(0, P_REQ, drain, 0)

    @pl.when(h == KV - 1)
    def _():
        def blanked(i, c):
            @pl.when(mask[i] == 0)
            def _():
                pltpu.make_async_copy(zeros, full_ref.at[i], zero_sem).wait()

            return c

        lax.fori_loop(0, NPSG, blanked, 0)


def qry_back(req, slot, owner, kvg, q, do, kq, vq, me):
    keys = P_REQ * PLEN + PLEN
    wide = pl.BlockSpec((PLEN, G * D), lambda h: (0, h))
    thin = pl.BlockSpec((PLEN, D), lambda h: (0, h))
    smem = pl.BlockSpec(memory_space=pltpu.SMEM)
    hbm = pl.BlockSpec(memory_space=pl.ANY)
    return pl.pallas_call(
        qry_kernel,
        grid=(KV,),
        in_specs=[smem, smem, smem, hbm, wide, wide, thin, thin, smem],
        out_specs=[wide, thin, thin, hbm],
        out_shape=[
            jax.ShapeDtypeStruct(q.shape, BF16),
            jax.ShapeDtypeStruct(kq.shape, BF16),
            jax.ShapeDtypeStruct(vq.shape, BF16),
            jax.ShapeDtypeStruct((NPSG, 2, PLEN, KV * D), BF16),
        ],
        scratch_shapes=[
            pltpu.VMEM((G * PLEN, D), BF16),
            pltpu.VMEM((G * PLEN, D), BF16),
            pltpu.VMEM((D, G * PLEN), BF16),
            pltpu.VMEM((D, G * PLEN), BF16),
            pltpu.VMEM((P_REQ * PLEN, D), BF16),
            pltpu.VMEM((P_REQ * PLEN, D), BF16),
            pltpu.VMEM((NT, D, TK), BF16),
            pltpu.VMEM((keys, G * PLEN), F32),
            pltpu.VMEM((keys, G * PLEN), F32),
            pltpu.VMEM((NT + 1, 1, G * PLEN), F32),
            pltpu.VMEM((D, G * PLEN), F32),
            pltpu.VMEM((P_REQ * PLEN, D), BF16),
            pltpu.VMEM((P_REQ * PLEN, D), BF16),
            pltpu.VMEM((2, PLEN, KV * D), BF16),
            pltpu.SMEM((P_REQ,), jnp.int32),
            pltpu.SMEM((NPSG,), jnp.int32),
            pltpu.SemaphoreType.DMA((2,)),
            pltpu.SemaphoreType.DMA((2,)),
            pltpu.SemaphoreType.DMA,
        ],
        compiler_params=pltpu.CompilerParams(vmem_limit_bytes=48 * 1024 * 1024),
        cost_estimate=pl.CostEstimate(flops=2 * 5 * 2 * 1024 * 2176 * 128, bytes_accessed=16 * 1024 * 1024, transcendentals=2 * 1024 * 2176),
        name="qry_back",
    )(req, slot, owner, kvg, q, do, kq, vq, me)


MESH = pl.DeviceIdType.MESH


def place():
    me = lax.axis_index("psg")
    return me // 8, lax.rem(me // 2, 4), lax.rem(me, 2)


def at_plane(z, x, c):
    return {"psg": (z * 4 + x) * 2 + c}


def turn(i, by):
    return lax.rem(i + by + 4, 4)


def greet(devices):
    barrier = pltpu.get_barrier_semaphore()
    for device in devices:
        pl.semaphore_signal(barrier, inc=1, device_id=device, device_id_type=MESH)
    pl.semaphore_wait(barrier, len(devices))


def plane_neighbours(z, x, c):
    return [
        at_plane(turn(z, 1), x, c),
        at_plane(turn(z, -1), x, c),
        at_plane(z, turn(x, 1), c),
        at_plane(z, turn(x, -1), c),
        at_plane(z, x, 1 - c),
    ]


class Sender:
    def __init__(self, sems):
        self.sems = sems
        self.started = []

    def __call__(self, src, dst, recv_sem, device):
        copy = pltpu.make_async_remote_copy(
            src_ref=src, dst_ref=dst, send_sem=self.sems.at[len(self.started)], recv_sem=recv_sem,
            device_id=device, device_id_type=MESH,
        )
        copy.start()
        self.started.append(copy)

    def finish(self):
        for copy in self.started:
            copy.wait_send()


def arrived(ref, sem):
    pltpu.make_async_copy(ref, ref, sem).wait()


def lane_device(a, b, c):
    return at_plane(a * (1 - c) + b * c, b * (1 - c) + a * c, c)


def gather_kernel(
    k_ref, v_ref, wk_ref, wv_ref, all_ref, near_ref, far_ref,
    send_sem, recv_sem, core_sem, local_sem, swap_sem, near_sem, near_core_sem, far_sem,
):
    z, x, c = place()
    y = lax.axis_index("head")
    a = z * (1 - c) + x * c
    b = x * (1 - c) + z * c
    half = k_ref.shape[0] // 2
    share = far_ref.shape[1]
    refs = (k_ref, v_ref)
    weights = (wk_ref, wv_ref)
    mine = [pltpu.make_async_copy(ref.at[pl.ds(c * half, half)], all_ref.at[c, a, b, c, i], local_sem.at[i]) for i, ref in enumerate(refs)]
    for copy in mine:
        copy.start()
    greet(plane_neighbours(z, x, c) + [{"head": turn(y, 1)}, {"head": turn(y, -1)}])
    send = Sender(send_sem)
    partner = at_plane(z, x, 1 - c)
    for i, ref in enumerate(refs):
        send(ref.at[pl.ds((1 - c) * half, half)], all_ref.at[1 - c, b, a, c, i], swap_sem.at[i], partner)

    def columns(head):
        return pl.ds((2 * head + c) * share, share)

    for i, ref in enumerate(weights):
        for s, by in ((1, 1), (0, -1)):
            to = turn(y, by)
            send(ref.at[columns(to)], near_ref.at[s, i, pl.ds(c * share, share)], near_sem.at[s, i], {"head": to})
    for copy in mine:
        copy.wait()
    for i in range(2):
        arrived(all_ref.at[c, a, b, 1 - c, i], swap_sem.at[i])

    def whole(i, j, to):
        block = all_ref.at[c, i, j]
        send(block, block, recv_sem.at[0, i, j], to)

    def piece(i, j, part, to):
        block = all_ref.at[c, i, j, part]
        send(block, block, recv_sem.at[part, i, j], to)

    def core(i, j):
        block = all_ref.at[c, i, j]
        send(block, block, core_sem.at[i, j], partner)

    def wait_whole(i, j):
        arrived(all_ref.at[c, i, j], recv_sem.at[0, i, j])

    def wait_pieces(i, j):
        for part in range(2):
            arrived(all_ref.at[c, i, j, part], recv_sem.at[part, i, j])

    def along_a(i, j):
        for by in (1, -1):
            whole(i, j, lane_device(turn(a, by), b, c))

    ways = ((-1, 0), (1, 1))
    for by in (1, -1):
        whole(a, b, lane_device(a, turn(b, by), c))
    along_a(a, b)
    across = [pltpu.make_async_copy(ref.at[columns(turn(y, 2))], far_ref.at[i], far_sem.at[i]) for i, ref in enumerate(weights)]
    for copy in across:
        copy.start()
    for by, part in ways:
        j = turn(b, by)
        wait_whole(a, j)
        piece(a, j, part, lane_device(a, turn(b, -by), c))
    for by, part in ways:
        along_a(a, turn(b, by))

    def far(bo):
        j = turn(b, bo)
        for by, part in ways:
            i = turn(a, by)
            wait_whole(i, j)
            piece(i, j, part, lane_device(turn(a, -by), b, c))

    far(0)
    wait_pieces(a, turn(b, 2))
    along_a(a, turn(b, 2))
    for bo in (0, -1, 1, 2):
        core(a, turn(b, bo))
    for by, _ in ways:
        core(turn(a, by), b)
    for bo in (-1, 1, 2):
        far(bo)
        for by, _ in ways:
            core(turn(a, by), turn(b, bo))
    for s in range(2):
        for i in range(2):
            block = near_ref.at[s, i, pl.ds(c * share, share)]
            arrived(block, near_sem.at[s, i])
            send(block, block, near_core_sem.at[s, i], partner)
    for bo in (0, -1, 1, 2):
        wait_pieces(turn(a, 2), turn(b, bo))
        core(turn(a, 2), turn(b, bo))
    for i in range(4):
        for j in range(4):
            arrived(all_ref.at[1 - c, i, j], core_sem.at[i, j])
    for s in range(2):
        for i in range(2):
            arrived(near_ref.at[s, i, pl.ds((1 - c) * share, share)], near_core_sem.at[s, i])
    for copy in across:
        copy.wait()
    send.finish()


def gather_plane(k, v, w_key, w_value):
    rows, cols = k.shape
    width, depth = w_key.shape
    share = width // 8
    hbm = pl.BlockSpec(memory_space=pl.ANY)
    dma = pltpu.SemaphoreType.DMA
    return pl.pallas_call(
        gather_kernel,
        in_specs=[hbm] * 4,
        out_specs=[hbm] * 3,
        out_shape=[
            jax.ShapeDtypeStruct((2, 4, 4, 2, 2, rows // 2, cols), BF16),
            jax.ShapeDtypeStruct((2, 2, 2 * share, depth), BF16),
            jax.ShapeDtypeStruct((2, share, depth), BF16),
        ],
        scratch_shapes=[dma((46,)), dma((2, 4, 4)), dma((4, 4)), dma((2,)), dma((2,)), dma((2, 2)), dma((2, 2)), dma((2,))],
        compiler_params=pltpu.CompilerParams(collective_id=0, has_side_effects=True),
        name="gather_plane",
    )(k, v, w_key, w_value)


JOBS = 3


def tail_kernel(
    full_ref, own_k_ref, own_v_ref, qk_ref, qv_ref, wk_ref, wv_ref, near_ref, far_ref, dx_psg_ref, dx_qry_ref,
    mine, other, relay1, side1, part, relay2, side2, stage, swap, rows, weights, acc, terms,
    send_sem, core_sem, relay1_sem, side1_sem, relay2_sem, side2_sem, swap_sem, local_sem,
    load_sem, far_sem, rows_sem, out_sem,
):
    z, x, c = place()
    y = lax.axis_index("head")
    a = z * (1 - c) + x * c
    b = x * (1 - c) + z * c
    partner = at_plane(z, x, 1 - c)
    steps = (1, -1)
    halves = (pl.ds(0, 2), pl.ds(2, 2))
    quarter = dx_qry_ref.shape[0]
    width = dx_qry_ref.shape[1] // 4
    share = width // 2
    heads = [y, turn(y, 1), turn(y, -1), turn(y, 2)]
    mirror = (0, 2, 1, 3)

    loads = {}
    for q in range(2):
        for by in (2, 1, -1, 0):
            i = turn(a, by)
            loads[q, by] = pltpu.make_async_copy(full_ref.at[c, i, :, :, :, :, q], mine.at[q, i], local_sem.at[q, i])
            loads[q, by].start()
    weight_loads = []
    for i, ref in enumerate((wk_ref, wv_ref)):
        weight_loads.append(pltpu.make_async_copy(ref.at[pl.ds(y * width, width)], weights.at[0, i], load_sem.at[0, i]))
        for s in range(2):
            weight_loads.append(pltpu.make_async_copy(near_ref.at[s, i], weights.at[1 + s, i], load_sem.at[1 + s, i]))
        weight_loads.append(pltpu.make_async_copy(far_ref.at[i], weights.at[3, i, pl.ds(c * share, share)], load_sem.at[3, i]))
    for load in weight_loads:
        load.start()
    for i, ref in enumerate((qk_ref, qv_ref)):
        rows[2, 0, i] = ref[...]
    greet(plane_neighbours(z, x, c) + [{"head": head} for head in heads[1:]])
    send = Sender(send_sem)

    def spread(job):
        for p in (3, 1, 2):
            send(rows.at[job, 0], rows.at[job, mirror[p]], rows_sem.at[job, mirror[p]], {"head": heads[p]})

    spread(2)
    for q in range(2):
        for by in (2, 1, -1, 0):
            i = turn(b, by)
            send(full_ref.at[1 - c, i, :, :, :, :, q], other.at[q, i], core_sem.at[q, i], partner)
        if q == 0:
            for i in range(2):
                send(far_ref.at[i], weights.at[3, i, pl.ds(c * share, share)], far_sem.at[i], partner)

    def pair(q, by):
        i = turn(a, by)
        loads[q, by].wait()
        arrived(other.at[q, i], core_sem.at[q, i])
        mine[q, i] = mine[q, i] + other[q, i]
        return i

    def ring1_first(q):
        i = pair(q, 2)
        for s in range(2):
            to = lane_device(turn(a, steps[s]), b, c)
            send(mine.at[q, i, halves[s]], relay1.at[q, s], relay1_sem.at[q, s], to)
        for s in range(2):
            i = pair(q, steps[s])
            send(mine.at[q, i, halves[1 - s]], side1.at[q, s, halves[1 - s]], side1_sem.at[q, s, 1 - s], lane_device(i, b, c))

    def ring1_second(q):
        for s in range(2):
            i = turn(a, steps[s])
            arrived(relay1.at[q, s], relay1_sem.at[q, s])
            mine[q, i, halves[s]] = mine[q, i, halves[s]] + relay1[q, s]
            send(mine.at[q, i, halves[s]], side1.at[q, s, halves[s]], side1_sem.at[q, s, s], lane_device(i, b, c))
        pair(q, 0)

    def join1(q, j):
        total = mine[q, a, j].astype(F32)
        for s in range(2):
            total = total + side1[q, s, j].astype(F32)
        part[q, j] = total.astype(BF16)

    def ring2_first(q):
        for s in range(2):
            for t in range(2):
                arrived(side1.at[q, s, halves[t]], side1_sem.at[q, s, t])
        j = turn(b, 2)
        join1(q, j)
        for s in range(2):
            send(part.at[q, j, s], relay2.at[q, s], relay2_sem.at[q, s], lane_device(a, turn(b, steps[s]), c))
        for s in range(2):
            j = turn(b, steps[s])
            join1(q, j)
            send(part.at[q, j, 1 - s], side2.at[q, s, 1 - s], side2_sem.at[q, s, 1 - s], lane_device(a, j, c))
        join1(q, b)

    def ring2_second(q):
        for s in range(2):
            j = turn(b, steps[s])
            arrived(relay2.at[q, s], relay2_sem.at[q, s])
            part[q, j, s] = part[q, j, s] + relay2[q, s]
            send(part.at[q, j, s], side2.at[q, s, s], side2_sem.at[q, s, s], lane_device(a, j, c))

    def ring2_last(q):
        for t in range(2):
            total = part[q, b, t].astype(F32)
            for s in range(2):
                arrived(side2.at[q, s, t], side2_sem.at[q, s, t])
                total = total + side2[q, s, t].astype(F32)
            stage[q, t] = total.astype(BF16)
        send(stage.at[q, 1 - c], swap.at[q], swap_sem.at[q], partner)

    def close(q, n, total_of):
        for i, own_ref in enumerate((own_k_ref, own_v_ref)):
            for g in range(2):
                h = 2 * n + g
                top = pl.multiple_of((2 * h + q) * quarter, quarter)
                grad = own_ref[pl.ds(top, quarter), :] + total_of(i, g).astype(F32)
                rows[q, 0, i, pl.ds(pl.multiple_of(h * quarter, quarter), quarter), :] = grad.astype(BF16)

    def finish_rows(q):
        close(q, c, lambda i, g: stage[q, c, i, g])
        arrived(swap.at[q], swap_sem.at[q])
        close(q, 1 - c, lambda i, g: swap[q, i, g])
        spread(q)

    def product(job, p):
        for j in range(4):
            cols = pl.ds(j * (width // 4), width // 4)
            total = dot_t(rows[job, p, 0], weights[p, 0, cols, :]) + dot_t(rows[job, p, 1], weights[p, 1, cols, :])
            if p > 0:
                total = acc[:, cols] + total
            if p < 3:
                acc[:, cols] = total
            else:
                total = total.astype(BF16)
                for d in range(4):
                    terms[job, d, :, cols] = total[d * quarter:(d + 1) * quarter]

    def job_terms(job, out_ref, top):
        for p in range(4):
            if p > 0:
                arrived(rows.at[job, p], rows_sem.at[job, p])
            product(job, p)
        place_of = (pl.ds(top, quarter), pl.ds(pl.multiple_of(y * width, width), width))
        for p in (3, 1, 2):
            send(terms.at[job, heads[p]], out_ref.at[place_of], out_sem.at[job, mirror[p]], {"head": heads[p]})
        out_ref[place_of] = terms[job, y]

    def job_wait(job, out_ref, top):
        for p in (1, 2, 3):
            cols = pl.ds(pl.multiple_of(heads[p] * width, width), width)
            arrived(out_ref.at[pl.ds(top, quarter), cols], out_sem.at[job, p])

    ring1_first(0)
    for load in weight_loads:
        load.wait()
    for i in range(2):
        arrived(weights.at[3, i, pl.ds((1 - c) * share, share)], far_sem.at[i])
    job_terms(2, dx_qry_ref, 0)
    ring1_second(0)
    ring1_first(1)
    ring2_first(0)
    ring1_second(1)
    ring2_second(0)
    ring2_last(0)
    finish_rows(0)
    ring2_first(1)
    job_terms(0, dx_psg_ref, 0)
    ring2_second(1)
    ring2_last(1)
    finish_rows(1)
    job_terms(1, dx_psg_ref, quarter)
    job_wait(2, dx_qry_ref, 0)
    job_wait(0, dx_psg_ref, 0)
    job_wait(1, dx_psg_ref, quarter)
    send.finish()


def tail(full, own_k, own_v, gk_qry, gv_qry, w_key, w_value, near, far):
    rows, cols = own_k.shape
    width, depth = w_key.shape
    quarter = rows // 8
    hbm = pl.BlockSpec(memory_space=pl.ANY)
    vmem = pl.BlockSpec(memory_space=pltpu.VMEM)
    dma = pltpu.SemaphoreType.DMA
    block = (2, 2, 2, quarter, cols)
    full = full.reshape(2, 4, 4, 2, 2, 2, 2, quarter, cols)
    return pl.pallas_call(
        tail_kernel,
        in_specs=[hbm, vmem, vmem, vmem, vmem, hbm, hbm, hbm, hbm],
        out_specs=[vmem, vmem],
        out_shape=[jax.ShapeDtypeStruct((2 * quarter, width), BF16), jax.ShapeDtypeStruct((quarter, width), BF16)],
        scratch_shapes=[
            pltpu.VMEM((2, 4, 4) + block, BF16),
            pltpu.VMEM((2, 4, 4) + block, BF16),
            pltpu.VMEM((2, 2, 2) + block, BF16),
            pltpu.VMEM((2, 2, 4) + block, BF16),
            pltpu.VMEM((2, 4) + block, BF16),
            pltpu.VMEM((2, 2) + block[1:], BF16),
            pltpu.VMEM((2, 2) + block, BF16),
            pltpu.VMEM((2,) + block, BF16),
            pltpu.VMEM((2,) + block[1:], BF16),
            pltpu.VMEM((JOBS, 4, 2, 4 * quarter, cols), BF16),
            pltpu.VMEM((4, 2, width // 4, depth), BF16),
            pltpu.VMEM((4 * quarter, width // 4), F32),
            pltpu.VMEM((JOBS, 4, quarter, width // 4), BF16),
            dma((56,)),
            dma((2, 4)),
            dma((2, 2)),
            dma((2, 2, 2)),
            dma((2, 2)),
            dma((2, 2, 2)),
            dma((2,)),
            dma((2, 4)),
            dma((4, 2)),
            dma((2,)),
            dma((JOBS, 4)),
            dma((JOBS, 4)),
        ],
        compiler_params=pltpu.CompilerParams(collective_id=3, has_side_effects=True, vmem_limit_bytes=48 * 1024 * 1024),
        name="tail",
    )(full, own_k, own_v, gk_qry, gv_qry, w_key, w_value, near, far)


def local(q_psg, k_psg, v_psg, do_psg, q_qry, k_qry, v_qry, do_qry, w_key, w_value, req_passages, passage_slot, query_owner):
    me = lax.axis_index("psg").astype(jnp.int32).reshape(1)
    every, near, far = gather_plane(k_psg, v_psg, w_key, w_value)
    far = lax.ppermute(far, "head", [(i, (i + 2) % 4) for i in range(4)])
    dq_psg, own_k, own_v = psg_back(q_psg, k_psg, v_psg, do_psg)
    dq_qry, gk_qry, gv_qry, full = qry_back(
        req_passages, passage_slot, query_owner, every.reshape(NPSG, 2, PLEN, -1), q_qry, do_qry, k_qry, v_qry, me
    )
    dx_psg, dx_qry = tail(full, own_k, own_v, gk_qry, gv_qry, w_key, w_value, near, far)
    return dq_psg, dq_qry, dx_psg, dx_qry


def solution(mesh):
    rows = P("psg", "head")
    return jax.shard_map(
        local,
        mesh=mesh,
        in_specs=(rows,) * 8 + (P(None, "head"),) * 2 + (P(),) * 3,
        out_specs=(rows, rows, P(("psg", "head"), None), P(("psg", "head"), None)),
        check_vma=False,
    )
```

```python
import functools

import jax
import jax.numpy as jnp
from jax import lax
from jax.experimental import pallas as pl
from jax.experimental.pallas import tpu as pltpu
from jax.sharding import PartitionSpec as P

D = 128
G = 8
PLEN = 128
KV = 2
NPSG = 64
REQ = 32
P_REQ = 16
CB = 256
C = D ** -0.5
C2 = C * 1.4426950408889634
F32 = jnp.float32
BF16 = jnp.bfloat16


def stack(x):
    return jnp.concatenate([x[:, g * D:(g + 1) * D] for g in range(G)], axis=0)


def dot(a, b):
    return jnp.dot(a, b, preferred_element_type=F32)


def dot_t(a, b):
    return lax.dot_general(a, b, (((1,), (1,)), ((), ())), preferred_element_type=F32)


def causal_cols(shape):
    key = lax.broadcasted_iota(jnp.int32, shape, 0)
    qry = lax.broadcasted_iota(jnp.int32, shape, 1) % PLEN
    return key <= qry


def passage(q, k, v, do, dq_ref, rows, left):
    qs = stack(q)
    dos = stack(do)
    kt = k.T
    gk = jnp.zeros((PLEN, D), F32)
    gv = jnp.zeros((PLEN, D), F32)
    for b in range(G * PLEN // CB):
        cols = slice(b * CB, (b + 1) * CB)
        s = dot_t(k, qs[cols])
        s = jnp.where(causal_cols(s.shape), s, -1e30)
        e = jnp.exp2((s - jnp.max(s, axis=0, keepdims=True)) * C2)
        inv = 1.0 / jnp.sum(e, axis=0, keepdims=True)
        dp = dot_t(v, dos[cols])
        p = e * inv
        delta = jnp.sum(p * dp, axis=0, keepdims=True)
        ds = (p * (dp - delta)).astype(BF16)
        gk += dot(ds, qs[cols])
        gv += dot(p.astype(BF16), dos[cols])
        dqt = dot(kt, ds) * C
        for i in range(CB // PLEN):
            at = left + (b * (CB // PLEN) + i) * D
            dq_ref[rows, at:at + D] = dqt[:, i * PLEN:(i + 1) * PLEN].T.astype(BF16)
    return gk * C, gv


TK = 1024
TP = TK // PLEN
NT = P_REQ * PLEN // TK


def spot(slot):
    n = slot % 2
    c = slot // 2 % 2
    x = slot // 4 % 4
    z = slot // 16
    return n * 32 + jnp.where(n == 0, z * 4 + x, x * 4 + z) * 2 + c


def qry_kernel(
    req_ref, slot_ref, owner_ref, me_ref, kvg_ref, q_ref, do_ref, kq_ref, vq_ref,
    dq_ref, gk_ref, gv_ref, full_ref,
    kv, qs, dos, qst, dost, ktbuf, sbuf, dpbuf, dqt, gbuf, zeros, slots, mask,
    in_sem, out_sem, zero_sem,
):
    me = me_ref[0]
    zeros[...] = jnp.zeros_like(zeros)
    request = jnp.int32(0)
    for r in range(REQ):
        request = jnp.where(owner_ref[r] == me, r, request)

    def clear(i, carry):
        mask[i] = 0
        return carry

    lax.fori_loop(0, NPSG, clear, 0)

    def pick(j, carry):
        slot = spot(slot_ref[req_ref[request, j]])
        slots[j] = slot
        mask[slot] = 1
        pltpu.make_async_copy(kvg_ref.at[slot], kv.at[j], in_sem).start()
        return carry

    lax.fori_loop(0, P_REQ, pick, 0)

    def blank(wait):
        def one(i, carry):
            @pl.when(mask[i] == 0)
            def _():
                copy = pltpu.make_async_copy(zeros, full_ref.at[i], zero_sem)
                copy.wait() if wait else copy.start()

            return carry

        lax.fori_loop(0, NPSG, one, 0)

    blank(False)

    def land(j, carry):
        pltpu.make_async_copy(kvg_ref.at[slots[j]], kv.at[j], in_sem).wait()
        return carry

    blocks = [slice(i * CB, (i + 1) * CB) for i in range(G * PLEN // CB)]
    own = slice(P_REQ * PLEN, P_REQ * PLEN + PLEN)

    def tile(t, part, cols):
        return kv[pl.ds(t * TP, TP), part, :, cols].reshape(TK, D)

    def tile_rows(t):
        return pl.ds(pl.multiple_of(t * TK, TK), TK)

    def fold(x, op):
        return op(x.reshape(-1, 8, x.shape[1]), axis=0)

    for h in range(KV):
        cols = slice(h * D, (h + 1) * D)
        wide = slice(h * G * D, (h + 1) * G * D)
        qs[...] = stack(q_ref[:, wide])
        dos[...] = stack(do_ref[:, wide])
        qst[...] = qs[...].T
        dost[...] = dos[...].T
        kq = kq_ref[:, cols]
        vq = vq_ref[:, cols]

        def scores(keys, rows, masked, high):
            highs = []
            for b in blocks:
                s = dot(keys, qst[:, b])
                if masked:
                    s = jnp.where(causal_cols(s.shape), s, -1e30)
                sbuf[rows, b] = s
                highs.append(jnp.maximum(high[:, b], fold(s, jnp.max)))
            return jnp.concatenate(highs, axis=1)

        def score_tile(t, high):
            keys = tile(t, 0, cols)
            ktbuf[t] = keys.T
            return scores(keys, tile_rows(t), False, high)

        high = scores(kq, own, True, jnp.full((8, G * PLEN), -1e30, F32))
        if h == 0:
            lax.fori_loop(0, P_REQ, land, 0)
        high = lax.fori_loop(0, NT, score_tile, high)
        m2 = jnp.max(high, axis=0, keepdims=True) * C2

        def sums(values, rows, carry):
            l, num = carry
            ls, nums = [], []
            for b in blocks:
                dp = dot(values, dost[:, b])
                dpbuf[rows, b] = dp
                e = jnp.exp2(sbuf[rows, b] * C2 - m2[:, b])
                ls.append(l[:, b] + fold(e, jnp.sum))
                nums.append(num[:, b] + fold(e * dp, jnp.sum))
            return jnp.concatenate(ls, axis=1), jnp.concatenate(nums, axis=1)

        def sum_tile(t, carry):
            return sums(tile(t, 1, cols), tile_rows(t), carry)

        nothing = jnp.zeros((8, G * PLEN), F32)
        carry = sums(vq, own, (nothing, nothing))
        l, num = lax.fori_loop(0, NT, sum_tile, carry)
        l = jnp.sum(l, axis=0, keepdims=True)
        delta = jnp.sum(num, axis=0, keepdims=True) / l
        level = m2 + jnp.log2(l)

        def grads(kt, rows, first):
            gk = gv = None
            for b in blocks:
                p = jnp.exp2(sbuf[rows, b] * C2 - level[:, b])
                ds = (p * (dpbuf[rows, b] - delta[:, b])).astype(BF16)
                dk = dot(ds, qs[b, :])
                dv = dot(p.astype(BF16), dos[b, :])
                gk = dk if gk is None else gk + dk
                gv = dv if gv is None else gv + dv
                more = dot(kt, ds)
                dqt[:, b] = more if first else dqt[:, b] + more
            return (gk * C).astype(BF16), gv.astype(BF16)

        gk, gv = grads(kq.T, own, True)
        gk_ref[:, cols] = gk
        gv_ref[:, cols] = gv

        def grad_tile(t, carry):
            gk, gv = grads(ktbuf[t], tile_rows(t), False)
            for i in range(TP):
                j = t * TP + i
                gbuf[j, 0, :, cols] = gk[i * PLEN:(i + 1) * PLEN]
                gbuf[j, 1, :, cols] = gv[i * PLEN:(i + 1) * PLEN]
                if h == KV - 1:
                    pltpu.make_async_copy(gbuf.at[j], full_ref.at[slots[j]], out_sem).start()
            return carry

        lax.fori_loop(0, NT, grad_tile, 0)
        for g in range(G):
            left = h * G * D + g * D
            dq_ref[:, left:left + D] = (dqt[:, g * PLEN:(g + 1) * PLEN] * C).T.astype(BF16)

    def drain(j, carry):
        pltpu.make_async_copy(gbuf.at[j], full_ref.at[slots[j]], out_sem).wait()
        return carry

    lax.fori_loop(0, P_REQ, drain, 0)
    blank(True)


def qry_back(req, slot, owner, me, kvg, q, do, kq, vq):
    keys = P_REQ * PLEN + PLEN
    smem = pl.BlockSpec(memory_space=pltpu.SMEM)
    vmem = pl.BlockSpec(memory_space=pltpu.VMEM)
    return pl.pallas_call(
        qry_kernel,
        in_specs=[smem] * 4 + [pl.BlockSpec(memory_space=pl.ANY)] + [vmem] * 4,
        out_specs=[vmem, vmem, vmem, pl.BlockSpec(memory_space=pl.ANY)],
        out_shape=[
            jax.ShapeDtypeStruct(q.shape, BF16),
            jax.ShapeDtypeStruct(kq.shape, BF16),
            jax.ShapeDtypeStruct(vq.shape, BF16),
            jax.ShapeDtypeStruct((NPSG, 2, PLEN, KV * D), BF16),
        ],
        scratch_shapes=[
            pltpu.VMEM((P_REQ, 2, PLEN, KV * D), BF16),
            pltpu.VMEM((G * PLEN, D), BF16),
            pltpu.VMEM((G * PLEN, D), BF16),
            pltpu.VMEM((D, G * PLEN), BF16),
            pltpu.VMEM((D, G * PLEN), BF16),
            pltpu.VMEM((NT, D, TK), BF16),
            pltpu.VMEM((keys, G * PLEN), F32),
            pltpu.VMEM((keys, G * PLEN), F32),
            pltpu.VMEM((D, G * PLEN), F32),
            pltpu.VMEM((P_REQ, 2, PLEN, KV * D), BF16),
            pltpu.VMEM((2, PLEN, KV * D), BF16),
            pltpu.SMEM((P_REQ,), jnp.int32),
            pltpu.SMEM((NPSG,), jnp.int32),
            pltpu.SemaphoreType.DMA,
            pltpu.SemaphoreType.DMA,
            pltpu.SemaphoreType.DMA,
        ],
        compiler_params=pltpu.CompilerParams(vmem_limit_bytes=48 * 1024 * 1024),
        cost_estimate=pl.CostEstimate(flops=2 * 5 * 2 * 1024 * 2176 * 128, bytes_accessed=16 * 1024 * 1024, transcendentals=2 * 1024 * 2176),
        name="qry_back",
    )(req, slot, owner, me, kvg, q, do, kq, vq)


MESH = pl.DeviceIdType.MESH


def place():
    me = lax.axis_index("psg")
    return me // 8, lax.rem(me // 2, 4), lax.rem(me, 2)


def at_plane(z, x, c):
    return {"psg": (z * 4 + x) * 2 + c}


def turn(i, by):
    return lax.rem(i + by + 4, 4)


def greet(devices):
    barrier = pltpu.get_barrier_semaphore()
    for device in devices:
        pl.semaphore_signal(barrier, inc=1, device_id=device, device_id_type=MESH)
    pl.semaphore_wait(barrier, len(devices))


def plane_neighbours(z, x, c):
    return [
        at_plane(turn(z, 1), x, c),
        at_plane(turn(z, -1), x, c),
        at_plane(z, turn(x, 1), c),
        at_plane(z, turn(x, -1), c),
        at_plane(z, x, 1 - c),
    ]


class Sender:
    def __init__(self, sems):
        self.sems = sems
        self.started = []

    def __call__(self, src, dst, recv_sem, device):
        copy = pltpu.make_async_remote_copy(
            src_ref=src, dst_ref=dst, send_sem=self.sems.at[len(self.started)], recv_sem=recv_sem,
            device_id=device, device_id_type=MESH,
        )
        copy.start()
        self.started.append(copy)

    def finish(self):
        for copy in self.started:
            copy.wait_send()


def arrived(ref, sem):
    pltpu.make_async_copy(ref, ref, sem).wait()


def lane_device(a, b, c):
    return at_plane(a * (1 - c) + b * c, b * (1 - c) + a * c, c)


def gather_kernel(
    q_ref, k_ref, v_ref, do_ref, wk_ref, wv_ref, all_ref, near_ref, far_ref, dq_ref, own_k_ref, own_v_ref,
    lane, q_buf, do_buf,
    send_sem, recv_sem, core_sem, local_sem, swap_sem, near_sem, near_core_sem, far_sem, load_sem, keep_sem,
):
    z, x, c = place()
    y = lax.axis_index("head")
    a = z * (1 - c) + x * c
    b = x * (1 - c) + z * c
    half = k_ref.shape[0] // 2
    share = far_ref.shape[1]
    refs = (k_ref, v_ref)
    weights = (wk_ref, wv_ref)
    mine = [pltpu.make_async_copy(ref.at[pl.ds(c * half, half)], lane.at[a, b, c, i], local_sem.at[i]) for i, ref in enumerate(refs)]
    loads = [pltpu.make_async_copy(ref, buf, load_sem.at[i]) for i, (ref, buf) in enumerate(((q_ref, q_buf), (do_ref, do_buf)))]
    for copy in mine + loads:
        copy.start()
    greet(plane_neighbours(z, x, c) + [{"head": turn(y, 1)}, {"head": turn(y, -1)}])
    send = Sender(send_sem)
    partner = at_plane(z, x, 1 - c)
    for i, ref in enumerate(refs):
        send(ref.at[pl.ds((1 - c) * half, half)], lane.at[b, a, c, i], swap_sem.at[i], partner)

    def columns(head):
        return pl.ds((2 * head + c) * share, share)

    for i, ref in enumerate(weights):
        for s, by in ((1, 1), (0, -1)):
            to = turn(y, by)
            send(ref.at[columns(to)], near_ref.at[s, i, pl.ds(c * share, share)], near_sem.at[s, i], {"head": to})
    for copy in mine:
        copy.wait()
    for i in range(2):
        arrived(lane.at[a, b, 1 - c, i], swap_sem.at[i])

    def whole(i, j, to):
        send(lane.at[i, j], lane.at[i, j], recv_sem.at[0, i, j], to)

    def piece(i, j, part, to):
        send(lane.at[i, j, part], lane.at[i, j, part], recv_sem.at[part, i, j], to)

    def keep(i, j):
        return pltpu.make_async_copy(lane.at[i, j], all_ref.at[c, i, j], keep_sem.at[i, j])

    def core(i, j):
        send(lane.at[i, j], all_ref.at[c, i, j], core_sem.at[i, j], partner)
        keep(i, j).start()

    def wait_whole(i, j):
        arrived(lane.at[i, j], recv_sem.at[0, i, j])

    def wait_pieces(i, j):
        for part in range(2):
            arrived(lane.at[i, j, part], recv_sem.at[part, i, j])

    def along_a(i, j):
        for by in (1, -1):
            whole(i, j, lane_device(turn(a, by), b, c))

    def own_passage(n, h):
        rows = slice(n * PLEN, (n + 1) * PLEN)
        thin = slice(h * D, (h + 1) * D)
        wide = slice(h * G * D, (h + 1) * G * D)
        gk, gv = passage(q_buf[rows, wide], k_ref[rows, thin], v_ref[rows, thin], do_buf[rows, wide], dq_ref, rows, h * G * D)
        own_k_ref[rows, thin] = gk
        own_v_ref[rows, thin] = gv

    ways = ((-1, 0), (1, 1))
    for by in (1, -1):
        whole(a, b, lane_device(a, turn(b, by), c))
    along_a(a, b)
    across = [pltpu.make_async_copy(ref.at[columns(turn(y, 2))], far_ref.at[i], far_sem.at[i]) for i, ref in enumerate(weights)]
    for copy in across:
        copy.start()
    for copy in loads:
        copy.wait()
    own_passage(0, 0)
    own_passage(0, 1)
    for by, part in ways:
        j = turn(b, by)
        wait_whole(a, j)
        piece(a, j, part, lane_device(a, turn(b, -by), c))
    for by, part in ways:
        along_a(a, turn(b, by))
    own_passage(1, 0)

    def far(bo):
        j = turn(b, bo)
        for by, part in ways:
            i = turn(a, by)
            wait_whole(i, j)
            piece(i, j, part, lane_device(turn(a, -by), b, c))

    far(0)
    wait_pieces(a, turn(b, 2))
    along_a(a, turn(b, 2))
    own_passage(1, 1)
    for bo in (0, -1, 1, 2):
        core(a, turn(b, bo))
    for by, _ in ways:
        core(turn(a, by), b)
    for bo in (-1, 1, 2):
        far(bo)
        for by, _ in ways:
            core(turn(a, by), turn(b, bo))
    for s in range(2):
        for i in range(2):
            block = near_ref.at[s, i, pl.ds(c * share, share)]
            arrived(block, near_sem.at[s, i])
            send(block, block, near_core_sem.at[s, i], partner)
    for bo in (0, -1, 1, 2):
        wait_pieces(turn(a, 2), turn(b, bo))
        core(turn(a, 2), turn(b, bo))
    for i in range(4):
        for j in range(4):
            arrived(all_ref.at[1 - c, i, j], core_sem.at[i, j])
            keep(i, j).wait()
    for s in range(2):
        for i in range(2):
            arrived(near_ref.at[s, i, pl.ds((1 - c) * share, share)], near_core_sem.at[s, i])
    for copy in across:
        copy.wait()
    send.finish()


def gather_plane(q, k, v, do, w_key, w_value):
    rows, cols = k.shape
    width, depth = w_key.shape
    share = width // 8
    hbm = pl.BlockSpec(memory_space=pl.ANY)
    vmem = pl.BlockSpec(memory_space=pltpu.VMEM)
    dma = pltpu.SemaphoreType.DMA
    return pl.pallas_call(
        gather_kernel,
        in_specs=[hbm, vmem, vmem, hbm, hbm, hbm],
        out_specs=[hbm, hbm, hbm, vmem, vmem, vmem],
        out_shape=[
            jax.ShapeDtypeStruct((2, 4, 4, 2, 2, rows // 2, cols), BF16),
            jax.ShapeDtypeStruct((2, 2, 2 * share, depth), BF16),
            jax.ShapeDtypeStruct((2, share, depth), BF16),
            jax.ShapeDtypeStruct(q.shape, BF16),
            jax.ShapeDtypeStruct(k.shape, F32),
            jax.ShapeDtypeStruct(v.shape, F32),
        ],
        scratch_shapes=[
            pltpu.VMEM((4, 4, 2, 2, rows // 2, cols), BF16),
            pltpu.VMEM(q.shape, BF16),
            pltpu.VMEM(q.shape, BF16),
            dma((46,)), dma((2, 4, 4)), dma((4, 4)), dma((2,)), dma((2,)), dma((2, 2)), dma((2, 2)), dma((2,)), dma((2,)),
            dma((4, 4)),
        ],
        compiler_params=pltpu.CompilerParams(collective_id=0, has_side_effects=True, vmem_limit_bytes=40 * 1024 * 1024),
        name="gather_plane",
    )(q, k, v, do, w_key, w_value)


CUTS = 2
JOBS = CUTS + 1
ORDER = [
    ("f", 0), ("n", 0), (0, 0), ("f", 1), ("o", 0), ("w", 0), (0, 1), ("n", 1), ("o", 1), (1, 0), ("q", 0), (1, 1), (2, 0),
    (3, 0), (4, 0), (2, 1), (5, 0), (3, 1), (4, 1), (5, 1), (6, 0), (6, 1),
]


def tail_kernel(
    full_ref, own_k_ref, own_v_ref, qk_ref, qv_ref, wk_ref, wv_ref, near_ref, far_ref, dx_psg_ref, dx_qry_ref,
    mine, other, relay1, side1, part, relay2, side2, stage, swap, rows, weights, acc, terms,
    send_sem, core_sem, relay1_sem, side1_sem, relay2_sem, side2_sem, swap_sem, local_sem,
    load_sem, far_sem, rows_sem, out_sem,
):
    z, x, c = place()
    y = lax.axis_index("head")
    a = z * (1 - c) + x * c
    b = x * (1 - c) + z * c
    partner = at_plane(z, x, 1 - c)
    steps = (1, -1)
    halves = (pl.ds(0, 2), pl.ds(2, 2))
    quarter = dx_qry_ref.shape[0]
    width = dx_qry_ref.shape[1] // 4
    share = width // 2
    heads = [y, turn(y, 1), turn(y, -1), turn(y, 2)]
    mirror = (0, 2, 1, 3)
    few = dx_psg_ref.shape[0] // CUTS
    size = [few] * CUTS + [quarter]

    loads = {}
    for q in range(CUTS):
        for by in (2, 1, -1, 0):
            i = turn(a, by)
            loads[q, by] = pltpu.make_async_copy(full_ref.at[c, i, :, :, :, :, q], mine.at[q, i], local_sem.at[q, i])
            loads[q, by].start()
    weight_loads = []
    for i, ref in enumerate((wk_ref, wv_ref)):
        weight_loads.append(pltpu.make_async_copy(ref.at[pl.ds(y * width, width)], weights.at[0, i], load_sem.at[0, i]))
        for s in range(2):
            weight_loads.append(pltpu.make_async_copy(near_ref.at[s, i], weights.at[1 + s, i], load_sem.at[1 + s, i]))
        weight_loads.append(pltpu.make_async_copy(far_ref.at[i], weights.at[3, i, pl.ds(c * share, share)], load_sem.at[3, i]))
    for load in weight_loads:
        load.start()
    for i, ref in enumerate((qk_ref, qv_ref)):
        rows[CUTS, 0, i] = ref[...]
    greet(plane_neighbours(z, x, c) + [{"head": head} for head in heads[1:]])
    send = Sender(send_sem)

    def spread(job):
        used = pl.ds(0, 4 * size[job])
        for p in (3, 1, 2):
            for i in range(2):
                send(rows.at[job, 0, i, used], rows.at[job, mirror[p], i, used], rows_sem.at[job, mirror[p], i], {"head": heads[p]})

    spread(CUTS)

    def stage0(q, by):
        i = turn(b, by)
        send(full_ref.at[1 - c, i, :, :, :, :, q], other.at[q, i], core_sem.at[q, i], partner)

    def share_far():
        for i in range(2):
            send(far_ref.at[i], weights.at[3, i, pl.ds(c * share, share)], far_sem.at[i], partner)

    def pair(q, by):
        i = turn(a, by)
        loads[q, by].wait()
        arrived(other.at[q, i], core_sem.at[q, i])
        mine[q, i] = mine[q, i] + other[q, i]
        return i

    def ring1_far(q):
        i = pair(q, 2)
        for s in range(2):
            to = lane_device(turn(a, steps[s]), b, c)
            send(mine.at[q, i, halves[s]], relay1.at[q, s], relay1_sem.at[q, s], to)

    def ring1_near(q):
        for s in range(2):
            i = pair(q, steps[s])
            arrived(relay1.at[q, s], relay1_sem.at[q, s])
            mine[q, i, halves[s]] = mine[q, i, halves[s]] + relay1[q, s]
            send(mine.at[q, i], side1.at[q, s], side1_sem.at[q, s], lane_device(i, b, c))

    def join1(q, j):
        total = mine[q, a, j].astype(F32)
        for s in range(2):
            total = total + side1[q, s, j].astype(F32)
        part[q, j] = total.astype(BF16)

    def ring2_far(q):
        pair(q, 0)
        for s in range(2):
            arrived(side1.at[q, s], side1_sem.at[q, s])
        j = turn(b, 2)
        join1(q, j)
        for s in range(2):
            send(part.at[q, j, s], relay2.at[q, s], relay2_sem.at[q, s], lane_device(a, turn(b, steps[s]), c))
        for by in (1, -1, 0):
            join1(q, turn(b, by))

    def ring2_near(q):
        for s in range(2):
            j = turn(b, steps[s])
            arrived(relay2.at[q, s], relay2_sem.at[q, s])
            part[q, j, s] = part[q, j, s] + relay2[q, s]
            send(part.at[q, j], side2.at[q, s], side2_sem.at[q, s], lane_device(a, j, c))

    def ring2_last(q):
        total = part[q, b].astype(F32)
        for s in range(2):
            arrived(side2.at[q, s], side2_sem.at[q, s])
            total = total + side2[q, s].astype(F32)
        stage[q] = total.astype(BF16)
        send(stage.at[q, 1 - c], swap.at[q], swap_sem.at[q], partner)

    def close(q, n, total_of):
        for i, own_ref in enumerate((own_k_ref, own_v_ref)):
            for g in range(2):
                h = 2 * n + g
                top = pl.multiple_of((CUTS * h + q) * few, few)
                grad = own_ref[pl.ds(top, few), :] + total_of(i, g).astype(F32)
                rows[q, 0, i, pl.ds(pl.multiple_of(h * few, few), few), :] = grad.astype(BF16)

    def finish_rows(q):
        close(q, c, lambda i, g: stage[q, c, i, g])
        arrived(swap.at[q], swap_sem.at[q])
        close(q, 1 - c, lambda i, g: swap[q, i, g])
        spread(q)

    def product(job, p):
        used = pl.ds(0, 4 * size[job])
        for j in range(4):
            cols = pl.ds(j * (width // 4), width // 4)
            total = dot_t(rows[job, p, 0, used], weights[p, 0, cols, :]) + dot_t(rows[job, p, 1, used], weights[p, 1, cols, :])
            if p > 0:
                total = acc[used, cols] + total
            if p < 3:
                acc[used, cols] = total
            else:
                total = total.astype(BF16)
                for d in range(4):
                    terms[job, d, pl.ds(0, size[job]), cols] = total[d * size[job]:(d + 1) * size[job]]

    def target(job):
        return (dx_qry_ref, 0) if job == CUTS else (dx_psg_ref, job * few)

    def job_terms(job):
        out_ref, top = target(job)
        used = pl.ds(0, size[job])
        for p in range(4):
            if p > 0:
                for i in range(2):
                    block = rows.at[job, p, i, pl.ds(0, 4 * size[job])]
                    arrived(block, rows_sem.at[job, p, i])
            product(job, p)
        place_of = (pl.ds(top, size[job]), pl.ds(pl.multiple_of(y * width, width), width))
        for p in (3, 1, 2):
            send(terms.at[job, heads[p], used], out_ref.at[place_of], out_sem.at[job, mirror[p]], {"head": heads[p]})
        out_ref[place_of] = terms[job, y, used]

    def job_wait(job):
        out_ref, top = target(job)
        for p in (1, 2, 3):
            cols = pl.ds(pl.multiple_of(heads[p] * width, width), width)
            arrived(out_ref.at[pl.ds(top, size[job]), cols], out_sem.at[job, p])

    def query_job():
        for load in weight_loads:
            load.wait()
        for i in range(2):
            arrived(weights.at[3, i, pl.ds((1 - c) * share, share)], far_sem.at[i])
        job_terms(CUTS)

    steps_of = {
        "f": lambda q: stage0(q, 2),
        "n": lambda q: (stage0(q, 1), stage0(q, -1)),
        "o": lambda q: stage0(q, 0),
        "w": lambda q: share_far(),
        "q": lambda q: query_job(),
        0: ring1_far,
        1: ring1_near,
        2: ring2_far,
        3: ring2_near,
        4: ring2_last,
        5: finish_rows,
        6: job_terms,
    }
    for step, q in ORDER:
        steps_of[step](q)
    for job in [CUTS] + list(range(CUTS)):
        job_wait(job)
    send.finish()


def tail(full, own_k, own_v, gk_qry, gv_qry, w_key, w_value, near, far):
    rows, cols = own_k.shape
    width, depth = w_key.shape
    quarter = rows // 8
    few = rows // 4 // CUTS
    hbm = pl.BlockSpec(memory_space=pl.ANY)
    vmem = pl.BlockSpec(memory_space=pltpu.VMEM)
    dma = pltpu.SemaphoreType.DMA
    block = (2, 2, 2, few, cols)
    full = full.reshape(2, 4, 4, 2, 2, 2, CUTS, few, cols)
    return pl.pallas_call(
        tail_kernel,
        in_specs=[hbm, vmem, vmem, vmem, vmem, hbm, hbm, hbm, hbm],
        out_specs=[vmem, vmem],
        out_shape=[jax.ShapeDtypeStruct((2 * quarter, width), BF16), jax.ShapeDtypeStruct((quarter, width), BF16)],
        scratch_shapes=[
            pltpu.VMEM((CUTS, 4, 4) + block, BF16),
            pltpu.VMEM((CUTS, 4, 4) + block, BF16),
            pltpu.VMEM((CUTS, 2, 2) + block, BF16),
            pltpu.VMEM((CUTS, 2, 4) + block, BF16),
            pltpu.VMEM((CUTS, 4) + block, BF16),
            pltpu.VMEM((CUTS, 2) + block[1:], BF16),
            pltpu.VMEM((CUTS, 2) + block, BF16),
            pltpu.VMEM((CUTS,) + block, BF16),
            pltpu.VMEM((CUTS,) + block[1:], BF16),
            pltpu.VMEM((JOBS, 4, 2, 4 * quarter, cols), BF16),
            pltpu.VMEM((4, 2, width // 4, depth), BF16),
            pltpu.VMEM((4 * quarter, width // 4), F32),
            pltpu.VMEM((JOBS, 4, quarter, width // 4), BF16),
            dma((13 * CUTS + 2 + 9 * JOBS,)),
            dma((CUTS, 4)),
            dma((CUTS, 2)),
            dma((CUTS, 2)),
            dma((CUTS, 2)),
            dma((CUTS, 2)),
            dma((CUTS,)),
            dma((CUTS, 4)),
            dma((4, 2)),
            dma((2,)),
            dma((JOBS, 4, 2)),
            dma((JOBS, 4)),
        ],
        compiler_params=pltpu.CompilerParams(collective_id=3, has_side_effects=True, vmem_limit_bytes=48 * 1024 * 1024),
        name="tail",
    )(full, own_k, own_v, gk_qry, gv_qry, w_key, w_value, near, far)


def local(q_psg, k_psg, v_psg, do_psg, q_qry, k_qry, v_qry, do_qry, w_key, w_value, req_passages, passage_slot, query_owner):
    me = lax.axis_index("psg").astype(jnp.int32).reshape(1)
    every, near, far, dq_psg, own_k, own_v = gather_plane(q_psg, k_psg, v_psg, do_psg, w_key, w_value)
    far = lax.ppermute(far, "head", [(i, (i + 2) % 4) for i in range(4)])
    dq_qry, gk_qry, gv_qry, full = qry_back(
        req_passages, passage_slot, query_owner, me, every.reshape(NPSG, 2, PLEN, -1), q_qry, do_qry, k_qry, v_qry
    )
    dx_psg, dx_qry = tail(full, own_k, own_v, gk_qry, gv_qry, w_key, w_value, near, far)
    return dq_psg, dq_qry, dx_psg, dx_qry


def solution(mesh):
    rows = P("psg", "head")
    return jax.shard_map(
        local,
        mesh=mesh,
        in_specs=(rows,) * 8 + (P(None, "head"),) * 2 + (P(),) * 3,
        out_specs=(rows, rows, P(("psg", "head"), None), P(("psg", "head"), None)),
        check_vma=False,
    )
```

```python
import functools

import jax
import jax.numpy as jnp
from jax import lax
from jax.experimental import pallas as pl
from jax.experimental.pallas import tpu as pltpu
from jax.sharding import PartitionSpec as P

D = 128
G = 8
PLEN = 128
KV = 2
NPSG = 64
REQ = 32
P_REQ = 16
CB = 256
C = D ** -0.5
C2 = C * 1.4426950408889634
VMEM = 62 * 1024 * 1024
F32 = jnp.float32
BF16 = jnp.bfloat16


def stack(x):
    return jnp.concatenate([x[:, g * D:(g + 1) * D] for g in range(G)], axis=0)


def dot(a, b):
    return jnp.dot(a, b, preferred_element_type=F32)


def dot_t(a, b):
    return lax.dot_general(a, b, (((1,), (1,)), ((), ())), preferred_element_type=F32)


def causal_cols(shape):
    key = lax.broadcasted_iota(jnp.int32, shape, 0)
    qry = lax.broadcasted_iota(jnp.int32, shape, 1) % PLEN
    return key <= qry


def passage(q, k, v, do, dq_ref, rows, left):
    qs = stack(q)
    dos = stack(do)
    kt = k.T
    gk = jnp.zeros((PLEN, D), F32)
    gv = jnp.zeros((PLEN, D), F32)
    for b in range(G * PLEN // CB):
        cols = slice(b * CB, (b + 1) * CB)
        s = dot_t(k, qs[cols])
        s = jnp.where(causal_cols(s.shape), s, -1e30)
        e = jnp.exp2((s - jnp.max(s, axis=0, keepdims=True)) * C2)
        inv = 1.0 / jnp.sum(e, axis=0, keepdims=True)
        dp = dot_t(v, dos[cols])
        p = e * inv
        delta = jnp.sum(p * dp, axis=0, keepdims=True)
        ds = (p * (dp - delta)).astype(BF16)
        gk += dot(ds, qs[cols])
        gv += dot(p.astype(BF16), dos[cols])
        dqt = dot(kt, ds) * C
        for i in range(CB // PLEN):
            at = left + (b * (CB // PLEN) + i) * D
            dq_ref[rows, at:at + D] = dqt[:, i * PLEN:(i + 1) * PLEN].T.astype(BF16)
    return gk * C, gv


TK = 1024
TP = TK // PLEN
NT = P_REQ * PLEN // TK


def spot(slot):
    n = slot % 2
    c = slot // 2 % 2
    x = slot // 4 % 4
    z = slot // 16
    return n * 32 + jnp.where(n == 0, z * 4 + x, x * 4 + z) * 2 + c


def qry_kernel(
    req_ref, slot_ref, owner_ref, me_ref, kvg_ref, q_any, do_any, kq_any, vq_any, dq_in_ref,
    dq_ref, gk_ref, gv_ref, full_ref, dq_out_ref,
    kv, q_ref, do_ref, kq_ref, vq_ref, qs, dos, qst, dost, ktbuf, sbuf, dpbuf, dqt, gbuf, zeros, slots, mask,
    load_sem, in_sem, out_sem, zero_sem, hand_sem,
):
    me = me_ref[0]
    hand_on = pltpu.make_async_copy(dq_in_ref, dq_out_ref, hand_sem)
    pairs = ((q_any, q_ref), (do_any, do_ref), (kq_any, kq_ref), (vq_any, vq_ref))
    loads = [pltpu.make_async_copy(ref, buf, load_sem.at[i]) for i, (ref, buf) in enumerate(pairs)]
    for copy in loads:
        copy.start()
    zeros[...] = jnp.zeros_like(zeros)
    request = jnp.int32(0)
    for r in range(REQ):
        request = jnp.where(owner_ref[r] == me, r, request)

    def clear(i, carry):
        mask[i] = 0
        return carry

    lax.fori_loop(0, NPSG, clear, 0)

    def pick(j, carry):
        slot = spot(slot_ref[req_ref[request, j]])
        slots[j] = slot
        mask[slot] = 1
        pltpu.make_async_copy(kvg_ref.at[slot], kv.at[j], in_sem).start()
        return carry

    lax.fori_loop(0, P_REQ, pick, 0)

    def blank(wait):
        def one(i, carry):
            @pl.when(mask[i] == 0)
            def _():
                copy = pltpu.make_async_copy(zeros, full_ref.at[i], zero_sem)
                copy.wait() if wait else copy.start()

            return carry

        lax.fori_loop(0, NPSG, one, 0)

    blank(False)
    for copy in loads:
        copy.wait()
    hand_on.start()

    def land(j, carry):
        pltpu.make_async_copy(kvg_ref.at[slots[j]], kv.at[j], in_sem).wait()
        return carry

    blocks = [slice(i * CB, (i + 1) * CB) for i in range(G * PLEN // CB)]
    own = slice(P_REQ * PLEN, P_REQ * PLEN + PLEN)

    def tile(t, part, cols):
        return kv[pl.ds(t * TP, TP), part, :, cols].reshape(TK, D)

    def tile_rows(t):
        return pl.ds(pl.multiple_of(t * TK, TK), TK)

    def fold(x, op):
        return op(x.reshape(-1, 8, x.shape[1]), axis=0)

    for h in range(KV):
        cols = slice(h * D, (h + 1) * D)
        wide = slice(h * G * D, (h + 1) * G * D)
        qs[...] = stack(q_ref[:, wide])
        dos[...] = stack(do_ref[:, wide])
        qst[...] = qs[...].T
        dost[...] = dos[...].T
        kq = kq_ref[:, cols]
        vq = vq_ref[:, cols]

        def scores(keys, rows, masked, high):
            highs = []
            for b in blocks:
                s = dot(keys, qst[:, b])
                if masked:
                    s = jnp.where(causal_cols(s.shape), s, -1e30)
                sbuf[rows, b] = s
                highs.append(jnp.maximum(high[:, b], fold(s, jnp.max)))
            return jnp.concatenate(highs, axis=1)

        def score_tile(t, high):
            keys = tile(t, 0, cols)
            ktbuf[t] = keys.T
            return scores(keys, tile_rows(t), False, high)

        high = scores(kq, own, True, jnp.full((8, G * PLEN), -1e30, F32))
        if h == 0:
            lax.fori_loop(0, P_REQ, land, 0)
        high = lax.fori_loop(0, NT, score_tile, high)
        m2 = jnp.max(high, axis=0, keepdims=True) * C2

        def sums(values, rows, carry):
            l, num = carry
            ls, nums = [], []
            for b in blocks:
                dp = dot(values, dost[:, b])
                dpbuf[rows, b] = dp
                e = jnp.exp2(sbuf[rows, b] * C2 - m2[:, b])
                ls.append(l[:, b] + fold(e, jnp.sum))
                nums.append(num[:, b] + fold(e * dp, jnp.sum))
            return jnp.concatenate(ls, axis=1), jnp.concatenate(nums, axis=1)

        def sum_tile(t, carry):
            return sums(tile(t, 1, cols), tile_rows(t), carry)

        nothing = jnp.zeros((8, G * PLEN), F32)
        carry = sums(vq, own, (nothing, nothing))
        l, num = lax.fori_loop(0, NT, sum_tile, carry)
        l = jnp.sum(l, axis=0, keepdims=True)
        delta = jnp.sum(num, axis=0, keepdims=True) / l
        level = m2 + jnp.log2(l)

        def grads(kt, rows, first):
            gk = gv = None
            for b in blocks:
                p = jnp.exp2(sbuf[rows, b] * C2 - level[:, b])
                ds = (p * (dpbuf[rows, b] - delta[:, b])).astype(BF16)
                dk = dot(ds, qs[b, :])
                dv = dot(p.astype(BF16), dos[b, :])
                gk = dk if gk is None else gk + dk
                gv = dv if gv is None else gv + dv
                more = dot(kt, ds)
                dqt[:, b] = more if first else dqt[:, b] + more
            return (gk * C).astype(BF16), gv.astype(BF16)

        gk, gv = grads(kq.T, own, True)
        gk_ref[:, cols] = gk
        gv_ref[:, cols] = gv

        def grad_tile(t, carry):
            gk, gv = grads(ktbuf[t], tile_rows(t), False)
            for i in range(TP):
                j = t * TP + i
                gbuf[j, 0, :, cols] = gk[i * PLEN:(i + 1) * PLEN]
                gbuf[j, 1, :, cols] = gv[i * PLEN:(i + 1) * PLEN]
                if h == KV - 1:
                    pltpu.make_async_copy(gbuf.at[j], full_ref.at[slots[j]], out_sem).start()
            return carry

        lax.fori_loop(0, NT, grad_tile, 0)
        for g in range(G):
            left = h * G * D + g * D
            dq_ref[:, left:left + D] = (dqt[:, g * PLEN:(g + 1) * PLEN] * C).T.astype(BF16)

    def drain(j, carry):
        pltpu.make_async_copy(gbuf.at[j], full_ref.at[slots[j]], out_sem).wait()
        return carry

    lax.fori_loop(0, P_REQ, drain, 0)
    blank(True)
    hand_on.wait()


def qry_back(req, slot, owner, me, kvg, q, do, kq, vq, dq_psg):
    keys = P_REQ * PLEN + PLEN
    smem = pl.BlockSpec(memory_space=pltpu.SMEM)
    hbm = pl.BlockSpec(memory_space=pltpu.HBM)
    vmem = pl.BlockSpec(memory_space=pltpu.VMEM)
    return pl.pallas_call(
        qry_kernel,
        in_specs=[smem] * 4 + [hbm] * 6,
        out_specs=[vmem, vmem, vmem, hbm, hbm],
        out_shape=[
            jax.ShapeDtypeStruct(q.shape, BF16),
            jax.ShapeDtypeStruct(kq.shape, BF16),
            jax.ShapeDtypeStruct(vq.shape, BF16),
            jax.ShapeDtypeStruct((NPSG, 2, PLEN, KV * D), BF16),
            jax.ShapeDtypeStruct(dq_psg.shape, BF16),
        ],
        scratch_shapes=[
            pltpu.VMEM((P_REQ, 2, PLEN, KV * D), BF16),
            pltpu.VMEM(q.shape, BF16),
            pltpu.VMEM(q.shape, BF16),
            pltpu.VMEM(kq.shape, BF16),
            pltpu.VMEM(kq.shape, BF16),
            pltpu.VMEM((G * PLEN, D), BF16),
            pltpu.VMEM((G * PLEN, D), BF16),
            pltpu.VMEM((D, G * PLEN), BF16),
            pltpu.VMEM((D, G * PLEN), BF16),
            pltpu.VMEM((NT, D, TK), BF16),
            pltpu.VMEM((keys, G * PLEN), F32),
            pltpu.VMEM((keys, G * PLEN), F32),
            pltpu.VMEM((D, G * PLEN), F32),
            pltpu.VMEM((P_REQ, 2, PLEN, KV * D), BF16),
            pltpu.VMEM((2, PLEN, KV * D), BF16),
            pltpu.SMEM((P_REQ,), jnp.int32),
            pltpu.SMEM((NPSG,), jnp.int32),
            pltpu.SemaphoreType.DMA((4,)),
            pltpu.SemaphoreType.DMA,
            pltpu.SemaphoreType.DMA,
            pltpu.SemaphoreType.DMA,
            pltpu.SemaphoreType.DMA,
        ],
        compiler_params=pltpu.CompilerParams(vmem_limit_bytes=VMEM),
        cost_estimate=pl.CostEstimate(flops=2 * 5 * 2 * 1024 * 2176 * 128, bytes_accessed=16 * 1024 * 1024, transcendentals=2 * 1024 * 2176),
        name="qry_back",
    )(req, slot, owner, me, kvg, q, do, kq, vq, dq_psg)


MESH = pl.DeviceIdType.MESH


def place():
    me = lax.axis_index("psg")
    return me // 8, lax.rem(me // 2, 4), lax.rem(me, 2)


def at_plane(z, x, c):
    return {"psg": (z * 4 + x) * 2 + c}


def turn(i, by):
    return lax.rem(i + by + 4, 4)


def greet(devices):
    barrier = pltpu.get_barrier_semaphore()
    for device in devices:
        pl.semaphore_signal(barrier, inc=1, device_id=device, device_id_type=MESH)
    pl.semaphore_wait(barrier, len(devices))


def plane_neighbours(z, x, c):
    return [
        at_plane(turn(z, 1), x, c),
        at_plane(turn(z, -1), x, c),
        at_plane(z, turn(x, 1), c),
        at_plane(z, turn(x, -1), c),
        at_plane(z, x, 1 - c),
    ]


class Sender:
    def __init__(self, sems):
        self.sems = sems
        self.started = []

    def __call__(self, src, dst, recv_sem, device):
        copy = pltpu.make_async_remote_copy(
            src_ref=src, dst_ref=dst, send_sem=self.sems.at[len(self.started)], recv_sem=recv_sem,
            device_id=device, device_id_type=MESH,
        )
        copy.start()
        self.started.append(copy)

    def finish(self):
        for copy in self.started:
            copy.wait_send()


def arrived(ref, sem):
    pltpu.make_async_copy(ref, ref, sem).wait()


def lane_device(a, b, c):
    return at_plane(a * (1 - c) + b * c, b * (1 - c) + a * c, c)


def gather_kernel(
    q_ref, k_ref, v_ref, do_ref, wk_ref, wv_ref, all_ref, near_ref, far_ref, first_ref, dq_ref, own_k_ref, own_v_ref,
    lane, q_buf, do_buf, k_buf, v_buf, dq_buf, own_k_buf, own_v_buf,
    send_sem, recv_sem, core_sem, local_sem, swap_sem, near_sem, near_core_sem, far_sem, load_sem, keep_sem, first_sem, out_sem,
):
    z, x, c = place()
    y = lax.axis_index("head")
    a = z * (1 - c) + x * c
    b = x * (1 - c) + z * c
    half = k_ref.shape[0] // 2
    share = 2 * first_ref.shape[0]
    refs = (k_ref, v_ref)
    weights = (wk_ref, wv_ref)
    mine = [pltpu.make_async_copy(ref.at[pl.ds(c * half, half)], lane.at[a, b, c, i], local_sem.at[i]) for i, ref in enumerate(refs)]
    loads = [pltpu.make_async_copy(ref, buf, load_sem.at[i]) for i, (ref, buf) in enumerate(((q_ref, q_buf), (do_ref, do_buf), (k_ref, k_buf), (v_ref, v_buf)))]
    for copy in mine + loads:
        copy.start()
    greet(plane_neighbours(z, x, c) + [{"head": turn(y, by)} for by in (1, -1, 2)])
    send = Sender(send_sem)
    partner = at_plane(z, x, 1 - c)
    for i, ref in enumerate(refs):
        send(ref.at[pl.ds((1 - c) * half, half)], lane.at[b, a, c, i], swap_sem.at[i], partner)

    def columns(head):
        return pl.ds((2 * head + c) * share, share)

    for i, ref in enumerate(weights):
        for s, by in ((1, 1), (0, -1)):
            to = turn(y, by)
            send(ref.at[columns(to)], near_ref.at[s, i, pl.ds(c * share, share)], near_sem.at[s, i], {"head": to})
    for copy in mine:
        copy.wait()

    def whole(i, j, to):
        send(lane.at[i, j], lane.at[i, j], recv_sem.at[0, i, j], to)

    def piece(i, j, part, to):
        send(lane.at[i, j, part], lane.at[i, j, part], recv_sem.at[part, i, j], to)

    def keep(i, j):
        return pltpu.make_async_copy(lane.at[i, j], all_ref.at[c, i, j], keep_sem.at[i, j])

    def core(i, j):
        send(lane.at[i, j], all_ref.at[c, i, j], core_sem.at[i, j], partner)
        keep(i, j).start()

    def wait_whole(i, j):
        arrived(lane.at[i, j], recv_sem.at[0, i, j])

    def wait_pieces(i, j):
        for part in range(2):
            arrived(lane.at[i, j, part], recv_sem.at[part, i, j])

    def along_a(i, j):
        for by in (1, -1):
            whole(i, j, lane_device(turn(a, by), b, c))

    def own_passage(n, h):
        rows = slice(n * PLEN, (n + 1) * PLEN)
        thin = slice(h * D, (h + 1) * D)
        wide = slice(h * G * D, (h + 1) * G * D)
        gk, gv = passage(q_buf[rows, wide], k_buf[rows, thin], v_buf[rows, thin], do_buf[rows, wide], dq_buf, rows, h * G * D)
        own_k_buf[rows, thin] = gk
        own_v_buf[rows, thin] = gv

    ways = ((-1, 0), (1, 1))
    for part in (c, 1 - c):
        if part is not c:
            for i in range(2):
                arrived(lane.at[a, b, part, i], swap_sem.at[i])
        for by in (1, -1):
            piece(a, b, part, lane_device(a, turn(b, by), c))
        for by in (1, -1):
            piece(a, b, part, lane_device(turn(a, by), b, c))
    opposite = turn(y, 2)
    few = share // 2
    left = (2 * opposite + c) * share
    send(wk_ref.at[pl.ds(left, few)], first_ref, first_sem, {"head": opposite})
    across = [
        pltpu.make_async_copy(wk_ref.at[pl.ds(left + few, few)], far_ref.at[pl.ds(0, few)], far_sem.at[0]),
        pltpu.make_async_copy(wv_ref.at[pl.ds(left, share)], far_ref.at[pl.ds(few, share)], far_sem.at[1]),
    ]
    for copy in across:
        copy.start()
    for copy in loads:
        copy.wait()
    own_passage(0, 0)
    own_passage(0, 1)
    for by, part in ways:
        j = turn(b, by)
        wait_pieces(a, j)
        piece(a, j, part, lane_device(a, turn(b, -by), c))
    for by, part in ways:
        along_a(a, turn(b, by))
    own_passage(1, 0)

    def far(bo):
        j = turn(b, bo)
        for by, part in ways:
            i = turn(a, by)
            (wait_pieces if bo == 0 else wait_whole)(i, j)
            piece(i, j, part, lane_device(turn(a, -by), b, c))

    far(0)
    wait_pieces(a, turn(b, 2))
    along_a(a, turn(b, 2))
    own_passage(1, 1)
    results = ((dq_buf, dq_ref), (own_k_buf, own_k_ref), (own_v_buf, own_v_ref))
    stores = [pltpu.make_async_copy(buf, ref, out_sem.at[i]) for i, (buf, ref) in enumerate(results)]
    for copy in stores:
        copy.start()
    for bo in (0, -1, 1, 2):
        core(a, turn(b, bo))
    for by, _ in ways:
        core(turn(a, by), b)
    for bo in (-1, 1, 2):
        far(bo)
        for by, _ in ways:
            core(turn(a, by), turn(b, bo))
    for s in range(2):
        for i in range(2):
            block = near_ref.at[s, i, pl.ds(c * share, share)]
            arrived(block, near_sem.at[s, i])
            send(block, block, near_core_sem.at[s, i], partner)
    for bo in (0, -1, 1, 2):
        wait_pieces(turn(a, 2), turn(b, bo))
        core(turn(a, 2), turn(b, bo))
    for i in range(4):
        for j in range(4):
            arrived(all_ref.at[1 - c, i, j], core_sem.at[i, j])
            keep(i, j).wait()
    for s in range(2):
        for i in range(2):
            arrived(near_ref.at[s, i, pl.ds((1 - c) * share, share)], near_core_sem.at[s, i])
    for copy in across + stores:
        copy.wait()
    arrived(first_ref, first_sem)
    send.finish()


def gather_plane(q, k, v, do, w_key, w_value):
    rows, cols = k.shape
    width, depth = w_key.shape
    share = width // 8
    hbm = pl.BlockSpec(memory_space=pltpu.HBM)
    dma = pltpu.SemaphoreType.DMA
    return pl.pallas_call(
        gather_kernel,
        in_specs=[hbm] * 6,
        out_specs=[hbm] * 7,
        out_shape=[
            jax.ShapeDtypeStruct((2, 4, 4, 2, 2, rows // 2, cols), BF16),
            jax.ShapeDtypeStruct((2, 2, 2 * share, depth), BF16),
            jax.ShapeDtypeStruct((3 * share // 2, depth), BF16),
            jax.ShapeDtypeStruct((share // 2, depth), BF16),
            jax.ShapeDtypeStruct(q.shape, BF16),
            jax.ShapeDtypeStruct(k.shape, F32),
            jax.ShapeDtypeStruct(v.shape, F32),
        ],
        scratch_shapes=[
            pltpu.VMEM((4, 4, 2, 2, rows // 2, cols), BF16),
            pltpu.VMEM(q.shape, BF16),
            pltpu.VMEM(q.shape, BF16),
            pltpu.VMEM(k.shape, BF16),
            pltpu.VMEM(k.shape, BF16),
            pltpu.VMEM(q.shape, BF16),
            pltpu.VMEM(k.shape, F32),
            pltpu.VMEM(k.shape, F32),
            dma((51,)), dma((2, 4, 4)), dma((4, 4)), dma((2,)), dma((2,)), dma((2, 2)), dma((2, 2)), dma((2,)), dma((4,)),
            dma((4, 4)), dma, dma((3,)),
        ],
        compiler_params=pltpu.CompilerParams(collective_id=0, has_side_effects=True, vmem_limit_bytes=VMEM),
        name="gather_plane",
    )(q, k, v, do, w_key, w_value)


CUTS = 2
JOBS = CUTS + 1
ORDER = [
    ("f", 0), ("n", 0), (0, 0), ("f", 1), ("o", 0), ("w", 0), (0, 1), ("n", 1), ("o", 1), (1, 0), (1, 1),
    (2, 0), ("q", 0), (3, 0), (2, 1), (3, 1), (4, 0), (4, 1),
]


def tail_kernel(
    full_ref, own_k_ref, own_v_ref, qk_ref, qv_ref, wk_ref, wv_ref, near_ref, far_ref, first_ref, dx_psg_ref, dx_qry_ref,
    mine, other, relay1, side1, part, got, rows, weights, acc, terms,
    send_sem, core_sem, relay1_sem, side1_sem, got_sem, local_sem,
    load_sem, far_sem, rows_sem, out_sem, query_sem,
):
    z, x, c = place()
    y = lax.axis_index("head")
    a = z * (1 - c) + x * c
    b = x * (1 - c) + z * c
    partner = at_plane(z, x, 1 - c)
    steps = (1, -1)
    halves = (pl.ds(0, 2), pl.ds(2, 2))
    quarter = dx_qry_ref.shape[0]
    width = dx_qry_ref.shape[1] // 4
    share = width // 2
    heads = [y, turn(y, 1), turn(y, -1), turn(y, 2)]
    mirror = (0, 2, 1, 3)
    few = dx_psg_ref.shape[0] // CUTS
    size = [few] * CUTS + [quarter]

    loads = {}
    for q in range(CUTS):
        for by in (2, 1, -1, 0):
            i = turn(a, by)
            loads[q, by] = pltpu.make_async_copy(full_ref.at[c, i, :, :, :, :, q], mine.at[q, i], local_sem.at[q, i])
            loads[q, by].start()
    weight_loads = []
    for i, ref in enumerate((wk_ref, wv_ref)):
        weight_loads.append(pltpu.make_async_copy(ref.at[pl.ds(y * width, width)], weights.at[0, i], load_sem.at[0, i]))
        for s in range(2):
            weight_loads.append(pltpu.make_async_copy(near_ref.at[s, i], weights.at[1 + s, i], load_sem.at[1 + s, i]))
    cut = share // 2
    far_parts = (
        (first_ref, (3, 0, pl.ds(c * share, cut))),
        (far_ref.at[pl.ds(0, cut)], (3, 0, pl.ds(c * share + cut, cut))),
        (far_ref.at[pl.ds(cut, share)], (3, 1, pl.ds(c * share, share))),
    )
    for i, (ref, to) in enumerate(far_parts):
        weight_loads.append(pltpu.make_async_copy(ref, weights.at[to], load_sem.at[3, i]))
    for load in weight_loads:
        load.start()
    query_loads = [pltpu.make_async_copy(ref, rows.at[CUTS, 0, i], query_sem.at[i]) for i, ref in enumerate((qk_ref, qv_ref))]
    for load in query_loads:
        load.start()
    senders = [partner, lane_device(turn(a, 1), b, c), lane_device(turn(a, -1), b, c)]
    senders += [at_plane(z, turn(x, by), 0) for by in (1, -1, 2)] + [at_plane(turn(z, by), x, 1) for by in (1, -1, 2)]
    greet(senders + [{"head": head} for head in heads[1:]])
    send = Sender(send_sem)

    def spread(job):
        used = pl.ds(0, 4 * size[job])
        for p in (3, 1, 2):
            for i in range(2):
                send(rows.at[job, 0, i, used], rows.at[job, mirror[p], i, used], rows_sem.at[job, mirror[p], i], {"head": heads[p]})

    for load in query_loads:
        load.wait()
    spread(CUTS)

    def stage0(q, by):
        i = turn(b, by)
        send(full_ref.at[1 - c, i, :, :, :, :, q], other.at[q, i], core_sem.at[q, i], partner)

    def share_far():
        for i, (ref, to) in enumerate(far_parts):
            send(ref, weights.at[to], far_sem.at[i], partner)

    def pair(q, by):
        i = turn(a, by)
        loads[q, by].wait()
        arrived(other.at[q, i], core_sem.at[q, i])
        mine[q, i] = mine[q, i] + other[q, i]
        return i

    def ring1_far(q):
        i = pair(q, 2)
        for s in range(2):
            to = lane_device(turn(a, steps[s]), b, c)
            send(mine.at[q, i, halves[s]], relay1.at[q, s], relay1_sem.at[q, s], to)

    def ring1_near(q):
        for s in range(2):
            i = pair(q, steps[s])
            arrived(relay1.at[q, s], relay1_sem.at[q, s])
            mine[q, i, halves[s]] = mine[q, i, halves[s]] + relay1[q, s]
            send(mine.at[q, i], side1.at[q, s], side1_sem.at[q, s], lane_device(i, b, c))

    def join1(q, j):
        total = mine[q, a, j].astype(F32)
        for s in range(2):
            total = total + side1[q, s, j].astype(F32)
        part[q, j] = total.astype(BF16)

    def ring2(q):
        pair(q, 0)
        for s in range(2):
            arrived(side1.at[q, s], side1_sem.at[q, s])
        for r, by in enumerate((2, 1, -1, 0)):
            j = turn(b, by)
            join1(q, j)
            for core in range(2):
                if by != 0:
                    to = at_plane(a * (1 - c) + j * c, j * (1 - c) + a * c, core)
                    send(part.at[q, j, core], got.at[q, c, r], got_sem.at[q, c, r], to)
        send(part.at[q, b, 1 - c], got.at[q, c, 3], got_sem.at[q, c, 3], partner)

    def finish_rows(q):
        for n in range(2):
            for r in range(3):
                arrived(got.at[q, n, r], got_sem.at[q, n, r])
        arrived(got.at[q, 1 - c, 3], got_sem.at[q, 1 - c, 3])
        got[q, c, 3] = part[q, b, c]
        for n in range(2):
            for i, own_ref in enumerate((own_k_ref, own_v_ref)):
                total = got[q, n, 0, i].astype(F32)
                for r in range(1, 4):
                    total = total + got[q, n, r, i].astype(F32)
                for g in range(2):
                    h = 2 * n + g
                    top = (CUTS * h + q) * few
                    rows[q, 0, i, h * few:(h + 1) * few, :] = (own_ref[top:top + few, :] + total[g]).astype(BF16)
        spread(q)

    def product(job, p, done):
        used = pl.ds(0, 4 * size[job])
        for j in range(4):
            cols = pl.ds(j * (width // 4), width // 4)
            total = dot_t(rows[job, p, 0, used], weights[p, 0, cols, :]) + dot_t(rows[job, p, 1, used], weights[p, 1, cols, :])
            if p > 0:
                total = acc[used, cols] + total
            if p < 3:
                acc[used, cols] = total
            else:
                total = total.astype(BF16)
                for d in range(4):
                    terms[job, d, pl.ds(0, size[job]), cols] = total[d * size[job]:(d + 1) * size[job]]
                done(j)

    def target(job):
        return (dx_qry_ref, 0) if job == CUTS else (dx_psg_ref, job * few)

    def piece_of(job, head, j):
        out_ref, top = target(job)
        left = head * width + j * (width // 4)
        return out_ref.at[pl.ds(top, size[job]), pl.ds(pl.multiple_of(left, width // 4), width // 4)]

    def job_terms(job):
        used = pl.ds(0, size[job])

        def done(j):
            cols = pl.ds(j * (width // 4), width // 4)
            for p in (3, 1, 2):
                send(terms.at[job, heads[p], used, cols], piece_of(job, y, j), out_sem.at[job, mirror[p], j], {"head": heads[p]})

        for p in range(4):
            if p > 0:
                for i in range(2):
                    block = rows.at[job, p, i, pl.ds(0, 4 * size[job])]
                    arrived(block, rows_sem.at[job, p, i])
            product(job, p, done)
        out_ref, top = target(job)
        out_ref[pl.ds(top, size[job]), pl.ds(pl.multiple_of(y * width, width), width)] = terms[job, y, used]

    def job_wait(job):
        for p in (1, 2, 3):
            for j in range(4):
                arrived(piece_of(job, heads[p], j), out_sem.at[job, p, j])

    def query_job():
        for load in weight_loads:
            load.wait()
        there = (1 - c) * share
        for i, to in enumerate(((3, 0, pl.ds(there, cut)), (3, 0, pl.ds(there + cut, cut)), (3, 1, pl.ds(there, share)))):
            arrived(weights.at[to], far_sem.at[i])
        job_terms(CUTS)

    steps_of = {
        "f": lambda q: stage0(q, 2),
        "n": lambda q: (stage0(q, 1), stage0(q, -1)),
        "o": lambda q: stage0(q, 0),
        "w": lambda q: share_far(),
        "q": lambda q: query_job(),
        0: ring1_far,
        1: ring1_near,
        2: ring2,
        3: finish_rows,
        4: job_terms,
    }
    for step, q in ORDER:
        steps_of[step](q)
    for job in [CUTS] + list(range(CUTS)):
        job_wait(job)
    send.finish()


def tail(full, own_k, own_v, gk_qry, gv_qry, w_key, w_value, near, far, first):
    rows, cols = own_k.shape
    width, depth = w_key.shape
    quarter = rows // 8
    few = rows // 4 // CUTS
    hbm = pl.BlockSpec(memory_space=pltpu.HBM)
    vmem = pl.BlockSpec(memory_space=pltpu.VMEM)
    dma = pltpu.SemaphoreType.DMA
    block = (2, 2, 2, few, cols)
    full = full.reshape(2, 4, 4, 2, 2, 2, CUTS, few, cols)
    return pl.pallas_call(
        tail_kernel,
        in_specs=[hbm, vmem, vmem, hbm, hbm, hbm, hbm, hbm, pl.BlockSpec(memory_space=pl.ANY), hbm],
        out_specs=[vmem, vmem],
        out_shape=[jax.ShapeDtypeStruct((2 * quarter, width), BF16), jax.ShapeDtypeStruct((quarter, width), BF16)],
        scratch_shapes=[
            pltpu.VMEM((CUTS, 4, 4) + block, BF16),
            pltpu.VMEM((CUTS, 4, 4) + block, BF16),
            pltpu.VMEM((CUTS, 2, 2) + block, BF16),
            pltpu.VMEM((CUTS, 2, 4) + block, BF16),
            pltpu.VMEM((CUTS, 4) + block, BF16),
            pltpu.VMEM((CUTS, 2, 4) + block[1:], BF16),
            pltpu.VMEM((JOBS, 4, 2, 4 * quarter, cols), BF16),
            pltpu.VMEM((4, 2, width // 4, depth), BF16),
            pltpu.VMEM((4 * quarter, width // 4), F32),
            pltpu.VMEM((JOBS, 4, quarter, width // 4), BF16),
            dma((15 * CUTS + 3 + 18 * JOBS,)),
            dma((CUTS, 4)),
            dma((CUTS, 2)),
            dma((CUTS, 2)),
            dma((CUTS, 2, 4)),
            dma((CUTS, 4)),
            dma((4, 3)),
            dma((3,)),
            dma((JOBS, 4, 2)),
            dma((JOBS, 4, 4)),
            dma((2,)),
        ],
        compiler_params=pltpu.CompilerParams(collective_id=3, has_side_effects=True, vmem_limit_bytes=48 * 1024 * 1024),
        name="tail",
    )(full, own_k, own_v, gk_qry, gv_qry, w_key, w_value, near, far, first)


def local(q_psg, k_psg, v_psg, do_psg, q_qry, k_qry, v_qry, do_qry, w_key, w_value, req_passages, passage_slot, query_owner):
    me = lax.axis_index("psg").astype(jnp.int32).reshape(1)
    every, near, far, first, dq_psg, own_k, own_v = gather_plane(q_psg, k_psg, v_psg, do_psg, w_key, w_value)
    far = lax.ppermute(far, "head", [(i, (i + 2) % 4) for i in range(4)])
    dq_qry, gk_qry, gv_qry, full, dq_psg = qry_back(
        req_passages, passage_slot, query_owner, me, every.reshape(NPSG, 2, PLEN, -1), q_qry, do_qry, k_qry, v_qry, dq_psg
    )
    dx_psg, dx_qry = tail(full, own_k, own_v, gk_qry, gv_qry, w_key, w_value, near, far, first)
    return dq_psg, dq_qry, dx_psg, dx_qry


def solution(mesh):
    rows = P("psg", "head")
    return jax.shard_map(
        local,
        mesh=mesh,
        in_specs=(rows,) * 8 + (P(None, "head"),) * 2 + (P(),) * 3,
        out_specs=(rows, rows, P(("psg", "head"), None), P(("psg", "head"), None)),
        check_vma=False,
    )
```

```python
import functools

import jax
import jax.numpy as jnp
from jax import lax
from jax.experimental import pallas as pl
from jax.experimental.pallas import tpu as pltpu
from jax.sharding import PartitionSpec as P

D = 128
G = 8
PLEN = 128
KV = 2
NPSG = 64
REQ = 32
P_REQ = 16
CB = 256
C = D ** -0.5
C2 = C * 1.4426950408889634
VMEM = 62 * 1024 * 1024
F32 = jnp.float32
BF16 = jnp.bfloat16


def stack(x):
    return jnp.concatenate([x[:, g * D:(g + 1) * D] for g in range(G)], axis=0)


def dot(a, b):
    return jnp.dot(a, b, preferred_element_type=F32)


def dot_t(a, b):
    return lax.dot_general(a, b, (((1,), (1,)), ((), ())), preferred_element_type=F32)


def causal_cols(shape):
    key = lax.broadcasted_iota(jnp.int32, shape, 0)
    qry = lax.broadcasted_iota(jnp.int32, shape, 1) % PLEN
    return key <= qry


def passage(q, k, v, do, dq_ref, rows, left):
    qs = stack(q)
    dos = stack(do)
    kt = k.T
    gk = jnp.zeros((PLEN, D), F32)
    gv = jnp.zeros((PLEN, D), F32)
    for b in range(G * PLEN // CB):
        cols = slice(b * CB, (b + 1) * CB)
        s = dot_t(k, qs[cols])
        s = jnp.where(causal_cols(s.shape), s, -1e30)
        e = jnp.exp2((s - jnp.max(s, axis=0, keepdims=True)) * C2)
        inv = 1.0 / jnp.sum(e, axis=0, keepdims=True)
        dp = dot_t(v, dos[cols])
        p = e * inv
        delta = jnp.sum(p * dp, axis=0, keepdims=True)
        ds = (p * (dp - delta)).astype(BF16)
        gk += dot(ds, qs[cols])
        gv += dot(p.astype(BF16), dos[cols])
        dqt = dot(kt, ds) * C
        for i in range(CB // PLEN):
            at = left + (b * (CB // PLEN) + i) * D
            dq_ref[rows, at:at + D] = dqt[:, i * PLEN:(i + 1) * PLEN].T.astype(BF16)
    return gk * C, gv


TK = 1024
TP = TK // PLEN
NT = P_REQ * PLEN // TK


def spot(slot):
    n = slot % 2
    c = slot // 2 % 2
    x = slot // 4 % 4
    z = slot // 16
    return n * 32 + jnp.where(n == 0, z * 4 + x, x * 4 + z) * 2 + c


def qry_kernel(
    req_ref, slot_ref, owner_ref, me_ref, kvg_ref, q_any, do_any, kq_any, vq_any, dq_in_ref,
    dq_ref, g_ref, full_ref, dq_out_ref,
    held, kv, q_ref, do_ref, kq_ref, vq_ref, qs, dos, qst, dost, ktbuf, sbuf, dpbuf, dqt, gbuf, zeros, slots, mask,
    load_sem, in_sem, out_sem, zero_sem, hand_sem,
):
    me = me_ref[0]
    take = pltpu.make_async_copy(dq_in_ref, held, hand_sem.at[0])
    give = pltpu.make_async_copy(held, dq_out_ref, hand_sem.at[1])
    pairs = ((q_any, q_ref), (do_any, do_ref), (kq_any, kq_ref), (vq_any, vq_ref))
    loads = [pltpu.make_async_copy(ref, buf, load_sem.at[i]) for i, (ref, buf) in enumerate(pairs)]
    for copy in loads:
        copy.start()
    zeros[...] = jnp.zeros_like(zeros)
    request = jnp.int32(0)
    for r in range(REQ):
        request = jnp.where(owner_ref[r] == me, r, request)

    def clear(i, carry):
        mask[i] = 0
        return carry

    lax.fori_loop(0, NPSG, clear, 0)

    def pick(j, carry):
        slot = spot(slot_ref[req_ref[request, j]])
        slots[j] = slot
        mask[slot] = 1
        pltpu.make_async_copy(kvg_ref.at[slot], kv.at[j], in_sem).start()
        return carry

    lax.fori_loop(0, P_REQ, pick, 0)

    def blank(wait):
        def one(i, carry):
            @pl.when(mask[i] == 0)
            def _():
                copy = pltpu.make_async_copy(zeros, full_ref.at[i], zero_sem)
                copy.wait() if wait else copy.start()

            return carry

        lax.fori_loop(0, NPSG, one, 0)

    blank(False)
    for copy in loads:
        copy.wait()
    take.start()

    def land(j, carry):
        pltpu.make_async_copy(kvg_ref.at[slots[j]], kv.at[j], in_sem).wait()
        return carry

    blocks = [slice(i * CB, (i + 1) * CB) for i in range(G * PLEN // CB)]
    own = slice(P_REQ * PLEN, P_REQ * PLEN + PLEN)

    def tile(t, part, cols):
        return kv[pl.ds(t * TP, TP), part, :, cols].reshape(TK, D)

    def tile_rows(t):
        return pl.ds(pl.multiple_of(t * TK, TK), TK)

    def fold(x, op):
        return op(x.reshape(-1, 8, x.shape[1]), axis=0)

    for h in range(KV):
        cols = slice(h * D, (h + 1) * D)
        wide = slice(h * G * D, (h + 1) * G * D)
        qs[...] = stack(q_ref[:, wide])
        dos[...] = stack(do_ref[:, wide])
        qst[...] = qs[...].T
        dost[...] = dos[...].T
        kq = kq_ref[:, cols]
        vq = vq_ref[:, cols]

        def scores(keys, rows, masked, high):
            highs = []
            for b in blocks:
                s = dot(keys, qst[:, b])
                if masked:
                    s = jnp.where(causal_cols(s.shape), s, -1e30)
                sbuf[rows, b] = s
                highs.append(jnp.maximum(high[:, b], fold(s, jnp.max)))
            return jnp.concatenate(highs, axis=1)

        def score_tile(t, high):
            keys = tile(t, 0, cols)
            ktbuf[t] = keys.T
            return scores(keys, tile_rows(t), False, high)

        high = scores(kq, own, True, jnp.full((8, G * PLEN), -1e30, F32))
        if h == 0:
            lax.fori_loop(0, P_REQ, land, 0)
        high = lax.fori_loop(0, NT, score_tile, high)
        m2 = jnp.max(high, axis=0, keepdims=True) * C2

        def sums(values, rows, carry):
            l, num = carry
            ls, nums = [], []
            for b in blocks:
                dp = dot(values, dost[:, b])
                dpbuf[rows, b] = dp
                e = jnp.exp2(sbuf[rows, b] * C2 - m2[:, b])
                ls.append(l[:, b] + fold(e, jnp.sum))
                nums.append(num[:, b] + fold(e * dp, jnp.sum))
            return jnp.concatenate(ls, axis=1), jnp.concatenate(nums, axis=1)

        def sum_tile(t, carry):
            return sums(tile(t, 1, cols), tile_rows(t), carry)

        nothing = jnp.zeros((8, G * PLEN), F32)
        carry = sums(vq, own, (nothing, nothing))
        l, num = lax.fori_loop(0, NT, sum_tile, carry)
        l = jnp.sum(l, axis=0, keepdims=True)
        delta = jnp.sum(num, axis=0, keepdims=True) / l
        level = m2 + jnp.log2(l)

        def grads(kt, rows, first):
            gk = gv = None
            for b in blocks:
                p = jnp.exp2(sbuf[rows, b] * C2 - level[:, b])
                ds = (p * (dpbuf[rows, b] - delta[:, b])).astype(BF16)
                dk = dot(ds, qs[b, :])
                dv = dot(p.astype(BF16), dos[b, :])
                gk = dk if gk is None else gk + dk
                gv = dv if gv is None else gv + dv
                more = dot(kt, ds)
                dqt[:, b] = more if first else dqt[:, b] + more
            return (gk * C).astype(BF16), gv.astype(BF16)

        if h == 0:
            take.wait()
            give.start()
        gk, gv = grads(kq.T, own, True)
        g_ref[0, :, cols] = gk
        g_ref[1, :, cols] = gv

        def grad_tile(t, carry):
            gk, gv = grads(ktbuf[t], tile_rows(t), False)
            for i in range(TP):
                j = t * TP + i
                gbuf[j, 0, :, cols] = gk[i * PLEN:(i + 1) * PLEN]
                gbuf[j, 1, :, cols] = gv[i * PLEN:(i + 1) * PLEN]
                if h == KV - 1:
                    pltpu.make_async_copy(gbuf.at[j], full_ref.at[slots[j]], out_sem).start()
            return carry

        lax.fori_loop(0, NT, grad_tile, 0)
        for g in range(G):
            left = h * G * D + g * D
            dq_ref[:, left:left + D] = (dqt[:, g * PLEN:(g + 1) * PLEN] * C).T.astype(BF16)

    def drain(j, carry):
        pltpu.make_async_copy(gbuf.at[j], full_ref.at[slots[j]], out_sem).wait()
        return carry

    lax.fori_loop(0, P_REQ, drain, 0)
    blank(True)
    give.wait()


def qry_back(req, slot, owner, me, kvg, q, do, kq, vq, dq_psg):
    keys = P_REQ * PLEN + PLEN
    smem = pl.BlockSpec(memory_space=pltpu.SMEM)
    hbm = pl.BlockSpec(memory_space=pltpu.HBM)
    vmem = pl.BlockSpec(memory_space=pltpu.VMEM)
    return pl.pallas_call(
        qry_kernel,
        in_specs=[smem] * 4 + [hbm] * 6,
        out_specs=[vmem, vmem, hbm, hbm],
        out_shape=[
            jax.ShapeDtypeStruct(q.shape, BF16),
            jax.ShapeDtypeStruct((2,) + kq.shape, BF16),
            jax.ShapeDtypeStruct((NPSG, 2, PLEN, KV * D), BF16),
            jax.ShapeDtypeStruct(dq_psg.shape, BF16),
        ],
        scratch_shapes=[
            pltpu.VMEM(dq_psg.shape, BF16),
            pltpu.VMEM((P_REQ, 2, PLEN, KV * D), BF16),
            pltpu.VMEM(q.shape, BF16),
            pltpu.VMEM(q.shape, BF16),
            pltpu.VMEM(kq.shape, BF16),
            pltpu.VMEM(kq.shape, BF16),
            pltpu.VMEM((G * PLEN, D), BF16),
            pltpu.VMEM((G * PLEN, D), BF16),
            pltpu.VMEM((D, G * PLEN), BF16),
            pltpu.VMEM((D, G * PLEN), BF16),
            pltpu.VMEM((NT, D, TK), BF16),
            pltpu.VMEM((keys, G * PLEN), F32),
            pltpu.VMEM((keys, G * PLEN), F32),
            pltpu.VMEM((D, G * PLEN), F32),
            pltpu.VMEM((P_REQ, 2, PLEN, KV * D), BF16),
            pltpu.VMEM((2, PLEN, KV * D), BF16),
            pltpu.SMEM((P_REQ,), jnp.int32),
            pltpu.SMEM((NPSG,), jnp.int32),
            pltpu.SemaphoreType.DMA((4,)),
            pltpu.SemaphoreType.DMA,
            pltpu.SemaphoreType.DMA,
            pltpu.SemaphoreType.DMA,
            pltpu.SemaphoreType.DMA((2,)),
        ],
        compiler_params=pltpu.CompilerParams(vmem_limit_bytes=VMEM),
        cost_estimate=pl.CostEstimate(flops=2 * 5 * 2 * 1024 * 2176 * 128, bytes_accessed=16 * 1024 * 1024, transcendentals=2 * 1024 * 2176),
        name="qry_back",
    )(req, slot, owner, me, kvg, q, do, kq, vq, dq_psg)


MESH = pl.DeviceIdType.MESH


def place():
    me = lax.axis_index("psg")
    return me // 8, lax.rem(me // 2, 4), lax.rem(me, 2)


def at_plane(z, x, c):
    return {"psg": (z * 4 + x) * 2 + c}


def turn(i, by):
    return lax.rem(i + by + 4, 4)


def greet(devices):
    barrier = pltpu.get_barrier_semaphore()
    for device in devices:
        pl.semaphore_signal(barrier, inc=1, device_id=device, device_id_type=MESH)
    pl.semaphore_wait(barrier, len(devices))


def plane_neighbours(z, x, c):
    return [
        at_plane(turn(z, 1), x, c),
        at_plane(turn(z, -1), x, c),
        at_plane(z, turn(x, 1), c),
        at_plane(z, turn(x, -1), c),
        at_plane(z, x, 1 - c),
    ]


class Sender:
    def __init__(self, sems):
        self.sems = sems
        self.started = []

    def __call__(self, src, dst, recv_sem, device):
        copy = pltpu.make_async_remote_copy(
            src_ref=src, dst_ref=dst, send_sem=self.sems.at[len(self.started)], recv_sem=recv_sem,
            device_id=device, device_id_type=MESH,
        )
        copy.start()
        self.started.append(copy)

    def finish(self):
        for copy in self.started:
            copy.wait_send()


def arrived(ref, sem):
    pltpu.make_async_copy(ref, ref, sem).wait()


def lane_device(a, b, c):
    return at_plane(a * (1 - c) + b * c, b * (1 - c) + a * c, c)


def gather_kernel(
    q_ref, k_ref, v_ref, do_ref, wk_ref, wv_ref, all_ref, near_ref, far_ref, first_ref, dq_ref, own_k_ref, own_v_ref,
    lane, q_buf, do_buf, k_buf, v_buf, dq_buf, own_k_buf, own_v_buf, far_buf,
    send_sem, recv_sem, core_sem, local_sem, swap_sem, near_sem, near_core_sem, far_sem, load_sem, keep_sem, first_sem, out_sem,
):
    z, x, c = place()
    y = lax.axis_index("head")
    a = z * (1 - c) + x * c
    b = x * (1 - c) + z * c
    half = k_ref.shape[0] // 2
    share = 2 * first_ref.shape[0]
    refs = (k_ref, v_ref)
    weights = (wk_ref, wv_ref)
    mine = [pltpu.make_async_copy(ref.at[pl.ds(c * half, half)], lane.at[a, b, c, i], local_sem.at[i]) for i, ref in enumerate(refs)]
    loads = [pltpu.make_async_copy(ref, buf, load_sem.at[i]) for i, (ref, buf) in enumerate(((q_ref, q_buf), (do_ref, do_buf), (k_ref, k_buf), (v_ref, v_buf)))]
    for copy in mine + loads:
        copy.start()
    greet(plane_neighbours(z, x, c) + [{"head": turn(y, by)} for by in (1, -1, 2)])
    send = Sender(send_sem)
    partner = at_plane(z, x, 1 - c)
    for i, ref in enumerate(refs):
        send(ref.at[pl.ds((1 - c) * half, half)], lane.at[b, a, c, i], swap_sem.at[i], partner)

    def columns(head):
        return pl.ds((2 * head + c) * share, share)

    for i, ref in enumerate(weights):
        for s, by in ((1, 1), (0, -1)):
            to = turn(y, by)
            send(ref.at[columns(to)], near_ref.at[s, i, pl.ds(c * share, share)], near_sem.at[s, i], {"head": to})
    for copy in mine:
        copy.wait()

    def whole(i, j, to):
        send(lane.at[i, j], lane.at[i, j], recv_sem.at[0, i, j], to)

    def piece(i, j, part, to):
        send(lane.at[i, j, part], lane.at[i, j, part], recv_sem.at[part, i, j], to)

    def keep(i, j):
        return pltpu.make_async_copy(lane.at[i, j], all_ref.at[c, i, j], keep_sem.at[i, j])

    def core(i, j):
        send(lane.at[i, j], all_ref.at[c, i, j], core_sem.at[i, j], partner)
        keep(i, j).start()

    def wait_whole(i, j):
        arrived(lane.at[i, j], recv_sem.at[0, i, j])

    def wait_pieces(i, j):
        for part in range(2):
            arrived(lane.at[i, j, part], recv_sem.at[part, i, j])

    def along_a(i, j):
        for by in (1, -1):
            whole(i, j, lane_device(turn(a, by), b, c))

    def own_passage(n, h):
        rows = slice(n * PLEN, (n + 1) * PLEN)
        thin = slice(h * D, (h + 1) * D)
        wide = slice(h * G * D, (h + 1) * G * D)
        gk, gv = passage(q_buf[rows, wide], k_buf[rows, thin], v_buf[rows, thin], do_buf[rows, wide], dq_buf, rows, h * G * D)
        own_k_buf[rows, thin] = gk
        own_v_buf[rows, thin] = gv

    ways = ((-1, 0), (1, 1))
    for part in (c, 1 - c):
        if part is not c:
            for i in range(2):
                arrived(lane.at[a, b, part, i], swap_sem.at[i])
        for by in (1, -1):
            piece(a, b, part, lane_device(a, turn(b, by), c))
        for by in (1, -1):
            piece(a, b, part, lane_device(turn(a, by), b, c))
    opposite = turn(y, 2)
    few = share // 2
    left = (2 * opposite + c) * share
    send(wk_ref.at[pl.ds(left, few)], first_ref, first_sem, {"head": opposite})
    across = [
        pltpu.make_async_copy(wk_ref.at[pl.ds(left + few, few)], far_buf.at[pl.ds(0, few)], far_sem.at[0]),
        pltpu.make_async_copy(wv_ref.at[pl.ds(left, share)], far_buf.at[pl.ds(few, share)], far_sem.at[1]),
    ]
    for copy in across:
        copy.start()
    for copy in loads:
        copy.wait()
    own_passage(0, 0)
    own_passage(0, 1)
    for by, part in ways:
        j = turn(b, by)
        wait_pieces(a, j)
        piece(a, j, part, lane_device(a, turn(b, -by), c))
    for by, part in ways:
        along_a(a, turn(b, by))
    own_passage(1, 0)

    def far(bo):
        j = turn(b, bo)
        for by, part in ways:
            i = turn(a, by)
            (wait_pieces if bo == 0 else wait_whole)(i, j)
            piece(i, j, part, lane_device(turn(a, -by), b, c))

    far(0)
    wait_pieces(a, turn(b, 2))
    along_a(a, turn(b, 2))
    own_passage(1, 1)
    for copy in across:
        copy.wait()
    results = ((dq_buf, dq_ref), (own_k_buf, own_k_ref), (own_v_buf, own_v_ref), (far_buf, far_ref))
    stores = [pltpu.make_async_copy(buf, ref, out_sem.at[i]) for i, (buf, ref) in enumerate(results)]
    for copy in stores:
        copy.start()
    for bo in (0, -1, 1, 2):
        core(a, turn(b, bo))
    for by, _ in ways:
        core(turn(a, by), b)
    for bo in (-1, 1, 2):
        far(bo)
        for by, _ in ways:
            core(turn(a, by), turn(b, bo))
    for s in range(2):
        for i in range(2):
            block = near_ref.at[s, i, pl.ds(c * share, share)]
            arrived(block, near_sem.at[s, i])
            send(block, block, near_core_sem.at[s, i], partner)
    for bo in (0, -1, 1, 2):
        wait_pieces(turn(a, 2), turn(b, bo))
        core(turn(a, 2), turn(b, bo))
    for i in range(4):
        for j in range(4):
            arrived(all_ref.at[1 - c, i, j], core_sem.at[i, j])
            keep(i, j).wait()
    for s in range(2):
        for i in range(2):
            arrived(near_ref.at[s, i, pl.ds((1 - c) * share, share)], near_core_sem.at[s, i])
    for copy in stores:
        copy.wait()
    arrived(first_ref, first_sem)
    send.finish()


def gather_plane(q, k, v, do, w_key, w_value):
    rows, cols = k.shape
    width, depth = w_key.shape
    share = width // 8
    hbm = pl.BlockSpec(memory_space=pltpu.HBM)
    dma = pltpu.SemaphoreType.DMA
    return pl.pallas_call(
        gather_kernel,
        in_specs=[hbm] * 6,
        out_specs=[hbm] * 7,
        out_shape=[
            jax.ShapeDtypeStruct((2, 4, 4, 2, 2, rows // 2, cols), BF16),
            jax.ShapeDtypeStruct((2, 2, 2 * share, depth), BF16),
            jax.ShapeDtypeStruct((3 * share // 2, depth), BF16),
            jax.ShapeDtypeStruct((share // 2, depth), BF16),
            jax.ShapeDtypeStruct(q.shape, BF16),
            jax.ShapeDtypeStruct(k.shape, F32),
            jax.ShapeDtypeStruct(v.shape, F32),
        ],
        scratch_shapes=[
            pltpu.VMEM((4, 4, 2, 2, rows // 2, cols), BF16),
            pltpu.VMEM(q.shape, BF16),
            pltpu.VMEM(q.shape, BF16),
            pltpu.VMEM(k.shape, BF16),
            pltpu.VMEM(k.shape, BF16),
            pltpu.VMEM(q.shape, BF16),
            pltpu.VMEM(k.shape, F32),
            pltpu.VMEM(k.shape, F32),
            pltpu.VMEM((3 * share // 2, depth), BF16),
            dma((51,)), dma((2, 4, 4)), dma((4, 4)), dma((2,)), dma((2,)), dma((2, 2)), dma((2, 2)), dma((2,)), dma((4,)),
            dma((4, 4)), dma, dma((4,)),
        ],
        compiler_params=pltpu.CompilerParams(collective_id=0, has_side_effects=True, vmem_limit_bytes=VMEM),
        name="gather_plane",
    )(q, k, v, do, w_key, w_value)


CUTS = 2
JOBS = CUTS + 1
ORDER = [
    ("f", 0), ("n", 0), (0, 0), ("f", 1), ("o", 0), ("w", 0), (0, 1), ("n", 1), ("o", 1), (1, 0), (1, 1),
    (2, 0), ("q", 0), (3, 0), (2, 1), (3, 1), (4, 0), (4, 1),
]


def tail_kernel(
    full_ref, own_k_ref, own_v_ref, query_ref, wk_ref, wv_ref, near_ref, far_ref, first_ref, dx_psg_ref, dx_qry_ref,
    mine, other, relay1, side1, part, got, rows, weights, acc, terms,
    send_sem, core_sem, relay1_sem, side1_sem, got_sem, local_sem,
    load_sem, far_sem, rows_sem, out_sem, query_sem,
):
    z, x, c = place()
    y = lax.axis_index("head")
    a = z * (1 - c) + x * c
    b = x * (1 - c) + z * c
    partner = at_plane(z, x, 1 - c)
    steps = (1, -1)
    halves = (pl.ds(0, 2), pl.ds(2, 2))
    quarter = dx_qry_ref.shape[0]
    width = dx_qry_ref.shape[1] // 4
    share = width // 2
    heads = [y, turn(y, 1), turn(y, -1), turn(y, 2)]
    mirror = (0, 2, 1, 3)
    few = dx_psg_ref.shape[0] // CUTS
    size = [few] * CUTS + [quarter]

    loads = {}
    for q in range(CUTS):
        for by in (2, 1, -1, 0):
            i = turn(a, by)
            loads[q, by] = pltpu.make_async_copy(full_ref.at[c, i, :, :, :, :, q], mine.at[q, i], local_sem.at[q, i])
            loads[q, by].start()
    weight_loads = []
    for i, ref in enumerate((wk_ref, wv_ref)):
        weight_loads.append(pltpu.make_async_copy(ref.at[pl.ds(y * width, width)], weights.at[0, i], load_sem.at[0, i]))
        for s in range(2):
            weight_loads.append(pltpu.make_async_copy(near_ref.at[s, i], weights.at[1 + s, i], load_sem.at[1 + s, i]))
    cut = share // 2
    far_parts = (
        (first_ref, (3, 0, pl.ds(c * share, cut))),
        (far_ref.at[pl.ds(0, cut)], (3, 0, pl.ds(c * share + cut, cut))),
        (far_ref.at[pl.ds(cut, share)], (3, 1, pl.ds(c * share, share))),
    )
    for i, (ref, to) in enumerate(far_parts):
        weight_loads.append(pltpu.make_async_copy(ref, weights.at[to], load_sem.at[3, i]))
    for load in weight_loads:
        load.start()
    query_load = pltpu.make_async_copy(query_ref, rows.at[CUTS, 0], query_sem)
    query_load.start()
    senders = [partner, lane_device(turn(a, 1), b, c), lane_device(turn(a, -1), b, c)]
    senders += [at_plane(z, turn(x, by), 0) for by in (1, -1, 2)] + [at_plane(turn(z, by), x, 1) for by in (1, -1, 2)]
    greet(senders + [{"head": head} for head in heads[1:]])
    send = Sender(send_sem)

    def spread(job):
        used = pl.ds(0, 4 * size[job])
        for p in (3, 1, 2):
            for i in range(2):
                send(rows.at[job, 0, i, used], rows.at[job, mirror[p], i, used], rows_sem.at[job, mirror[p], i], {"head": heads[p]})

    query_load.wait()
    spread(CUTS)

    def stage0(q, by):
        i = turn(b, by)
        send(full_ref.at[1 - c, i, :, :, :, :, q], other.at[q, i], core_sem.at[q, i], partner)

    def share_far():
        for i, (ref, to) in enumerate(far_parts):
            send(ref, weights.at[to], far_sem.at[i], partner)

    def pair(q, by):
        i = turn(a, by)
        loads[q, by].wait()
        arrived(other.at[q, i], core_sem.at[q, i])
        mine[q, i] = mine[q, i] + other[q, i]
        return i

    def ring1_far(q):
        i = pair(q, 2)
        for s in range(2):
            to = lane_device(turn(a, steps[s]), b, c)
            send(mine.at[q, i, halves[s]], relay1.at[q, s], relay1_sem.at[q, s], to)

    def ring1_near(q):
        for s in range(2):
            i = pair(q, steps[s])
            arrived(relay1.at[q, s], relay1_sem.at[q, s])
            mine[q, i, halves[s]] = mine[q, i, halves[s]] + relay1[q, s]
            send(mine.at[q, i], side1.at[q, s], side1_sem.at[q, s], lane_device(i, b, c))

    def join1(q, j):
        total = mine[q, a, j].astype(F32)
        for s in range(2):
            total = total + side1[q, s, j].astype(F32)
        part[q, j] = total.astype(BF16)

    def ring2(q):
        pair(q, 0)
        for s in range(2):
            arrived(side1.at[q, s], side1_sem.at[q, s])
        for r, by in enumerate((2, 1, -1, 0)):
            j = turn(b, by)
            join1(q, j)
            for core in range(2):
                if by != 0:
                    to = at_plane(a * (1 - c) + j * c, j * (1 - c) + a * c, core)
                    send(part.at[q, j, core], got.at[q, c, r], got_sem.at[q, c, r], to)
        send(part.at[q, b, 1 - c], got.at[q, c, 3], got_sem.at[q, c, 3], partner)

    def finish_rows(q):
        for n in range(2):
            for r in range(3):
                arrived(got.at[q, n, r], got_sem.at[q, n, r])
        arrived(got.at[q, 1 - c, 3], got_sem.at[q, 1 - c, 3])
        got[q, c, 3] = part[q, b, c]
        for n in range(2):
            for i, own_ref in enumerate((own_k_ref, own_v_ref)):
                total = got[q, n, 0, i].astype(F32)
                for r in range(1, 4):
                    total = total + got[q, n, r, i].astype(F32)
                for g in range(2):
                    h = 2 * n + g
                    top = (CUTS * h + q) * few
                    rows[q, 0, i, h * few:(h + 1) * few, :] = (own_ref[top:top + few, :] + total[g]).astype(BF16)
        spread(q)

    def product(job, p, done):
        used = pl.ds(0, 4 * size[job])
        for j in range(4):
            cols = pl.ds(j * (width // 4), width // 4)
            total = dot_t(rows[job, p, 0, used], weights[p, 0, cols, :]) + dot_t(rows[job, p, 1, used], weights[p, 1, cols, :])
            if p > 0:
                total = acc[used, cols] + total
            if p < 3:
                acc[used, cols] = total
            else:
                total = total.astype(BF16)
                for d in range(4):
                    terms[job, d, pl.ds(0, size[job]), cols] = total[d * size[job]:(d + 1) * size[job]]
                done(j)

    def target(job):
        return (dx_qry_ref, 0) if job == CUTS else (dx_psg_ref, job * few)

    def piece_of(job, head, j):
        out_ref, top = target(job)
        left = head * width + j * (width // 4)
        return out_ref.at[pl.ds(top, size[job]), pl.ds(pl.multiple_of(left, width // 4), width // 4)]

    def job_terms(job):
        used = pl.ds(0, size[job])

        def done(j):
            cols = pl.ds(j * (width // 4), width // 4)
            for p in (3, 1, 2):
                send(terms.at[job, heads[p], used, cols], piece_of(job, y, j), out_sem.at[job, mirror[p], j], {"head": heads[p]})

        for p in range(4):
            if p > 0:
                for i in range(2):
                    block = rows.at[job, p, i, pl.ds(0, 4 * size[job])]
                    arrived(block, rows_sem.at[job, p, i])
            product(job, p, done)
        out_ref, top = target(job)
        out_ref[pl.ds(top, size[job]), pl.ds(pl.multiple_of(y * width, width), width)] = terms[job, y, used]

    def job_wait(job):
        for p in (1, 2, 3):
            for j in range(4):
                arrived(piece_of(job, heads[p], j), out_sem.at[job, p, j])

    def query_job():
        for load in weight_loads:
            load.wait()
        there = (1 - c) * share
        for i, to in enumerate(((3, 0, pl.ds(there, cut)), (3, 0, pl.ds(there + cut, cut)), (3, 1, pl.ds(there, share)))):
            arrived(weights.at[to], far_sem.at[i])
        job_terms(CUTS)

    steps_of = {
        "f": lambda q: stage0(q, 2),
        "n": lambda q: (stage0(q, 1), stage0(q, -1)),
        "o": lambda q: stage0(q, 0),
        "w": lambda q: share_far(),
        "q": lambda q: query_job(),
        0: ring1_far,
        1: ring1_near,
        2: ring2,
        3: finish_rows,
        4: job_terms,
    }
    for step, q in ORDER:
        steps_of[step](q)
    for job in [CUTS] + list(range(CUTS)):
        job_wait(job)
    send.finish()


def tail(full, own_k, own_v, g_qry, w_key, w_value, near, far, first):
    rows, cols = own_k.shape
    width, depth = w_key.shape
    quarter = rows // 8
    few = rows // 4 // CUTS
    hbm = pl.BlockSpec(memory_space=pltpu.HBM)
    vmem = pl.BlockSpec(memory_space=pltpu.VMEM)
    dma = pltpu.SemaphoreType.DMA
    block = (2, 2, 2, few, cols)
    full = full.reshape(2, 4, 4, 2, 2, 2, CUTS, few, cols)
    return pl.pallas_call(
        tail_kernel,
        in_specs=[hbm, vmem, vmem, hbm, hbm, hbm, hbm, pl.BlockSpec(memory_space=pl.ANY), hbm],
        out_specs=[vmem, vmem],
        out_shape=[jax.ShapeDtypeStruct((2 * quarter, width), BF16), jax.ShapeDtypeStruct((quarter, width), BF16)],
        scratch_shapes=[
            pltpu.VMEM((CUTS, 4, 4) + block, BF16),
            pltpu.VMEM((CUTS, 4, 4) + block, BF16),
            pltpu.VMEM((CUTS, 2, 2) + block, BF16),
            pltpu.VMEM((CUTS, 2, 4) + block, BF16),
            pltpu.VMEM((CUTS, 4) + block, BF16),
            pltpu.VMEM((CUTS, 2, 4) + block[1:], BF16),
            pltpu.VMEM((JOBS, 4, 2, 4 * quarter, cols), BF16),
            pltpu.VMEM((4, 2, width // 4, depth), BF16),
            pltpu.VMEM((4 * quarter, width // 4), F32),
            pltpu.VMEM((JOBS, 4, quarter, width // 4), BF16),
            dma((15 * CUTS + 3 + 18 * JOBS,)),
            dma((CUTS, 4)),
            dma((CUTS, 2)),
            dma((CUTS, 2)),
            dma((CUTS, 2, 4)),
            dma((CUTS, 4)),
            dma((4, 3)),
            dma((3,)),
            dma((JOBS, 4, 2)),
            dma((JOBS, 4, 4)),
            dma,
        ],
        compiler_params=pltpu.CompilerParams(collective_id=3, has_side_effects=True, vmem_limit_bytes=48 * 1024 * 1024),
        name="tail",
    )(full, own_k, own_v, g_qry, w_key, w_value, near, far, first)


def local(q_psg, k_psg, v_psg, do_psg, q_qry, k_qry, v_qry, do_qry, w_key, w_value, req_passages, passage_slot, query_owner):
    me = lax.axis_index("psg").astype(jnp.int32).reshape(1)
    every, near, far, first, dq_psg, own_k, own_v = gather_plane(q_psg, k_psg, v_psg, do_psg, w_key, w_value)
    far = lax.ppermute(far, "head", [(i, (i + 2) % 4) for i in range(4)])
    dq_qry, g_qry, full, dq_psg = qry_back(
        req_passages, passage_slot, query_owner, me, every.reshape(NPSG, 2, PLEN, -1), q_qry, do_qry, k_qry, v_qry, dq_psg
    )
    dx_psg, dx_qry = tail(full, own_k, own_v, g_qry, w_key, w_value, near, far, first)
    return dq_psg, dq_qry, dx_psg, dx_qry


def solution(mesh):
    rows = P("psg", "head")
    return jax.shard_map(
        local,
        mesh=mesh,
        in_specs=(rows,) * 8 + (P(None, "head"),) * 2 + (P(),) * 3,
        out_specs=(rows, rows, P(("psg", "head"), None), P(("psg", "head"), None)),
        check_vma=False,
    )
```

```python
import functools

import jax
import jax.numpy as jnp
from jax import lax
from jax.experimental import pallas as pl
from jax.experimental.pallas import tpu as pltpu
from jax.sharding import PartitionSpec as P

D = 128
G = 8
PLEN = 128
KV = 2
NPSG = 64
REQ = 32
P_REQ = 16
CB = 256
C = D ** -0.5
C2 = C * 1.4426950408889634
VMEM = 62 * 1024 * 1024
F32 = jnp.float32
BF16 = jnp.bfloat16


def stack(x):
    return jnp.concatenate([x[:, g * D:(g + 1) * D] for g in range(G)], axis=0)


def dot(a, b):
    return jnp.dot(a, b, preferred_element_type=F32)


def dot_t(a, b):
    return lax.dot_general(a, b, (((1,), (1,)), ((), ())), preferred_element_type=F32)


def causal_cols(shape):
    key = lax.broadcasted_iota(jnp.int32, shape, 0)
    qry = lax.broadcasted_iota(jnp.int32, shape, 1) % PLEN
    return key <= qry


def passage(q, k, v, do, dq_ref, rows, left):
    qs = stack(q)
    dos = stack(do)
    kt = k.T
    gk = jnp.zeros((PLEN, D), F32)
    gv = jnp.zeros((PLEN, D), F32)
    for b in range(G * PLEN // CB):
        cols = slice(b * CB, (b + 1) * CB)
        s = dot_t(k, qs[cols])
        s = jnp.where(causal_cols(s.shape), s, -1e30)
        e = jnp.exp2((s - jnp.max(s, axis=0, keepdims=True)) * C2)
        inv = 1.0 / jnp.sum(e, axis=0, keepdims=True)
        dp = dot_t(v, dos[cols])
        p = e * inv
        delta = jnp.sum(p * dp, axis=0, keepdims=True)
        ds = (p * (dp - delta)).astype(BF16)
        gk += dot(ds, qs[cols])
        gv += dot(p.astype(BF16), dos[cols])
        dqt = dot(kt, ds) * C
        for i in range(CB // PLEN):
            at = left + (b * (CB // PLEN) + i) * D
            dq_ref[rows, at:at + D] = dqt[:, i * PLEN:(i + 1) * PLEN].T.astype(BF16)
    return gk * C, gv


TK = 1024
TP = TK // PLEN
NT = P_REQ * PLEN // TK


def spot(slot):
    n = slot % 2
    c = slot // 2 % 2
    x = slot // 4 % 4
    z = slot // 16
    return n * 32 + jnp.where(n == 0, z * 4 + x, x * 4 + z) * 2 + c


def qry_kernel(
    req_ref, slot_ref, owner_ref, me_ref, kvg_ref, q_any, do_any, kq_any, vq_any, dq_in_ref, cleared_ref,
    dq_ref, g_ref, full_ref, dq_out_ref,
    held, kv, q_ref, do_ref, kq_ref, vq_ref, qs, dos, qst, dost, ktbuf, sbuf, dpbuf, dqt, gbuf, slots,
    load_sem, in_sem, out_sem, hand_sem,
):
    me = me_ref[0]
    take = pltpu.make_async_copy(dq_in_ref, held, hand_sem.at[0])
    give = pltpu.make_async_copy(held, dq_out_ref, hand_sem.at[1])
    pairs = ((q_any, q_ref), (do_any, do_ref), (kq_any, kq_ref), (vq_any, vq_ref))
    loads = [pltpu.make_async_copy(ref, buf, load_sem.at[i]) for i, (ref, buf) in enumerate(pairs)]
    for copy in loads:
        copy.start()
    request = jnp.int32(0)
    for r in range(REQ):
        request = jnp.where(owner_ref[r] == me, r, request)

    def pick(j, carry):
        slot = spot(slot_ref[req_ref[request, j]])
        slots[j] = slot
        pltpu.make_async_copy(kvg_ref.at[slot], kv.at[j], in_sem).start()
        return carry

    lax.fori_loop(0, P_REQ, pick, 0)

    for copy in loads:
        copy.wait()
    take.start()

    def land(j, carry):
        pltpu.make_async_copy(kvg_ref.at[slots[j]], kv.at[j], in_sem).wait()
        return carry

    blocks = [slice(i * CB, (i + 1) * CB) for i in range(G * PLEN // CB)]
    own = slice(P_REQ * PLEN, P_REQ * PLEN + PLEN)

    def tile(t, part, cols):
        return kv[pl.ds(t * TP, TP), part, :, cols].reshape(TK, D)

    def tile_rows(t):
        return pl.ds(pl.multiple_of(t * TK, TK), TK)

    def fold(x, op):
        return op(x.reshape(-1, 8, x.shape[1]), axis=0)

    for h in range(KV):
        cols = slice(h * D, (h + 1) * D)
        wide = slice(h * G * D, (h + 1) * G * D)
        qs[...] = stack(q_ref[:, wide])
        dos[...] = stack(do_ref[:, wide])
        qst[...] = qs[...].T
        dost[...] = dos[...].T
        kq = kq_ref[:, cols]
        vq = vq_ref[:, cols]

        def scores(keys, rows, masked, high):
            highs = []
            for b in blocks:
                s = dot(keys, qst[:, b])
                if masked:
                    s = jnp.where(causal_cols(s.shape), s, -1e30)
                sbuf[rows, b] = s
                highs.append(jnp.maximum(high[:, b], fold(s, jnp.max)))
            return jnp.concatenate(highs, axis=1)

        def score_tile(t, high):
            keys = tile(t, 0, cols)
            ktbuf[t] = keys.T
            return scores(keys, tile_rows(t), False, high)

        high = scores(kq, own, True, jnp.full((8, G * PLEN), -1e30, F32))
        if h == 0:
            lax.fori_loop(0, P_REQ, land, 0)
        high = lax.fori_loop(0, NT, score_tile, high)
        m2 = jnp.max(high, axis=0, keepdims=True) * C2

        def sums(values, rows, carry):
            l, num = carry
            ls, nums = [], []
            for b in blocks:
                dp = dot(values, dost[:, b])
                dpbuf[rows, b] = dp
                e = jnp.exp2(sbuf[rows, b] * C2 - m2[:, b])
                ls.append(l[:, b] + fold(e, jnp.sum))
                nums.append(num[:, b] + fold(e * dp, jnp.sum))
            return jnp.concatenate(ls, axis=1), jnp.concatenate(nums, axis=1)

        def sum_tile(t, carry):
            return sums(tile(t, 1, cols), tile_rows(t), carry)

        nothing = jnp.zeros((8, G * PLEN), F32)
        carry = sums(vq, own, (nothing, nothing))
        l, num = lax.fori_loop(0, NT, sum_tile, carry)
        l = jnp.sum(l, axis=0, keepdims=True)
        delta = jnp.sum(num, axis=0, keepdims=True) / l
        level = m2 + jnp.log2(l)

        def grads(kt, rows, first):
            gk = gv = None
            for b in blocks:
                p = jnp.exp2(sbuf[rows, b] * C2 - level[:, b])
                ds = (p * (dpbuf[rows, b] - delta[:, b])).astype(BF16)
                dk = dot(ds, qs[b, :])
                dv = dot(p.astype(BF16), dos[b, :])
                gk = dk if gk is None else gk + dk
                gv = dv if gv is None else gv + dv
                more = dot(kt, ds)
                dqt[:, b] = more if first else dqt[:, b] + more
            return (gk * C).astype(BF16), gv.astype(BF16)

        if h == 0:
            take.wait()
            give.start()
        gk, gv = grads(kq.T, own, True)
        g_ref[0, :, cols] = gk
        g_ref[1, :, cols] = gv

        def grad_tile(t, carry):
            gk, gv = grads(ktbuf[t], tile_rows(t), False)
            for i in range(TP):
                j = t * TP + i
                gbuf[j, 0, :, cols] = gk[i * PLEN:(i + 1) * PLEN]
                gbuf[j, 1, :, cols] = gv[i * PLEN:(i + 1) * PLEN]
                if h == KV - 1:
                    pltpu.make_async_copy(gbuf.at[j], full_ref.at[slots[j]], out_sem).start()
            return carry

        lax.fori_loop(0, NT, grad_tile, 0)
        for g in range(G):
            left = h * G * D + g * D
            dq_ref[:, left:left + D] = (dqt[:, g * PLEN:(g + 1) * PLEN] * C).T.astype(BF16)

    def drain(j, carry):
        pltpu.make_async_copy(gbuf.at[j], full_ref.at[slots[j]], out_sem).wait()
        return carry

    lax.fori_loop(0, P_REQ, drain, 0)
    give.wait()


def qry_back(req, slot, owner, me, kvg, q, do, kq, vq, dq_psg, cleared):
    keys = P_REQ * PLEN + PLEN
    smem = pl.BlockSpec(memory_space=pltpu.SMEM)
    hbm = pl.BlockSpec(memory_space=pltpu.HBM)
    vmem = pl.BlockSpec(memory_space=pltpu.VMEM)
    return pl.pallas_call(
        qry_kernel,
        in_specs=[smem] * 4 + [hbm] * 7,
        input_output_aliases={10: 2},
        out_specs=[vmem, vmem, hbm, hbm],
        out_shape=[
            jax.ShapeDtypeStruct(q.shape, BF16),
            jax.ShapeDtypeStruct((2,) + kq.shape, BF16),
            jax.ShapeDtypeStruct((NPSG, 2, PLEN, KV * D), BF16),
            jax.ShapeDtypeStruct(dq_psg.shape, BF16),
        ],
        scratch_shapes=[
            pltpu.VMEM(dq_psg.shape, BF16),
            pltpu.VMEM((P_REQ, 2, PLEN, KV * D), BF16),
            pltpu.VMEM(q.shape, BF16),
            pltpu.VMEM(q.shape, BF16),
            pltpu.VMEM(kq.shape, BF16),
            pltpu.VMEM(kq.shape, BF16),
            pltpu.VMEM((G * PLEN, D), BF16),
            pltpu.VMEM((G * PLEN, D), BF16),
            pltpu.VMEM((D, G * PLEN), BF16),
            pltpu.VMEM((D, G * PLEN), BF16),
            pltpu.VMEM((NT, D, TK), BF16),
            pltpu.VMEM((keys, G * PLEN), F32),
            pltpu.VMEM((keys, G * PLEN), F32),
            pltpu.VMEM((D, G * PLEN), F32),
            pltpu.VMEM((P_REQ, 2, PLEN, KV * D), BF16),
            pltpu.SMEM((P_REQ,), jnp.int32),
            pltpu.SemaphoreType.DMA((4,)),
            pltpu.SemaphoreType.DMA,
            pltpu.SemaphoreType.DMA,
            pltpu.SemaphoreType.DMA((2,)),
        ],
        compiler_params=pltpu.CompilerParams(vmem_limit_bytes=VMEM),
        cost_estimate=pl.CostEstimate(flops=2 * 5 * 2 * 1024 * 2176 * 128, bytes_accessed=16 * 1024 * 1024, transcendentals=2 * 1024 * 2176),
        name="qry_back",
    )(req, slot, owner, me, kvg, q, do, kq, vq, dq_psg, cleared)


MESH = pl.DeviceIdType.MESH


def place():
    me = lax.axis_index("psg")
    return me // 8, lax.rem(me // 2, 4), lax.rem(me, 2)


def at_plane(z, x, c):
    return {"psg": (z * 4 + x) * 2 + c}


def turn(i, by):
    return lax.rem(i + by + 4, 4)


def greet(devices):
    barrier = pltpu.get_barrier_semaphore()
    for device in devices:
        pl.semaphore_signal(barrier, inc=1, device_id=device, device_id_type=MESH)
    pl.semaphore_wait(barrier, len(devices))


def plane_neighbours(z, x, c):
    return [
        at_plane(turn(z, 1), x, c),
        at_plane(turn(z, -1), x, c),
        at_plane(z, turn(x, 1), c),
        at_plane(z, turn(x, -1), c),
        at_plane(z, x, 1 - c),
    ]


class Sender:
    def __init__(self, sems):
        self.sems = sems
        self.started = []

    def __call__(self, src, dst, recv_sem, device):
        copy = pltpu.make_async_remote_copy(
            src_ref=src, dst_ref=dst, send_sem=self.sems.at[len(self.started)], recv_sem=recv_sem,
            device_id=device, device_id_type=MESH,
        )
        copy.start()
        self.started.append(copy)

    def finish(self):
        for copy in self.started:
            copy.wait_send()


def arrived(ref, sem):
    pltpu.make_async_copy(ref, ref, sem).wait()


def lane_device(a, b, c):
    return at_plane(a * (1 - c) + b * c, b * (1 - c) + a * c, c)


def gather_kernel(
    q_ref, k_ref, v_ref, do_ref, wk_ref, wv_ref, all_ref, near_ref, far_ref, first_ref, dq_ref, own_k_ref, own_v_ref, full_ref,
    lane, q_buf, do_buf, k_buf, v_buf, dq_buf, own_k_buf, own_v_buf, far_buf, zeros,
    send_sem, recv_sem, core_sem, local_sem, swap_sem, near_sem, near_core_sem, far_sem, load_sem, keep_sem, first_sem, out_sem, zero_sem,
):
    z, x, c = place()
    y = lax.axis_index("head")
    a = z * (1 - c) + x * c
    b = x * (1 - c) + z * c
    half = k_ref.shape[0] // 2
    share = 2 * first_ref.shape[0]
    refs = (k_ref, v_ref)
    weights = (wk_ref, wv_ref)
    mine = [pltpu.make_async_copy(ref.at[pl.ds(c * half, half)], lane.at[a, b, c, i], local_sem.at[i]) for i, ref in enumerate(refs)]
    loads = [pltpu.make_async_copy(ref, buf, load_sem.at[i]) for i, (ref, buf) in enumerate(((q_ref, q_buf), (do_ref, do_buf), (k_ref, k_buf), (v_ref, v_buf)))]
    for copy in mine + loads:
        copy.start()
    greet(plane_neighbours(z, x, c) + [{"head": turn(y, by)} for by in (1, -1, 2)])
    send = Sender(send_sem)
    partner = at_plane(z, x, 1 - c)
    for i, ref in enumerate(refs):
        send(ref.at[pl.ds((1 - c) * half, half)], lane.at[b, a, c, i], swap_sem.at[i], partner)

    def columns(head):
        return pl.ds((2 * head + c) * share, share)

    for i, ref in enumerate(weights):
        for s, by in ((1, 1), (0, -1)):
            to = turn(y, by)
            send(ref.at[columns(to)], near_ref.at[s, i, pl.ds(c * share, share)], near_sem.at[s, i], {"head": to})
    for copy in mine:
        copy.wait()

    def whole(i, j, to):
        send(lane.at[i, j], lane.at[i, j], recv_sem.at[0, i, j], to)

    def piece(i, j, part, to):
        send(lane.at[i, j, part], lane.at[i, j, part], recv_sem.at[part, i, j], to)

    def keep(i, j):
        return pltpu.make_async_copy(lane.at[i, j], all_ref.at[c, i, j], keep_sem.at[i, j])

    def core(i, j):
        send(lane.at[i, j], all_ref.at[c, i, j], core_sem.at[i, j], partner)
        keep(i, j).start()

    def wait_whole(i, j):
        arrived(lane.at[i, j], recv_sem.at[0, i, j])

    def wait_pieces(i, j):
        for part in range(2):
            arrived(lane.at[i, j, part], recv_sem.at[part, i, j])

    def along_a(i, j):
        for by in (1, -1):
            whole(i, j, lane_device(turn(a, by), b, c))

    def own_passage(n, h):
        rows = slice(n * PLEN, (n + 1) * PLEN)
        thin = slice(h * D, (h + 1) * D)
        wide = slice(h * G * D, (h + 1) * G * D)
        gk, gv = passage(q_buf[rows, wide], k_buf[rows, thin], v_buf[rows, thin], do_buf[rows, wide], dq_buf, rows, h * G * D)
        own_k_buf[rows, thin] = gk
        own_v_buf[rows, thin] = gv

    ways = ((-1, 0), (1, 1))
    for part in (c, 1 - c):
        if part is not c:
            for i in range(2):
                arrived(lane.at[a, b, part, i], swap_sem.at[i])
        for by in (1, -1):
            piece(a, b, part, lane_device(a, turn(b, by), c))
        for by in (1, -1):
            piece(a, b, part, lane_device(turn(a, by), b, c))
    opposite = turn(y, 2)
    few = share // 2
    left = (2 * opposite + c) * share
    send(wk_ref.at[pl.ds(left, few)], first_ref, first_sem, {"head": opposite})
    across = [
        pltpu.make_async_copy(wk_ref.at[pl.ds(left + few, few)], far_buf.at[pl.ds(0, few)], far_sem.at[0]),
        pltpu.make_async_copy(wv_ref.at[pl.ds(left, share)], far_buf.at[pl.ds(few, share)], far_sem.at[1]),
    ]
    for copy in across:
        copy.start()
    zeros[...] = jnp.zeros_like(zeros)
    some = zeros.shape[0]
    clears = [pltpu.make_async_copy(zeros, full_ref.at[pl.ds(i * some, some)], zero_sem.at[i]) for i in range(NPSG // some)]
    for copy in loads:
        copy.wait()
    for copy in clears:
        copy.start()
    own_passage(0, 0)
    own_passage(0, 1)
    for by, part in ways:
        j = turn(b, by)
        wait_pieces(a, j)
        piece(a, j, part, lane_device(a, turn(b, -by), c))
    for by, part in ways:
        along_a(a, turn(b, by))
    own_passage(1, 0)

    def far(bo):
        j = turn(b, bo)
        for by, part in ways:
            i = turn(a, by)
            (wait_pieces if bo == 0 else wait_whole)(i, j)
            piece(i, j, part, lane_device(turn(a, -by), b, c))

    far(0)
    wait_pieces(a, turn(b, 2))
    along_a(a, turn(b, 2))
    own_passage(1, 1)
    for copy in across:
        copy.wait()
    results = ((dq_buf, dq_ref), (own_k_buf, own_k_ref), (own_v_buf, own_v_ref), (far_buf, far_ref))
    stores = [pltpu.make_async_copy(buf, ref, out_sem.at[i]) for i, (buf, ref) in enumerate(results)]
    for copy in stores:
        copy.start()
    for bo in (0, -1, 1, 2):
        core(a, turn(b, bo))
    for by, _ in ways:
        core(turn(a, by), b)
    for bo in (-1, 1, 2):
        far(bo)
        for by, _ in ways:
            core(turn(a, by), turn(b, bo))
    for s in range(2):
        for i in range(2):
            block = near_ref.at[s, i, pl.ds(c * share, share)]
            arrived(block, near_sem.at[s, i])
            send(block, block, near_core_sem.at[s, i], partner)
    for bo in (0, -1, 1, 2):
        wait_pieces(turn(a, 2), turn(b, bo))
        core(turn(a, 2), turn(b, bo))
    for i in range(4):
        for j in range(4):
            arrived(all_ref.at[1 - c, i, j], core_sem.at[i, j])
            keep(i, j).wait()
    for s in range(2):
        for i in range(2):
            arrived(near_ref.at[s, i, pl.ds((1 - c) * share, share)], near_core_sem.at[s, i])
    for copy in stores + clears:
        copy.wait()
    arrived(first_ref, first_sem)
    send.finish()


def gather_plane(q, k, v, do, w_key, w_value):
    rows, cols = k.shape
    width, depth = w_key.shape
    share = width // 8
    hbm = pl.BlockSpec(memory_space=pltpu.HBM)
    dma = pltpu.SemaphoreType.DMA
    return pl.pallas_call(
        gather_kernel,
        in_specs=[hbm] * 6,
        out_specs=[hbm] * 8,
        out_shape=[
            jax.ShapeDtypeStruct((2, 4, 4, 2, 2, rows // 2, cols), BF16),
            jax.ShapeDtypeStruct((2, 2, 2 * share, depth), BF16),
            jax.ShapeDtypeStruct((3 * share // 2, depth), BF16),
            jax.ShapeDtypeStruct((share // 2, depth), BF16),
            jax.ShapeDtypeStruct(q.shape, BF16),
            jax.ShapeDtypeStruct(k.shape, F32),
            jax.ShapeDtypeStruct(v.shape, F32),
            jax.ShapeDtypeStruct((NPSG, 2, PLEN, KV * D), BF16),
        ],
        scratch_shapes=[
            pltpu.VMEM((4, 4, 2, 2, rows // 2, cols), BF16),
            pltpu.VMEM(q.shape, BF16),
            pltpu.VMEM(q.shape, BF16),
            pltpu.VMEM(k.shape, BF16),
            pltpu.VMEM(k.shape, BF16),
            pltpu.VMEM(q.shape, BF16),
            pltpu.VMEM(k.shape, F32),
            pltpu.VMEM(k.shape, F32),
            pltpu.VMEM((3 * share // 2, depth), BF16),
            pltpu.VMEM((8, 2, PLEN, KV * D), BF16),
            dma((51,)), dma((2, 4, 4)), dma((4, 4)), dma((2,)), dma((2,)), dma((2, 2)), dma((2, 2)), dma((2,)), dma((4,)),
            dma((4, 4)), dma, dma((4,)), dma((8,)),
        ],
        compiler_params=pltpu.CompilerParams(collective_id=0, has_side_effects=True, vmem_limit_bytes=VMEM),
        name="gather_plane",
    )(q, k, v, do, w_key, w_value)


CUTS = 2
JOBS = CUTS + 1
ORDER = [
    ("f", 0), ("n", 0), (0, 0), ("f", 1), ("o", 0), ("w", 0), (0, 1), ("n", 1), ("o", 1), (1, 0), (1, 1),
    (2, 0), ("q", 0), (3, 0), (2, 1), (3, 1), (4, 0), (4, 1),
]


def tail_kernel(
    full_ref, own_k_ref, own_v_ref, query_ref, wk_ref, wv_ref, near_ref, far_ref, first_ref, dx_psg_ref, dx_qry_ref,
    mine, other, relay1, side1, part, got, rows, weights, acc, terms,
    send_sem, core_sem, relay1_sem, side1_sem, got_sem, local_sem,
    load_sem, far_sem, rows_sem, out_sem, query_sem,
):
    z, x, c = place()
    y = lax.axis_index("head")
    a = z * (1 - c) + x * c
    b = x * (1 - c) + z * c
    partner = at_plane(z, x, 1 - c)
    steps = (1, -1)
    halves = (pl.ds(0, 2), pl.ds(2, 2))
    quarter = dx_qry_ref.shape[0]
    width = dx_qry_ref.shape[1] // 4
    share = width // 2
    heads = [y, turn(y, 1), turn(y, -1), turn(y, 2)]
    mirror = (0, 2, 1, 3)
    few = dx_psg_ref.shape[0] // CUTS
    size = [few] * CUTS + [quarter]

    loads = {}
    for q in range(CUTS):
        for by in (2, 1, -1, 0):
            i = turn(a, by)
            loads[q, by] = pltpu.make_async_copy(full_ref.at[c, i, :, :, :, :, q], mine.at[q, i], local_sem.at[q, i])
            loads[q, by].start()
    weight_loads = []
    for i, ref in enumerate((wk_ref, wv_ref)):
        weight_loads.append(pltpu.make_async_copy(ref.at[pl.ds(y * width, width)], weights.at[0, i], load_sem.at[0, i]))
        for s in range(2):
            weight_loads.append(pltpu.make_async_copy(near_ref.at[s, i], weights.at[1 + s, i], load_sem.at[1 + s, i]))
    cut = share // 2
    far_parts = (
        (first_ref, (3, 0, pl.ds(c * share, cut))),
        (far_ref.at[pl.ds(0, cut)], (3, 0, pl.ds(c * share + cut, cut))),
        (far_ref.at[pl.ds(cut, share)], (3, 1, pl.ds(c * share, share))),
    )
    for i, (ref, to) in enumerate(far_parts):
        weight_loads.append(pltpu.make_async_copy(ref, weights.at[to], load_sem.at[3, i]))
    for load in weight_loads:
        load.start()
    query_load = pltpu.make_async_copy(query_ref, rows.at[CUTS, 0], query_sem)
    query_load.start()
    senders = [partner, lane_device(turn(a, 1), b, c), lane_device(turn(a, -1), b, c)]
    senders += [at_plane(z, turn(x, by), 0) for by in (1, -1, 2)] + [at_plane(turn(z, by), x, 1) for by in (1, -1, 2)]
    greet(senders + [{"head": head} for head in heads[1:]])
    send = Sender(send_sem)

    def spread(job):
        used = pl.ds(0, 4 * size[job])
        for p in (3, 1, 2):
            for i in range(2):
                send(rows.at[job, 0, i, used], rows.at[job, mirror[p], i, used], rows_sem.at[job, mirror[p], i], {"head": heads[p]})

    query_load.wait()
    spread(CUTS)

    def stage0(q, by):
        i = turn(b, by)
        send(full_ref.at[1 - c, i, :, :, :, :, q], other.at[q, i], core_sem.at[q, i], partner)

    def share_far():
        for i, (ref, to) in enumerate(far_parts):
            send(ref, weights.at[to], far_sem.at[i], partner)

    def pair(q, by):
        i = turn(a, by)
        loads[q, by].wait()
        arrived(other.at[q, i], core_sem.at[q, i])
        mine[q, i] = mine[q, i] + other[q, i]
        return i

    def ring1_far(q):
        i = pair(q, 2)
        for s in range(2):
            to = lane_device(turn(a, steps[s]), b, c)
            send(mine.at[q, i, halves[s]], relay1.at[q, s], relay1_sem.at[q, s], to)

    def ring1_near(q):
        for s in range(2):
            i = pair(q, steps[s])
            arrived(relay1.at[q, s], relay1_sem.at[q, s])
            mine[q, i, halves[s]] = mine[q, i, halves[s]] + relay1[q, s]
            send(mine.at[q, i], side1.at[q, s], side1_sem.at[q, s], lane_device(i, b, c))

    def join1(q, j):
        total = mine[q, a, j].astype(F32)
        for s in range(2):
            total = total + side1[q, s, j].astype(F32)
        part[q, j] = total.astype(BF16)

    def ring2(q):
        pair(q, 0)
        for s in range(2):
            arrived(side1.at[q, s], side1_sem.at[q, s])
        for r, by in enumerate((2, 1, -1, 0)):
            j = turn(b, by)
            join1(q, j)
            for core in range(2):
                if by != 0:
                    to = at_plane(a * (1 - c) + j * c, j * (1 - c) + a * c, core)
                    send(part.at[q, j, core], got.at[q, c, r], got_sem.at[q, c, r], to)
        send(part.at[q, b, 1 - c], got.at[q, c, 3], got_sem.at[q, c, 3], partner)

    def finish_rows(q):
        for n in range(2):
            for r in range(3):
                arrived(got.at[q, n, r], got_sem.at[q, n, r])
        arrived(got.at[q, 1 - c, 3], got_sem.at[q, 1 - c, 3])
        got[q, c, 3] = part[q, b, c]
        for n in range(2):
            for i, own_ref in enumerate((own_k_ref, own_v_ref)):
                total = got[q, n, 0, i].astype(F32)
                for r in range(1, 4):
                    total = total + got[q, n, r, i].astype(F32)
                for g in range(2):
                    h = 2 * n + g
                    top = (CUTS * h + q) * few
                    rows[q, 0, i, h * few:(h + 1) * few, :] = (own_ref[top:top + few, :] + total[g]).astype(BF16)
        spread(q)

    def product(job, p, done):
        used = pl.ds(0, 4 * size[job])
        for j in range(4):
            cols = pl.ds(j * (width // 4), width // 4)
            total = dot_t(rows[job, p, 0, used], weights[p, 0, cols, :]) + dot_t(rows[job, p, 1, used], weights[p, 1, cols, :])
            if p > 0:
                total = acc[used, cols] + total
            if p < 3:
                acc[used, cols] = total
            else:
                total = total.astype(BF16)
                for d in range(4):
                    terms[job, d, pl.ds(0, size[job]), cols] = total[d * size[job]:(d + 1) * size[job]]
                done(j)

    def target(job):
        return (dx_qry_ref, 0) if job == CUTS else (dx_psg_ref, job * few)

    def piece_of(job, head, j):
        out_ref, top = target(job)
        left = head * width + j * (width // 4)
        return out_ref.at[pl.ds(top, size[job]), pl.ds(pl.multiple_of(left, width // 4), width // 4)]

    def job_terms(job):
        used = pl.ds(0, size[job])

        def done(j):
            cols = pl.ds(j * (width // 4), width // 4)
            for p in (3, 1, 2):
                send(terms.at[job, heads[p], used, cols], piece_of(job, y, j), out_sem.at[job, mirror[p], j], {"head": heads[p]})

        for p in range(4):
            if p > 0:
                for i in range(2):
                    block = rows.at[job, p, i, pl.ds(0, 4 * size[job])]
                    arrived(block, rows_sem.at[job, p, i])
            product(job, p, done)
        out_ref, top = target(job)
        out_ref[pl.ds(top, size[job]), pl.ds(pl.multiple_of(y * width, width), width)] = terms[job, y, used]

    def job_wait(job):
        for p in (1, 2, 3):
            for j in range(4):
                arrived(piece_of(job, heads[p], j), out_sem.at[job, p, j])

    def query_job():
        for load in weight_loads:
            load.wait()
        there = (1 - c) * share
        for i, to in enumerate(((3, 0, pl.ds(there, cut)), (3, 0, pl.ds(there + cut, cut)), (3, 1, pl.ds(there, share)))):
            arrived(weights.at[to], far_sem.at[i])
        job_terms(CUTS)

    steps_of = {
        "f": lambda q: stage0(q, 2),
        "n": lambda q: (stage0(q, 1), stage0(q, -1)),
        "o": lambda q: stage0(q, 0),
        "w": lambda q: share_far(),
        "q": lambda q: query_job(),
        0: ring1_far,
        1: ring1_near,
        2: ring2,
        3: finish_rows,
        4: job_terms,
    }
    for step, q in ORDER:
        steps_of[step](q)
    for job in [CUTS] + list(range(CUTS)):
        job_wait(job)
    send.finish()


def tail(full, own_k, own_v, g_qry, w_key, w_value, near, far, first):
    rows, cols = own_k.shape
    width, depth = w_key.shape
    quarter = rows // 8
    few = rows // 4 // CUTS
    hbm = pl.BlockSpec(memory_space=pltpu.HBM)
    vmem = pl.BlockSpec(memory_space=pltpu.VMEM)
    dma = pltpu.SemaphoreType.DMA
    block = (2, 2, 2, few, cols)
    full = full.reshape(2, 4, 4, 2, 2, 2, CUTS, few, cols)
    return pl.pallas_call(
        tail_kernel,
        in_specs=[hbm, vmem, vmem, hbm, hbm, hbm, hbm, pl.BlockSpec(memory_space=pl.ANY), hbm],
        out_specs=[vmem, vmem],
        out_shape=[jax.ShapeDtypeStruct((2 * quarter, width), BF16), jax.ShapeDtypeStruct((quarter, width), BF16)],
        scratch_shapes=[
            pltpu.VMEM((CUTS, 4, 4) + block, BF16),
            pltpu.VMEM((CUTS, 4, 4) + block, BF16),
            pltpu.VMEM((CUTS, 2, 2) + block, BF16),
            pltpu.VMEM((CUTS, 2, 4) + block, BF16),
            pltpu.VMEM((CUTS, 4) + block, BF16),
            pltpu.VMEM((CUTS, 2, 4) + block[1:], BF16),
            pltpu.VMEM((JOBS, 4, 2, 4 * quarter, cols), BF16),
            pltpu.VMEM((4, 2, width // 4, depth), BF16),
            pltpu.VMEM((4 * quarter, width // 4), F32),
            pltpu.VMEM((JOBS, 4, quarter, width // 4), BF16),
            dma((15 * CUTS + 3 + 18 * JOBS,)),
            dma((CUTS, 4)),
            dma((CUTS, 2)),
            dma((CUTS, 2)),
            dma((CUTS, 2, 4)),
            dma((CUTS, 4)),
            dma((4, 3)),
            dma((3,)),
            dma((JOBS, 4, 2)),
            dma((JOBS, 4, 4)),
            dma,
        ],
        compiler_params=pltpu.CompilerParams(collective_id=3, has_side_effects=True, vmem_limit_bytes=48 * 1024 * 1024),
        name="tail",
    )(full, own_k, own_v, g_qry, w_key, w_value, near, far, first)


def local(q_psg, k_psg, v_psg, do_psg, q_qry, k_qry, v_qry, do_qry, w_key, w_value, req_passages, passage_slot, query_owner):
    me = lax.axis_index("psg").astype(jnp.int32).reshape(1)
    every, near, far, first, dq_psg, own_k, own_v, cleared = gather_plane(q_psg, k_psg, v_psg, do_psg, w_key, w_value)
    far = lax.ppermute(far, "head", [(i, (i + 2) % 4) for i in range(4)])
    dq_qry, g_qry, full, dq_psg = qry_back(
        req_passages, passage_slot, query_owner, me, every.reshape(NPSG, 2, PLEN, -1), q_qry, do_qry, k_qry, v_qry, dq_psg, cleared
    )
    dx_psg, dx_qry = tail(full, own_k, own_v, g_qry, w_key, w_value, near, far, first)
    return dq_psg, dq_qry, dx_psg, dx_qry


def solution(mesh):
    rows = P("psg", "head")
    return jax.shard_map(
        local,
        mesh=mesh,
        in_specs=(rows,) * 8 + (P(None, "head"),) * 2 + (P(),) * 3,
        out_specs=(rows, rows, P(("psg", "head"), None), P(("psg", "head"), None)),
        check_vma=False,
    )
```

```python
import functools

import jax
import jax.numpy as jnp
from jax import lax
from jax.experimental import pallas as pl
from jax.experimental.pallas import tpu as pltpu
from jax.sharding import PartitionSpec as P

D = 128
G = 8
PLEN = 128
KV = 2
NPSG = 64
REQ = 32
P_REQ = 16
CB = 256
C = D ** -0.5
C2 = C * 1.4426950408889634
VMEM = 62 * 1024 * 1024
F32 = jnp.float32
BF16 = jnp.bfloat16


def stack(x):
    return jnp.concatenate([x[:, g * D:(g + 1) * D] for g in range(G)], axis=0)


def dot(a, b):
    return jnp.dot(a, b, preferred_element_type=F32)


def dot_t(a, b):
    return lax.dot_general(a, b, (((1,), (1,)), ((), ())), preferred_element_type=F32)


def causal_cols(shape):
    key = lax.broadcasted_iota(jnp.int32, shape, 0)
    qry = lax.broadcasted_iota(jnp.int32, shape, 1) % PLEN
    return key <= qry


def passage(q, k, v, do, dq_ref, rows, left):
    qs = stack(q)
    dos = stack(do)
    kt = k.T
    gk = jnp.zeros((PLEN, D), F32)
    gv = jnp.zeros((PLEN, D), F32)
    for b in range(G * PLEN // CB):
        cols = slice(b * CB, (b + 1) * CB)
        s = dot_t(k, qs[cols])
        s = jnp.where(causal_cols(s.shape), s, -1e30)
        e = jnp.exp2((s - jnp.max(s, axis=0, keepdims=True)) * C2)
        inv = 1.0 / jnp.sum(e, axis=0, keepdims=True)
        dp = dot_t(v, dos[cols])
        p = e * inv
        delta = jnp.sum(p * dp, axis=0, keepdims=True)
        ds = (p * (dp - delta)).astype(BF16)
        gk += dot(ds, qs[cols])
        gv += dot(p.astype(BF16), dos[cols])
        dqt = dot(kt, ds) * C
        for i in range(CB // PLEN):
            at = left + (b * (CB // PLEN) + i) * D
            dq_ref[rows, at:at + D] = dqt[:, i * PLEN:(i + 1) * PLEN].T.astype(BF16)
    return gk * C, gv


TK = 2048
TP = TK // PLEN
NT = P_REQ * PLEN // TK


def spot(slot):
    n = slot % 2
    c = slot // 2 % 2
    x = slot // 4 % 4
    z = slot // 16
    return n * 32 + jnp.where(n == 0, z * 4 + x, x * 4 + z) * 2 + c


def qry_kernel(
    req_ref, slot_ref, owner_ref, me_ref, kvg_ref, q_any, do_any, kq_any, vq_any, dq_in_ref, cleared_ref,
    dq_ref, g_ref, full_ref, dq_out_ref,
    held, kv, q_ref, do_ref, kq_ref, vq_ref, qs, dos, qst, dost, ktbuf, sbuf, dpbuf, dqt, gbuf, slots,
    load_sem, in_sem, out_sem, hand_sem,
):
    me = me_ref[0]
    take = pltpu.make_async_copy(dq_in_ref, held, hand_sem.at[0])
    give = pltpu.make_async_copy(held, dq_out_ref, hand_sem.at[1])
    pairs = ((q_any, q_ref), (do_any, do_ref), (kq_any, kq_ref), (vq_any, vq_ref))
    loads = [pltpu.make_async_copy(ref, buf, load_sem.at[i]) for i, (ref, buf) in enumerate(pairs)]
    for copy in loads:
        copy.start()
    request = jnp.int32(0)
    for r in range(REQ):
        request = jnp.where(owner_ref[r] == me, r, request)

    def pick(j, carry):
        slot = spot(slot_ref[req_ref[request, j]])
        slots[j] = slot
        pltpu.make_async_copy(kvg_ref.at[slot], kv.at[j], in_sem).start()
        return carry

    lax.fori_loop(0, P_REQ, pick, 0)

    for copy in loads:
        copy.wait()
    take.start()

    def land(j, carry):
        pltpu.make_async_copy(kvg_ref.at[slots[j]], kv.at[j], in_sem).wait()
        return carry

    blocks = [slice(i * CB, (i + 1) * CB) for i in range(G * PLEN // CB)]
    own = slice(P_REQ * PLEN, P_REQ * PLEN + PLEN)

    def tile(t, part, cols):
        return kv[pl.ds(t * TP, TP), part, :, cols].reshape(TK, D)

    def tile_rows(t):
        return pl.ds(pl.multiple_of(t * TK, TK), TK)

    def fold(x, op):
        return op(x.reshape(-1, 8, x.shape[1]), axis=0)

    for h in range(KV):
        cols = slice(h * D, (h + 1) * D)
        wide = slice(h * G * D, (h + 1) * G * D)
        qs[...] = stack(q_ref[:, wide])
        dos[...] = stack(do_ref[:, wide])
        qst[...] = qs[...].T
        dost[...] = dos[...].T
        kq = kq_ref[:, cols]
        vq = vq_ref[:, cols]

        def scores(keys, rows, masked, high):
            highs = []
            for b in blocks:
                s = dot(keys, qst[:, b])
                if masked:
                    s = jnp.where(causal_cols(s.shape), s, -1e30)
                sbuf[rows, b] = s
                highs.append(jnp.maximum(high[:, b], fold(s, jnp.max)))
            return jnp.concatenate(highs, axis=1)

        def score_tile(t, high):
            keys = tile(t, 0, cols)
            ktbuf[t] = keys.T
            return scores(keys, tile_rows(t), False, high)

        high = scores(kq, own, True, jnp.full((8, G * PLEN), -1e30, F32))
        if h == 0:
            lax.fori_loop(0, P_REQ, land, 0)
        high = lax.fori_loop(0, NT, score_tile, high)
        m2 = jnp.max(high, axis=0, keepdims=True) * C2

        def sums(values, rows, carry):
            l, num = carry
            ls, nums = [], []
            for b in blocks:
                dp = dot(values, dost[:, b])
                dpbuf[rows, b] = dp
                e = jnp.exp2(sbuf[rows, b] * C2 - m2[:, b])
                ls.append(l[:, b] + fold(e, jnp.sum))
                nums.append(num[:, b] + fold(e * dp, jnp.sum))
            return jnp.concatenate(ls, axis=1), jnp.concatenate(nums, axis=1)

        def sum_tile(t, carry):
            return sums(tile(t, 1, cols), tile_rows(t), carry)

        nothing = jnp.zeros((8, G * PLEN), F32)
        carry = sums(vq, own, (nothing, nothing))
        l, num = lax.fori_loop(0, NT, sum_tile, carry)
        l = jnp.sum(l, axis=0, keepdims=True)
        delta = jnp.sum(num, axis=0, keepdims=True) / l
        level = m2 + jnp.log2(l)

        def grads(kt, rows, first):
            gk = gv = None
            for b in blocks:
                p = jnp.exp2(sbuf[rows, b] * C2 - level[:, b])
                ds = (p * (dpbuf[rows, b] - delta[:, b])).astype(BF16)
                dk = dot(ds, qs[b, :])
                dv = dot(p.astype(BF16), dos[b, :])
                gk = dk if gk is None else gk + dk
                gv = dv if gv is None else gv + dv
                more = dot(kt, ds)
                dqt[:, b] = more if first else dqt[:, b] + more
            return (gk * C).astype(BF16), gv.astype(BF16)

        if h == 0:
            take.wait()
            give.start()
        gk, gv = grads(kq.T, own, True)
        g_ref[0, :, cols] = gk
        g_ref[1, :, cols] = gv

        def grad_tile(t, carry):
            gk, gv = grads(ktbuf[t], tile_rows(t), False)
            for i in range(TP):
                j = t * TP + i
                gbuf[j, 0, :, cols] = gk[i * PLEN:(i + 1) * PLEN]
                gbuf[j, 1, :, cols] = gv[i * PLEN:(i + 1) * PLEN]
                pltpu.make_async_copy(gbuf.at[j, :, :, cols], full_ref.at[slots[j], :, :, cols], out_sem).start()
            return carry

        lax.fori_loop(0, NT, grad_tile, 0)
        for g in range(G):
            left = h * G * D + g * D
            dq_ref[:, left:left + D] = (dqt[:, g * PLEN:(g + 1) * PLEN] * C).T.astype(BF16)

    def drain(j, carry):
        pltpu.make_async_copy(gbuf.at[j], full_ref.at[slots[j]], out_sem).wait()
        return carry

    lax.fori_loop(0, P_REQ, drain, 0)
    give.wait()


def qry_back(req, slot, owner, me, kvg, q, do, kq, vq, dq_psg, cleared):
    keys = P_REQ * PLEN + PLEN
    smem = pl.BlockSpec(memory_space=pltpu.SMEM)
    hbm = pl.BlockSpec(memory_space=pltpu.HBM)
    vmem = pl.BlockSpec(memory_space=pltpu.VMEM)
    return pl.pallas_call(
        qry_kernel,
        in_specs=[smem] * 4 + [hbm] * 7,
        input_output_aliases={10: 2},
        out_specs=[vmem, vmem, hbm, hbm],
        out_shape=[
            jax.ShapeDtypeStruct(q.shape, BF16),
            jax.ShapeDtypeStruct((2,) + kq.shape, BF16),
            jax.ShapeDtypeStruct((NPSG, 2, PLEN, KV * D), BF16),
            jax.ShapeDtypeStruct(dq_psg.shape, BF16),
        ],
        scratch_shapes=[
            pltpu.VMEM(dq_psg.shape, BF16),
            pltpu.VMEM((P_REQ, 2, PLEN, KV * D), BF16),
            pltpu.VMEM(q.shape, BF16),
            pltpu.VMEM(q.shape, BF16),
            pltpu.VMEM(kq.shape, BF16),
            pltpu.VMEM(kq.shape, BF16),
            pltpu.VMEM((G * PLEN, D), BF16),
            pltpu.VMEM((G * PLEN, D), BF16),
            pltpu.VMEM((D, G * PLEN), BF16),
            pltpu.VMEM((D, G * PLEN), BF16),
            pltpu.VMEM((NT, D, TK), BF16),
            pltpu.VMEM((keys, G * PLEN), F32),
            pltpu.VMEM((keys, G * PLEN), F32),
            pltpu.VMEM((D, G * PLEN), F32),
            pltpu.VMEM((P_REQ, 2, PLEN, KV * D), BF16),
            pltpu.SMEM((P_REQ,), jnp.int32),
            pltpu.SemaphoreType.DMA((4,)),
            pltpu.SemaphoreType.DMA,
            pltpu.SemaphoreType.DMA,
            pltpu.SemaphoreType.DMA((2,)),
        ],
        compiler_params=pltpu.CompilerParams(vmem_limit_bytes=VMEM),
        cost_estimate=pl.CostEstimate(flops=2 * 5 * 2 * 1024 * 2176 * 128, bytes_accessed=16 * 1024 * 1024, transcendentals=2 * 1024 * 2176),
        name="qry_back",
    )(req, slot, owner, me, kvg, q, do, kq, vq, dq_psg, cleared)


MESH = pl.DeviceIdType.MESH


def place():
    me = lax.axis_index("psg")
    return me // 8, lax.rem(me // 2, 4), lax.rem(me, 2)


def at_plane(z, x, c):
    return {"psg": (z * 4 + x) * 2 + c}


def turn(i, by):
    return lax.rem(i + by + 4, 4)


def greet(devices):
    barrier = pltpu.get_barrier_semaphore()
    for device in devices:
        pl.semaphore_signal(barrier, inc=1, device_id=device, device_id_type=MESH)
    pl.semaphore_wait(barrier, len(devices))


def plane_neighbours(z, x, c):
    return [
        at_plane(turn(z, 1), x, c),
        at_plane(turn(z, -1), x, c),
        at_plane(z, turn(x, 1), c),
        at_plane(z, turn(x, -1), c),
        at_plane(z, x, 1 - c),
    ]


class Sender:
    def __init__(self, sems):
        self.sems = sems
        self.started = []

    def __call__(self, src, dst, recv_sem, device):
        copy = pltpu.make_async_remote_copy(
            src_ref=src, dst_ref=dst, send_sem=self.sems.at[len(self.started)], recv_sem=recv_sem,
            device_id=device, device_id_type=MESH,
        )
        copy.start()
        self.started.append(copy)

    def finish(self):
        for copy in self.started:
            copy.wait_send()


def arrived(ref, sem):
    pltpu.make_async_copy(ref, ref, sem).wait()


def lane_device(a, b, c):
    return at_plane(a * (1 - c) + b * c, b * (1 - c) + a * c, c)


def gather_kernel(
    q_ref, k_ref, v_ref, do_ref, wk_ref, wv_ref, all_ref, near_ref, far_ref, first_ref, dq_ref, own_k_ref, own_v_ref, full_ref,
    lane, q_buf, do_buf, k_buf, v_buf, dq_buf, own_k_buf, own_v_buf, far_buf, zeros,
    send_sem, recv_sem, core_sem, local_sem, swap_sem, near_sem, near_core_sem, far_sem, load_sem, keep_sem, first_sem, out_sem, zero_sem,
):
    z, x, c = place()
    y = lax.axis_index("head")
    a = z * (1 - c) + x * c
    b = x * (1 - c) + z * c
    half = k_ref.shape[0] // 2
    share = 2 * first_ref.shape[0]
    refs = (k_ref, v_ref)
    weights = (wk_ref, wv_ref)
    mine = [pltpu.make_async_copy(ref.at[pl.ds(c * half, half)], lane.at[a, b, c, i], local_sem.at[i]) for i, ref in enumerate(refs)]
    loads = [pltpu.make_async_copy(ref, buf, load_sem.at[i]) for i, (ref, buf) in enumerate(((q_ref, q_buf), (do_ref, do_buf), (k_ref, k_buf), (v_ref, v_buf)))]
    for copy in mine + loads:
        copy.start()
    greet(plane_neighbours(z, x, c) + [{"head": turn(y, by)} for by in (1, -1, 2)])
    send = Sender(send_sem)
    partner = at_plane(z, x, 1 - c)
    for i, ref in enumerate(refs):
        send(ref.at[pl.ds((1 - c) * half, half)], lane.at[b, a, c, i], swap_sem.at[i], partner)

    def columns(head):
        return pl.ds((2 * head + c) * share, share)

    for i, ref in enumerate(weights):
        for s, by in ((1, 1), (0, -1)):
            to = turn(y, by)
            send(ref.at[columns(to)], near_ref.at[s, i, pl.ds(c * share, share)], near_sem.at[s, i], {"head": to})
    for copy in mine:
        copy.wait()

    def whole(i, j, to):
        send(lane.at[i, j], lane.at[i, j], recv_sem.at[0, i, j], to)

    def piece(i, j, part, to):
        send(lane.at[i, j, part], lane.at[i, j, part], recv_sem.at[part, i, j], to)

    def keep(i, j):
        return pltpu.make_async_copy(lane.at[i, j], all_ref.at[c, i, j], keep_sem.at[i, j])

    def core(i, j):
        send(lane.at[i, j], all_ref.at[c, i, j], core_sem.at[i, j], partner)
        keep(i, j).start()

    def wait_whole(i, j):
        arrived(lane.at[i, j], recv_sem.at[0, i, j])

    def wait_pieces(i, j):
        for part in range(2):
            arrived(lane.at[i, j, part], recv_sem.at[part, i, j])

    def along_a(i, j):
        for by in (1, -1):
            whole(i, j, lane_device(turn(a, by), b, c))

    def own_passage(n, h):
        rows = slice(n * PLEN, (n + 1) * PLEN)
        thin = slice(h * D, (h + 1) * D)
        wide = slice(h * G * D, (h + 1) * G * D)
        gk, gv = passage(q_buf[rows, wide], k_buf[rows, thin], v_buf[rows, thin], do_buf[rows, wide], dq_buf, rows, h * G * D)
        own_k_buf[rows, thin] = gk
        own_v_buf[rows, thin] = gv

    ways = ((-1, 0), (1, 1))
    for part in (c, 1 - c):
        if part is not c:
            for i in range(2):
                arrived(lane.at[a, b, part, i], swap_sem.at[i])
        for by in (1, -1):
            piece(a, b, part, lane_device(a, turn(b, by), c))
        for by in (1, -1):
            piece(a, b, part, lane_device(turn(a, by), b, c))
    opposite = turn(y, 2)
    few = share // 2
    left = (2 * opposite + c) * share
    send(wk_ref.at[pl.ds(left, few)], first_ref, first_sem, {"head": opposite})
    across = [
        pltpu.make_async_copy(wk_ref.at[pl.ds(left + few, few)], far_buf.at[pl.ds(0, few)], far_sem.at[0]),
        pltpu.make_async_copy(wv_ref.at[pl.ds(left, share)], far_buf.at[pl.ds(few, share)], far_sem.at[1]),
    ]
    for copy in across:
        copy.start()
    zeros[...] = jnp.zeros_like(zeros)
    some = zeros.shape[0]
    clears = [pltpu.make_async_copy(zeros, full_ref.at[pl.ds(i * some, some)], zero_sem.at[i]) for i in range(NPSG // some)]
    for copy in loads:
        copy.wait()
    for copy in clears:
        copy.start()
    own_passage(0, 0)
    own_passage(0, 1)
    for by, part in ways:
        j = turn(b, by)
        wait_pieces(a, j)
        piece(a, j, part, lane_device(a, turn(b, -by), c))
    for by, part in ways:
        along_a(a, turn(b, by))
    own_passage(1, 0)

    def far(bo):
        j = turn(b, bo)
        for by, part in ways:
            i = turn(a, by)
            (wait_pieces if bo == 0 else wait_whole)(i, j)
            piece(i, j, part, lane_device(turn(a, -by), b, c))

    far(0)
    wait_pieces(a, turn(b, 2))
    along_a(a, turn(b, 2))
    own_passage(1, 1)
    for copy in across:
        copy.wait()
    results = ((dq_buf, dq_ref), (own_k_buf, own_k_ref), (own_v_buf, own_v_ref), (far_buf, far_ref))
    stores = [pltpu.make_async_copy(buf, ref, out_sem.at[i]) for i, (buf, ref) in enumerate(results)]
    for copy in stores:
        copy.start()
    for bo in (0, -1, 1, 2):
        core(a, turn(b, bo))
    for by, _ in ways:
        core(turn(a, by), b)
    for bo in (-1, 1, 2):
        far(bo)
        for by, _ in ways:
            core(turn(a, by), turn(b, bo))
    for s in range(2):
        for i in range(2):
            block = near_ref.at[s, i, pl.ds(c * share, share)]
            arrived(block, near_sem.at[s, i])
            send(block, block, near_core_sem.at[s, i], partner)
    for bo in (0, -1, 1, 2):
        wait_pieces(turn(a, 2), turn(b, bo))
        core(turn(a, 2), turn(b, bo))
    for i in range(4):
        for j in range(4):
            arrived(all_ref.at[1 - c, i, j], core_sem.at[i, j])
            keep(i, j).wait()
    for s in range(2):
        for i in range(2):
            arrived(near_ref.at[s, i, pl.ds((1 - c) * share, share)], near_core_sem.at[s, i])
    for copy in stores + clears:
        copy.wait()
    arrived(first_ref, first_sem)
    send.finish()


def gather_plane(q, k, v, do, w_key, w_value):
    rows, cols = k.shape
    width, depth = w_key.shape
    share = width // 8
    hbm = pl.BlockSpec(memory_space=pltpu.HBM)
    dma = pltpu.SemaphoreType.DMA
    return pl.pallas_call(
        gather_kernel,
        in_specs=[hbm] * 6,
        out_specs=[hbm] * 8,
        out_shape=[
            jax.ShapeDtypeStruct((2, 4, 4, 2, 2, rows // 2, cols), BF16),
            jax.ShapeDtypeStruct((2, 2, 2 * share, depth), BF16),
            jax.ShapeDtypeStruct((3 * share // 2, depth), BF16),
            jax.ShapeDtypeStruct((share // 2, depth), BF16),
            jax.ShapeDtypeStruct(q.shape, BF16),
            jax.ShapeDtypeStruct(k.shape, F32),
            jax.ShapeDtypeStruct(v.shape, F32),
            jax.ShapeDtypeStruct((NPSG, 2, PLEN, KV * D), BF16),
        ],
        scratch_shapes=[
            pltpu.VMEM((4, 4, 2, 2, rows // 2, cols), BF16),
            pltpu.VMEM(q.shape, BF16),
            pltpu.VMEM(q.shape, BF16),
            pltpu.VMEM(k.shape, BF16),
            pltpu.VMEM(k.shape, BF16),
            pltpu.VMEM(q.shape, BF16),
            pltpu.VMEM(k.shape, F32),
            pltpu.VMEM(k.shape, F32),
            pltpu.VMEM((3 * share // 2, depth), BF16),
            pltpu.VMEM((8, 2, PLEN, KV * D), BF16),
            dma((51,)), dma((2, 4, 4)), dma((4, 4)), dma((2,)), dma((2,)), dma((2, 2)), dma((2, 2)), dma((2,)), dma((4,)),
            dma((4, 4)), dma, dma((4,)), dma((8,)),
        ],
        compiler_params=pltpu.CompilerParams(collective_id=0, has_side_effects=True, vmem_limit_bytes=VMEM),
        name="gather_plane",
    )(q, k, v, do, w_key, w_value)


CUTS = 2
JOBS = CUTS + 1
ORDER = [
    ("f", 0), ("n", 0), (0, 0), ("f", 1), ("o", 0), ("w", 0), (0, 1), ("n", 1), ("o", 1), (1, 0), (1, 1),
    (2, 0), ("q", 0), (3, 0), (2, 1), (3, 1), (4, 0), (4, 1),
]


def tail_kernel(
    full_ref, own_k_ref, own_v_ref, query_ref, wk_ref, wv_ref, near_ref, far_ref, first_ref, dx_psg_ref, dx_qry_ref,
    mine, other, relay1, side1, part, got, rows, weights, acc, terms,
    send_sem, core_sem, relay1_sem, side1_sem, got_sem, local_sem,
    load_sem, far_sem, rows_sem, out_sem, query_sem,
):
    z, x, c = place()
    y = lax.axis_index("head")
    a = z * (1 - c) + x * c
    b = x * (1 - c) + z * c
    partner = at_plane(z, x, 1 - c)
    steps = (1, -1)
    halves = (pl.ds(0, 2), pl.ds(2, 2))
    quarter = dx_qry_ref.shape[0]
    width = dx_qry_ref.shape[1] // 4
    share = width // 2
    heads = [y, turn(y, 1), turn(y, -1), turn(y, 2)]
    mirror = (0, 2, 1, 3)
    few = dx_psg_ref.shape[0] // CUTS
    size = [few] * CUTS + [quarter]

    loads = {}
    for q in range(CUTS):
        for by in (2, 1, -1, 0):
            i = turn(a, by)
            loads[q, by] = pltpu.make_async_copy(full_ref.at[c, i, :, :, :, :, q], mine.at[q, i], local_sem.at[q, i])
            loads[q, by].start()
    weight_loads = []
    for i, ref in enumerate((wk_ref, wv_ref)):
        weight_loads.append(pltpu.make_async_copy(ref.at[pl.ds(y * width, width)], weights.at[0, i], load_sem.at[0, i]))
        for s in range(2):
            weight_loads.append(pltpu.make_async_copy(near_ref.at[s, i], weights.at[1 + s, i], load_sem.at[1 + s, i]))
    cut = share // 2
    far_parts = (
        (first_ref, (3, 0, pl.ds(c * share, cut))),
        (far_ref.at[pl.ds(0, cut)], (3, 0, pl.ds(c * share + cut, cut))),
        (far_ref.at[pl.ds(cut, share)], (3, 1, pl.ds(c * share, share))),
    )
    for i, (ref, to) in enumerate(far_parts):
        weight_loads.append(pltpu.make_async_copy(ref, weights.at[to], load_sem.at[3, i]))
    for load in weight_loads:
        load.start()
    query_load = pltpu.make_async_copy(query_ref, rows.at[CUTS, 0], query_sem)
    query_load.start()
    senders = [partner, lane_device(turn(a, 1), b, c), lane_device(turn(a, -1), b, c)]
    senders += [at_plane(z, turn(x, by), 0) for by in (1, -1, 2)] + [at_plane(turn(z, by), x, 1) for by in (1, -1, 2)]
    greet(senders + [{"head": head} for head in heads[1:]])
    send = Sender(send_sem)

    def spread(job):
        used = pl.ds(0, 4 * size[job])
        for p in (3, 1, 2):
            for i in range(2):
                send(rows.at[job, 0, i, used], rows.at[job, mirror[p], i, used], rows_sem.at[job, mirror[p], i], {"head": heads[p]})

    query_load.wait()
    spread(CUTS)

    def stage0(q, by):
        i = turn(b, by)
        send(full_ref.at[1 - c, i, :, :, :, :, q], other.at[q, i], core_sem.at[q, i], partner)

    def share_far():
        for i, (ref, to) in enumerate(far_parts):
            send(ref, weights.at[to], far_sem.at[i], partner)

    def pair(q, by):
        i = turn(a, by)
        loads[q, by].wait()
        arrived(other.at[q, i], core_sem.at[q, i])
        mine[q, i] = mine[q, i] + other[q, i]
        return i

    def ring1_far(q):
        i = pair(q, 2)
        for s in range(2):
            to = lane_device(turn(a, steps[s]), b, c)
            send(mine.at[q, i, halves[s]], relay1.at[q, s], relay1_sem.at[q, s], to)

    def ring1_near(q):
        for s in range(2):
            i = pair(q, steps[s])
            arrived(relay1.at[q, s], relay1_sem.at[q, s])
            mine[q, i, halves[s]] = mine[q, i, halves[s]] + relay1[q, s]
            send(mine.at[q, i], side1.at[q, s], side1_sem.at[q, s], lane_device(i, b, c))

    def join1(q, j):
        total = mine[q, a, j].astype(F32)
        for s in range(2):
            total = total + side1[q, s, j].astype(F32)
        part[q, j] = total.astype(BF16)

    def ring2(q):
        pair(q, 0)
        for s in range(2):
            arrived(side1.at[q, s], side1_sem.at[q, s])
        for r, by in enumerate((2, 1, -1, 0)):
            j = turn(b, by)
            join1(q, j)
            for core in range(2):
                if by != 0:
                    to = at_plane(a * (1 - c) + j * c, j * (1 - c) + a * c, core)
                    send(part.at[q, j, core], got.at[q, c, r], got_sem.at[q, c, r], to)
        send(part.at[q, b, 1 - c], got.at[q, c, 3], got_sem.at[q, c, 3], partner)

    def finish_rows(q):
        for n in range(2):
            for r in range(3):
                arrived(got.at[q, n, r], got_sem.at[q, n, r])
        arrived(got.at[q, 1 - c, 3], got_sem.at[q, 1 - c, 3])
        got[q, c, 3] = part[q, b, c]
        for n in range(2):
            for i, own_ref in enumerate((own_k_ref, own_v_ref)):
                total = got[q, n, 0, i].astype(F32)
                for r in range(1, 4):
                    total = total + got[q, n, r, i].astype(F32)
                for g in range(2):
                    h = 2 * n + g
                    top = (CUTS * h + q) * few
                    rows[q, 0, i, h * few:(h + 1) * few, :] = (own_ref[top:top + few, :] + total[g]).astype(BF16)
        spread(q)

    def product(job, p, done):
        used = pl.ds(0, 4 * size[job])
        for j in range(4):
            cols = pl.ds(j * (width // 4), width // 4)
            total = dot_t(rows[job, p, 0, used], weights[p, 0, cols, :]) + dot_t(rows[job, p, 1, used], weights[p, 1, cols, :])
            if p > 0:
                total = acc[used, cols] + total
            if p < 3:
                acc[used, cols] = total
            else:
                total = total.astype(BF16)
                for d in range(4):
                    terms[job, d, pl.ds(0, size[job]), cols] = total[d * size[job]:(d + 1) * size[job]]
                done(j)

    def target(job):
        return (dx_qry_ref, 0) if job == CUTS else (dx_psg_ref, job * few)

    def piece_of(job, head, j):
        out_ref, top = target(job)
        left = head * width + j * (width // 4)
        return out_ref.at[pl.ds(top, size[job]), pl.ds(pl.multiple_of(left, width // 4), width // 4)]

    def job_terms(job):
        used = pl.ds(0, size[job])

        def done(j):
            cols = pl.ds(j * (width // 4), width // 4)
            for p in (3, 1, 2):
                send(terms.at[job, heads[p], used, cols], piece_of(job, y, j), out_sem.at[job, mirror[p], j], {"head": heads[p]})

        for p in range(4):
            if p > 0:
                for i in range(2):
                    block = rows.at[job, p, i, pl.ds(0, 4 * size[job])]
                    arrived(block, rows_sem.at[job, p, i])
            product(job, p, done)
        out_ref, top = target(job)
        out_ref[pl.ds(top, size[job]), pl.ds(pl.multiple_of(y * width, width), width)] = terms[job, y, used]

    def job_wait(job):
        for p in (1, 2, 3):
            for j in range(4):
                arrived(piece_of(job, heads[p], j), out_sem.at[job, p, j])

    def query_job():
        for load in weight_loads:
            load.wait()
        there = (1 - c) * share
        for i, to in enumerate(((3, 0, pl.ds(there, cut)), (3, 0, pl.ds(there + cut, cut)), (3, 1, pl.ds(there, share)))):
            arrived(weights.at[to], far_sem.at[i])
        job_terms(CUTS)

    steps_of = {
        "f": lambda q: stage0(q, 2),
        "n": lambda q: (stage0(q, 1), stage0(q, -1)),
        "o": lambda q: stage0(q, 0),
        "w": lambda q: share_far(),
        "q": lambda q: query_job(),
        0: ring1_far,
        1: ring1_near,
        2: ring2,
        3: finish_rows,
        4: job_terms,
    }
    for step, q in ORDER:
        steps_of[step](q)
    for job in [CUTS] + list(range(CUTS)):
        job_wait(job)
    send.finish()


def tail(full, own_k, own_v, g_qry, w_key, w_value, near, far, first):
    rows, cols = own_k.shape
    width, depth = w_key.shape
    quarter = rows // 8
    few = rows // 4 // CUTS
    hbm = pl.BlockSpec(memory_space=pltpu.HBM)
    vmem = pl.BlockSpec(memory_space=pltpu.VMEM)
    dma = pltpu.SemaphoreType.DMA
    block = (2, 2, 2, few, cols)
    full = full.reshape(2, 4, 4, 2, 2, 2, CUTS, few, cols)
    return pl.pallas_call(
        tail_kernel,
        in_specs=[hbm, vmem, vmem, hbm, hbm, hbm, hbm, pl.BlockSpec(memory_space=pl.ANY), hbm],
        out_specs=[vmem, vmem],
        out_shape=[jax.ShapeDtypeStruct((2 * quarter, width), BF16), jax.ShapeDtypeStruct((quarter, width), BF16)],
        scratch_shapes=[
            pltpu.VMEM((CUTS, 4, 4) + block, BF16),
            pltpu.VMEM((CUTS, 4, 4) + block, BF16),
            pltpu.VMEM((CUTS, 2, 2) + block, BF16),
            pltpu.VMEM((CUTS, 2, 4) + block, BF16),
            pltpu.VMEM((CUTS, 4) + block, BF16),
            pltpu.VMEM((CUTS, 2, 4) + block[1:], BF16),
            pltpu.VMEM((JOBS, 4, 2, 4 * quarter, cols), BF16),
            pltpu.VMEM((4, 2, width // 4, depth), BF16),
            pltpu.VMEM((4 * quarter, width // 4), F32),
            pltpu.VMEM((JOBS, 4, quarter, width // 4), BF16),
            dma((15 * CUTS + 3 + 18 * JOBS,)),
            dma((CUTS, 4)),
            dma((CUTS, 2)),
            dma((CUTS, 2)),
            dma((CUTS, 2, 4)),
            dma((CUTS, 4)),
            dma((4, 3)),
            dma((3,)),
            dma((JOBS, 4, 2)),
            dma((JOBS, 4, 4)),
            dma,
        ],
        compiler_params=pltpu.CompilerParams(collective_id=3, has_side_effects=True, vmem_limit_bytes=48 * 1024 * 1024),
        name="tail",
    )(full, own_k, own_v, g_qry, w_key, w_value, near, far, first)


def local(q_psg, k_psg, v_psg, do_psg, q_qry, k_qry, v_qry, do_qry, w_key, w_value, req_passages, passage_slot, query_owner):
    me = lax.axis_index("psg").astype(jnp.int32).reshape(1)
    every, near, far, first, dq_psg, own_k, own_v, cleared = gather_plane(q_psg, k_psg, v_psg, do_psg, w_key, w_value)
    far = lax.ppermute(far, "head", [(i, (i + 2) % 4) for i in range(4)])
    dq_qry, g_qry, full, dq_psg = qry_back(
        req_passages, passage_slot, query_owner, me, every.reshape(NPSG, 2, PLEN, -1), q_qry, do_qry, k_qry, v_qry, dq_psg, cleared
    )
    dx_psg, dx_qry = tail(full, own_k, own_v, g_qry, w_key, w_value, near, far, first)
    return dq_psg, dq_qry, dx_psg, dx_qry


def solution(mesh):
    rows = P("psg", "head")
    return jax.shard_map(
        local,
        mesh=mesh,
        in_specs=(rows,) * 8 + (P(None, "head"),) * 2 + (P(),) * 3,
        out_specs=(rows, rows, P(("psg", "head"), None), P(("psg", "head"), None)),
        check_vma=False,
    )
```
